32 devices in a mesh: dp: 8 (over z, core), tensor: 4 (over y, x).
Axes of the slice: x: 2, y: 2, z: 4, core: 2. Of those that a mesh axis runs over, the one named last changes fastest.
Arguments:
- tokens: bfloat16 [8192, 1536], P(('dp', 'tensor')), may hold values from -6 to 6
- norm_gain: float32 [1536], replicated, may hold values from 0.5 to 1.5
- gate_proj: bfloat16 [1536, 3072], P('dp', 'tensor'), may hold values from -0.15625 to 0.15625
- inner_proj: bfloat16 [1536, 3072], P('dp', 'tensor'), may hold values from -0.15625 to 0.15625
- shared_proj: bfloat16 [1536, 256], P('dp'), may hold values from -0.15625 to 0.15625
- step_proj: bfloat16 [1536, 48], P('dp', 'tensor'), may hold values from -0.15625 to 0.15625
- conv_inner: float32 [4, 3072], P(None, 'tensor'), may hold values from -3 to 3
- conv_inner_bias: float32 [3072], P('tensor'), may hold values from -3 to 3
- conv_shared: float32 [4, 256], replicated, may hold values from -3 to 3
- conv_shared_bias: float32 [256], replicated, may hold values from -3 to 3
- step_bias: float32 [48], P('tensor'), may hold values from -4.5 to -1.5
- decay_log: float32 [48], P('tensor'), may hold values from 0 to 2.77
- skip_gain: float32 [48], P('tensor'), may hold values from 0.5 to 1.5
- out_gain: float32 [3072], P('tensor'), may hold values from 0.5 to 1.5
- out_proj: bfloat16 [3072, 1536], P('tensor', 'dp'), may hold values from -0.109375 to 0.109375
- cotangent: bfloat16 [8192, 1536], P(('dp', 'tensor')), may hold values from -6 to 6
Outputs:
- mixed: bfloat16 [8192, 1536], P(('dp', 'tensor'))
- grad_tokens: float32 [8192, 1536], P(('dp', 'tensor'))
- grad_norm_gain: float32 [1536], replicated
- grad_gate_proj: float32 [1536, 3072], P('dp', 'tensor')
- grad_inner_proj: float32 [1536, 3072], P('dp', 'tensor')
- grad_shared_proj: float32 [1536, 256], P('dp')
- grad_step_proj: float32 [1536, 48], P('dp', 'tensor')
- grad_conv_inner: float32 [4, 3072], P(None, 'tensor')
- grad_conv_inner_bias: float32 [3072], P('tensor')
- grad_conv_shared: float32 [4, 256], replicated
- grad_conv_shared_bias: float32 [256], replicated
- grad_step_bias: float32 [48], P('tensor')
- grad_decay_log: float32 [48], P('tensor')
- grad_skip_gain: float32 [48], P('tensor')
- grad_out_gain: float32 [3072], P('tensor')
- grad_out_proj: float32 [3072, 1536], P('tensor', 'dp')
The draws below stay inside these ranges and needn't reach their ends.
All inputs are finite; a program needn't handle non-finite values.
Results may differ from the reference program's by a relative error of at most 0.012.
Values may be sent and summed in bfloat16 or wider, within the bound.
No kernel may reach another device: no remote copies, remote signals or barrier semaphores. Data moves between devices by JAX's collectives and lax.ppermute only.
A program may use at most 128 MiB of HBM per device.

```python
import jax
import jax.numpy as jnp
from jax import lax

D = 1536
HEADS = 48
HEAD_DIM = 64
STATE = 128
CONV = 4
SPAN = 256
SEQ = 1024
TOK_DEV = 256
DI = 3072
TOKENS = 8192
N_DP = 8
N_TENSOR = 4


def shard_levels(own_key, extent, split, least, top_value):
    def one(dim, parts):
        draws = jax.random.uniform(jax.random.fold_in(jax.random.fold_in(own_key, 6), dim), (parts,), jnp.float32, least / len(split), top_value / len(split))
        return jnp.repeat(jnp.exp(draws), extent[dim] // parts).reshape((-1,) + (1,) * (len(extent) - dim - 1))

    gain = one(*split[0])
    for cut in split[1:]:
        gain = gain * one(*cut)
    return gain


def gaussian(stream_key, dims, scale, limit, pieces=(), kind=jnp.bfloat16):
    values = scale * jax.random.normal(stream_key, dims, jnp.float32)
    if pieces:
        values = values * shard_levels(stream_key, dims, pieces, -0.22, 0.18)
    return jnp.clip(values, -limit, limit).astype(kind)


def setup_inputs(seed: int = 0) -> dict:
    key_list = jax.random.split(jax.random.key(seed), 17)
    tokens = gaussian(key_list[0], (TOKENS, D), 1.0, 6.0, ((0, 32),))
    norm_gain = jnp.clip(1.0 + 0.1 * jax.random.normal(key_list[1], (D,), jnp.float32), 0.5, 1.5)
    gate_proj = gaussian(key_list[2], (D, DI), D ** -0.5, 0.15625, ((0, 8), (1, 4)))
    inner_proj = gaussian(key_list[3], (D, DI), D ** -0.5, 0.15625, ((0, 8), (1, 4)))
    shared_proj = gaussian(key_list[4], (D, 2 * STATE), D ** -0.5, 0.15625, ((0, 8),))
    step_proj = gaussian(key_list[5], (D, HEADS), D ** -0.5, 0.15625, ((0, 8), (1, 4)))
    conv_inner = gaussian(key_list[6], (CONV, DI), CONV ** -0.5, 3.0, ((1, 4),), jnp.float32)
    conv_inner_bias = gaussian(key_list[7], (DI,), 0.5, 3.0, ((0, 4),), jnp.float32)
    conv_shared = gaussian(key_list[8], (CONV, 2 * STATE), CONV ** -0.5, 3.0, (), jnp.float32)
    conv_shared_bias = gaussian(key_list[9], (2 * STATE,), 0.5, 3.0, (), jnp.float32)
    step_bias = jnp.clip(-4.5 + 3.0 * jax.random.uniform(key_list[10], (HEADS,), jnp.float32) ** shard_levels(key_list[10], (HEADS,), ((0, 4),), -0.2, 0.2), -4.5, -1.5)
    decay_log = jnp.clip(2.77 * jax.random.uniform(key_list[11], (HEADS,), jnp.float32) ** shard_levels(key_list[11], (HEADS,), ((0, 4),), -0.2, 0.2), 0.0, 2.77)
    skip_gain = jnp.clip(0.5 + 1.0 * jax.random.uniform(key_list[12], (HEADS,), jnp.float32) ** shard_levels(key_list[12], (HEADS,), ((0, 4),), -0.2, 0.2), 0.5, 1.5)
    out_gain = jnp.clip(1.0 + 0.1 * jax.random.normal(key_list[13], (DI,), jnp.float32), 0.5, 1.5)
    out_proj = gaussian(key_list[14], (DI, D), DI ** -0.5, 0.109375, ((0, 4), (1, 8)))
    cotangent = gaussian(key_list[15], (TOKENS, D), 1.0, 6.0, ((0, 32),))
    return dict(tokens=tokens, norm_gain=norm_gain, gate_proj=gate_proj, inner_proj=inner_proj, shared_proj=shared_proj, step_proj=step_proj, conv_inner=conv_inner, conv_inner_bias=conv_inner_bias, conv_shared=conv_shared, conv_shared_bias=conv_shared_bias, step_bias=step_bias, decay_log=decay_log, skip_gain=skip_gain, out_gain=out_gain, out_proj=out_proj, cotangent=cotangent)


epsilon = 1e-05
highest = lax.Precision.HIGHEST

@jax.custom_vjp
def low(v):
    return lax.optimization_barrier(v.astype(jnp.bfloat16)).astype(jnp.float32)

@jax.custom_vjp
def low_back(v):
    return v

def low_keep(v):
    return (low(v), None)

def low_pass(kept, grad):
    return (grad,)

def back_keep(v):
    return (v, None)

def back_low(kept, grad):
    return (low(grad),)
low.defvjp(low_keep, low_pass)
low_back.defvjp(back_keep, back_low)

def conv_silu(values, weight, conv_bias):
    channels = values.shape[-1]
    blocks = values.reshape(-1, SEQ, channels)
    padded = jnp.pad(blocks, ((0, 0), (CONV - 1, 0), (0, 0)))
    summed = conv_bias + weight[0] * padded[:, 0:SEQ]
    for offset in range(1, CONV):
        summed = summed + weight[offset] * padded[:, offset:offset + SEQ]
    return jax.nn.silu(summed).reshape(-1, channels)

def scan_heads(values, step_sizes, decay_rates, write_state, read_state, skip_gain):
    head_count = step_sizes.shape[-1]
    spans = SEQ // SPAN
    shaped = values.reshape(-1, spans, SPAN, head_count, HEAD_DIM)
    step_blocks = step_sizes.reshape(-1, spans, SPAN, head_count)
    write_blocks = write_state.reshape(-1, spans, SPAN, STATE)
    read_blocks = read_state.reshape(-1, spans, SPAN, STATE)
    cumulated = jnp.cumsum(step_blocks * decay_rates, axis=2)
    places = jnp.arange(SPAN)
    causal = (places[:, None] >= places[None, :])[None, None, :, :, None]
    log_gaps = cumulated[:, :, :, None, :] - cumulated[:, :, None, :, :]
    kernel = jnp.exp(jnp.where(causal, log_gaps, -1e+30))
    scores = jnp.einsum('sctn,scun->sctu', read_blocks, write_blocks, precision=highest)
    weighted = shaped * step_blocks[..., None]
    within = jnp.einsum('sctuh,scuhp->scthp', scores[..., None] * kernel, weighted, precision=highest)
    final_log = cumulated[:, :, -1, :]
    tail_decay = jnp.exp(final_log[:, :, None, :] - cumulated)
    states = jnp.einsum('scuhp,scun->schpn', tail_decay[..., None] * weighted, write_blocks, precision=highest)
    carried = jnp.zeros_like(states[:, 0])
    entering = []
    for span_index in range(spans):
        entering.append(carried)
        carried = jnp.exp(final_log[:, span_index])[:, :, None, None] * carried + states[:, span_index]
    entering = jnp.stack(entering, axis=1)
    across = jnp.einsum('sctn,schpn->scthp', read_blocks, entering, precision=highest) * jnp.exp(cumulated)[..., None]
    result = within + across + skip_gain[:, None] * shaped
    return result.reshape(values.shape)

def layer_block(params, token_rows):
    norm_gain, gate_proj, inner_proj, shared_proj, step_proj, conv_inner, conv_inner_bias, conv_shared, conv_shared_bias, step_bias, decay_log, skip_gain, out_gain, out_proj = params
    inverse = lax.rsqrt(lax.optimization_barrier(jnp.mean(token_rows * token_rows, axis=-1, keepdims=True)) + epsilon)
    normed = low(token_rows * inverse * norm_gain)
    gate_values = low_back(jnp.dot(normed, gate_proj, precision=highest))
    inner_values = low_back(jnp.dot(normed, inner_proj, precision=highest))
    shared_values = low_back(jnp.dot(normed, shared_proj, precision=highest))
    step_values = low_back(jnp.dot(normed, step_proj, precision=highest))
    inner_conv = low(conv_silu(inner_values, conv_inner, conv_inner_bias))
    shared_conv = low(conv_silu(shared_values, conv_shared, conv_shared_bias))
    step_sizes = jax.nn.softplus(step_values + step_bias)
    scanned = scan_heads(inner_conv, step_sizes, -jnp.exp(decay_log), shared_conv[:, :STATE], shared_conv[:, STATE:], skip_gain)
    gated_rows = scanned * jax.nn.silu(gate_values)
    ratio = lax.rsqrt(lax.optimization_barrier(jnp.mean(gated_rows * gated_rows, axis=-1, keepdims=True)) + epsilon)
    out_normed = low(gated_rows * ratio * out_gain)
    return token_rows + jnp.dot(out_normed, out_proj, precision=highest)

def reference(tokens, norm_gain, gate_proj, inner_proj, shared_proj, step_proj, conv_inner, conv_inner_bias, conv_shared, conv_shared_bias, step_bias, decay_log, skip_gain, out_gain, out_proj, cotangent):
    params = tuple((array_item.astype(jnp.float32) for array_item in (norm_gain, gate_proj, inner_proj, shared_proj, step_proj, conv_inner, conv_inner_bias, conv_shared, conv_shared_bias, step_bias, decay_log, skip_gain, out_gain, out_proj)))
    groups = tokens.astype(jnp.float32).reshape(N_DP, TOK_DEV * N_TENSOR, D)

    def forward(weights, token_groups):

        def one_group(carried_zero, group_rows):
            return (carried_zero, jax.checkpoint(layer_block)(weights, group_rows))
        ignored, mixed_rows = lax.scan(one_group, jnp.zeros((), jnp.float32), token_groups)
        return mixed_rows
    mixed_rows, pullback = jax.vjp(forward, params, groups)
    weight_grads, grad_groups = pullback(cotangent.astype(jnp.float32).reshape(groups.shape))
    return (mixed_rows.reshape(TOKENS, D).astype(jnp.bfloat16), grad_groups.reshape(TOKENS, D), weight_grads[0], weight_grads[1], weight_grads[2], weight_grads[3], weight_grads[4], weight_grads[5], weight_grads[6], weight_grads[7], weight_grads[8], weight_grads[9], weight_grads[10], weight_grads[11], weight_grads[12], weight_grads[13])
```

```python
import jax
import jax.numpy as jnp
from jax import lax
from jax.sharding import PartitionSpec as P

HEAD_DIM = 64
STATE = 128
CONV = 4
SPAN = 256
SEQ = 1024
DI = 3072


epsilon = 1e-05
highest = lax.Precision.HIGHEST
f32 = jnp.float32
bf16 = jnp.bfloat16


def conv_silu(values, weight, conv_bias):
    channels = values.shape[-1]
    blocks = values.reshape(-1, SEQ, channels)
    padded = jnp.pad(blocks, ((0, 0), (CONV - 1, 0), (0, 0)))
    summed = conv_bias + weight[0] * padded[:, 0:SEQ]
    for offset in range(1, CONV):
        summed = summed + weight[offset] * padded[:, offset : offset + SEQ]
    return jax.nn.silu(summed).reshape(-1, channels)


def scan_heads(values, step_sizes, decay_rates, write_state, read_state, skip_gain):
    head_count = step_sizes.shape[-1]
    spans = SEQ // SPAN
    shaped = values.reshape(-1, spans, SPAN, head_count, HEAD_DIM)
    step_blocks = step_sizes.reshape(-1, spans, SPAN, head_count)
    write_blocks = write_state.reshape(-1, spans, SPAN, STATE)
    read_blocks = read_state.reshape(-1, spans, SPAN, STATE)
    cumulated = jnp.cumsum(step_blocks * decay_rates, axis=2)
    places = jnp.arange(SPAN)
    causal = (places[:, None] >= places[None, :])[None, None, :, :, None]
    log_gaps = cumulated[:, :, :, None, :] - cumulated[:, :, None, :, :]
    kernel = jnp.exp(jnp.where(causal, log_gaps, -1e30))
    scores = jnp.einsum("sctn,scun->sctu", read_blocks, write_blocks, precision=highest)
    weighted = shaped * step_blocks[..., None]
    within = jnp.einsum(
        "sctuh,scuhp->scthp", scores[..., None] * kernel, weighted, precision=highest
    )
    final_log = cumulated[:, :, -1, :]
    tail_decay = jnp.exp(final_log[:, :, None, :] - cumulated)
    states = jnp.einsum(
        "scuhp,scun->schpn", tail_decay[..., None] * weighted, write_blocks, precision=highest
    )
    carried = jnp.zeros_like(states[:, 0])
    entering = []
    for span_index in range(spans):
        entering.append(carried)
        carried = (
            jnp.exp(final_log[:, span_index])[:, :, None, None] * carried + states[:, span_index]
        )
    entering = jnp.stack(entering, axis=1)
    across = (
        jnp.einsum("sctn,schpn->scthp", read_blocks, entering, precision=highest)
        * jnp.exp(cumulated)[..., None]
    )
    result = within + across + skip_gain[:, None] * shaped
    return result.reshape(values.shape)


def gated_scan(inner_conv, shared_conv, gate_values, step_values, step_bias, decay_log, skip_gain):
    step_sizes = jax.nn.softplus(step_values + step_bias)
    scanned = scan_heads(
        inner_conv,
        step_sizes,
        -jnp.exp(decay_log),
        shared_conv[:, :STATE],
        shared_conv[:, STATE:],
        skip_gain,
    )
    return scanned * jax.nn.silu(gate_values)


def transposed(first_operand, second_operand):
    return lax.dot_general(
        first_operand, second_operand, (((1,), (1,)), ((), ())), preferred_element_type=f32
    )


def leading(first_operand, second_operand):
    return lax.dot_general(
        first_operand, second_operand, (((0,), (0,)), ((), ())), preferred_element_type=f32
    )


def plain(first_operand, second_operand):
    return jnp.dot(first_operand, second_operand, preferred_element_type=f32)


def rounded_copy(values):
    return lax.optimization_barrier(values.astype(bf16)).astype(f32)


def flip(values, count, axis, me):
    shape = values.shape
    width = shape[axis] // count
    bit = 1
    while bit < count:
        split = shape[:axis] + (count // (2 * bit), 2, bit * width) + shape[axis + 1 :]
        parts = values.reshape(split)
        first = lax.index_in_dim(parts, 0, axis + 1, keepdims=True)
        second = lax.index_in_dim(parts, 1, axis + 1, keepdims=True)
        swapped = lax.concatenate([second, first], axis + 1).reshape(shape)
        values = jnp.where((me & bit) != 0, swapped, values)
        bit *= 2
    return values


class Net:
    def __init__(self, dp, tensor):
        self.dp, self.tensor = dp, tensor
        self.chips = dp // 2
        self.place = lax.axis_index("dp")
        self.chip, self.core = self.place // 2, self.place % 2
        self.rank = lax.axis_index("tensor")

    def over_chips(self, values, k):
        return lax.ppermute(values, "dp", [(i, i ^ (2 * k)) for i in range(self.dp)])

    def over_core(self, values):
        return lax.ppermute(values, "dp", [(i, i ^ 1) for i in range(self.dp)])

    def over_tensor(self, values, k):
        return lax.ppermute(values, "tensor", [(i, i ^ k) for i in range(self.tensor)])

    def gather_dp(self, shard):
        mine = jnp.stack([shard] + [self.over_chips(shard, k) for k in range(1, self.chips)])
        other = self.over_core(mine)
        first = jnp.where(self.core == 0, mine, other)
        second = jnp.where(self.core == 0, other, mine)
        return jnp.stack([first, second], axis=1).reshape((-1,) + shard.shape[1:])

    def scatter_dp(self, values):
        split = values.reshape((self.chips, 2, -1) + values.shape[1:])
        keep = jnp.where(self.core == 0, split[:, 0], split[:, 1])
        give = jnp.where(self.core == 0, split[:, 1], split[:, 0]).astype(bf16)
        pair = keep + self.over_core(give).astype(f32)
        total = pair[0]
        for k in range(1, self.chips):
            total = total + self.over_chips(pair[k].astype(bf16), k).astype(f32)
        return total

    def gather_tensor(self, shard):
        if self.tensor != 4:
            return lax.all_gather(shard, "tensor", axis=0, tiled=True)
        half = shard.shape[0] // 2
        one, two = self.over_tensor(shard, 1), self.over_tensor(shard, 2)
        last = [self.over_tensor(one[:half], 2), self.over_tensor(two[half:], 1)]
        stacked = jnp.concatenate([shard, one, two] + last)
        return flip(stacked, 4, 0, self.rank)

    def scatter_tensor(self, values):
        if self.tensor != 4:
            low = values.astype(bf16)
            return lax.psum_scatter(low, "tensor", scatter_dimension=0, tiled=True).astype(f32)
        own, one, two, last = jnp.split(flip(values, 4, 0, self.rank), 4)
        half = own.shape[0] // 2
        low = last.astype(bf16)
        to_one = self.over_tensor(low[:half], 2).astype(f32)
        to_two = self.over_tensor(low[half:], 1).astype(f32)
        one = jnp.concatenate([one[:half] + to_one, one[half:]]).astype(bf16)
        two = jnp.concatenate([two[:half], two[half:] + to_two]).astype(bf16)
        return own + self.over_tensor(one, 1).astype(f32) + self.over_tensor(two, 2).astype(f32)

    def sum_tensor(self, values):
        total = values
        for k in range(1, self.tensor):
            total = total + self.over_tensor(values, k)
        return total

    def sum_dp(self, values):
        pair = values + self.over_core(values)
        total = pair
        for k in range(1, self.chips):
            total = total + self.over_chips(pair, k)
        return total


def local(
    net_of,
    tokens,
    norm_gain,
    gate_proj,
    inner_proj,
    shared_proj,
    step_proj,
    conv_inner,
    conv_inner_bias,
    conv_shared,
    conv_shared_bias,
    step_bias,
    decay_log,
    skip_gain,
    out_gain,
    out_proj,
    cotangent,
):
    net = net_of()
    channels = gate_proj.shape[1]
    heads = step_proj.shape[1]
    tokens_here = flip(tokens, net.chips, 1, net.chip)
    cot_here = flip(cotangent, net.chips, 1, net.chip)
    gain_here = flip(norm_gain, net.chips, 0, net.chip)
    token_rows = tokens_here.astype(f32)
    inverse = lax.rsqrt(jnp.mean(token_rows * token_rows, axis=-1, keepdims=True) + epsilon)
    unit = token_rows * inverse
    normed_low = (unit * gain_here).astype(bf16)
    padding = jnp.zeros((step_proj.shape[0], 128 - heads), bf16)
    scan_shard = jnp.concatenate([inner_proj, shared_proj, step_proj, padding], axis=1)
    rows = net.gather_tensor(normed_low)
    scan_full = net.gather_dp(scan_shard)
    gate_full = net.gather_dp(gate_proj)
    outward_full = net.gather_dp(out_proj.T)
    cot_rows = net.gather_tensor(cot_here)

    scan_values = plain(rows, scan_full)
    inner_values = scan_values[:, :channels]
    shared_values = scan_values[:, channels : channels + 2 * STATE]
    step_values = scan_values[:, channels + 2 * STATE : channels + 2 * STATE + heads]
    gate_values = plain(rows, gate_full)
    inner_conv, inner_pull = jax.vjp(conv_silu, inner_values, conv_inner, conv_inner_bias)
    shared_conv, shared_pull = jax.vjp(conv_silu, shared_values, conv_shared, conv_shared_bias)
    gated_rows, scan_pull = jax.vjp(
        gated_scan,
        rounded_copy(inner_conv),
        rounded_copy(shared_conv),
        gate_values,
        step_values,
        step_bias,
        decay_log,
        skip_gain,
    )
    grad_out = plain(cot_rows, outward_full)
    scaled = out_gain * grad_out
    sums = jnp.stack([jnp.sum(gated_rows * gated_rows, -1), jnp.sum(scaled * gated_rows, -1)])
    squares, dots = net.sum_tensor(sums)
    ratio = lax.rsqrt(squares / DI + epsilon)
    out_low = (out_gain * (gated_rows * ratio[:, None])).astype(bf16)
    branch = net.scatter_tensor(transposed(out_low, outward_full))
    mixed = flip((token_rows + branch).astype(bf16), net.chips, 1, net.chip)
    grad_out_proj = net.scatter_dp(leading(cot_rows, out_low)).T
    grad_out_gain = jnp.sum(grad_out * gated_rows * ratio[:, None], axis=0)
    grad_gated = scaled * ratio[:, None] - gated_rows * (ratio**3 / DI * dots)[:, None]
    (
        grad_inner_conv,
        grad_shared_conv,
        grad_gate_values,
        grad_step_values,
        grad_step_bias,
        grad_decay_log,
        grad_skip_gain,
    ) = scan_pull(grad_gated)
    grad_inner_values, grad_conv_inner, grad_conv_inner_bias = inner_pull(grad_inner_conv)
    grad_shared_values, grad_conv_shared, grad_conv_shared_bias = shared_pull(grad_shared_conv)
    gate_back = grad_gate_values.astype(bf16)
    scan_back = jnp.concatenate(
        [
            grad_inner_values.astype(bf16),
            grad_shared_values.astype(bf16),
            grad_step_values.astype(bf16),
            jnp.zeros((grad_step_values.shape[0], 128 - heads), bf16),
        ],
        axis=1,
    )
    grad_normed = net.scatter_tensor(
        transposed(gate_back, gate_full) + transposed(scan_back, scan_full)
    )
    gate_partial = leading(rows, gate_back)
    scan_partial = leading(rows, scan_back)
    grad_gate_proj = net.scatter_dp(gate_partial)
    grad_scan_proj = net.scatter_dp(scan_partial)
    grad_inner_proj = grad_scan_proj[:, :channels]
    grad_shared_proj = net.sum_tensor(grad_scan_proj[:, channels : channels + 2 * STATE])
    grad_step_proj = grad_scan_proj[:, channels + 2 * STATE : channels + 2 * STATE + heads]
    grad_gain_here = (
        jnp.sum(gate_full.astype(f32) * gate_partial, axis=1)
        + jnp.sum(scan_full.astype(f32) * scan_partial, axis=1)
    ) / gain_here
    grad_norm_gain = flip(grad_gain_here, net.chips, 0, net.chip)
    spread = grad_normed * gain_here
    grad_token_rows = (
        cot_here.astype(f32)
        + inverse * spread
        - unit * (inverse * jnp.mean(spread * unit, axis=-1, keepdims=True))
    )
    grad_tokens = flip(grad_token_rows, net.chips, 1, net.chip)
    own = (
        grad_conv_inner,
        grad_conv_inner_bias,
        grad_out_gain,
        grad_step_bias,
        grad_decay_log,
        grad_skip_gain,
    )
    common = (grad_conv_shared, grad_conv_shared_bias, grad_norm_gain)
    common_flat = net.sum_tensor(jnp.concatenate([v.reshape(-1) for v in common]))
    flat = net.sum_dp(jnp.concatenate([v.reshape(-1) for v in own] + [common_flat]))
    small = []
    start = 0
    for v in own + common:
        small.append(flat[start : start + v.size].reshape(v.shape))
        start += v.size
    (
        grad_conv_inner,
        grad_conv_inner_bias,
        grad_out_gain,
        grad_step_bias,
        grad_decay_log,
        grad_skip_gain,
        grad_conv_shared,
        grad_conv_shared_bias,
        grad_norm_gain,
    ) = small
    return (
        mixed,
        grad_tokens,
        grad_norm_gain,
        grad_gate_proj,
        grad_inner_proj,
        grad_shared_proj,
        grad_step_proj,
        grad_conv_inner,
        grad_conv_inner_bias,
        grad_conv_shared,
        grad_conv_shared_bias,
        grad_step_bias,
        grad_decay_log,
        grad_skip_gain,
        grad_out_gain,
        grad_out_proj,
    )


def solution(mesh):
    dp, tensor = mesh.shape["dp"], mesh.shape["tensor"]

    def on_device(*args):
        return local(lambda: Net(dp, tensor), *args)

    return jax.shard_map(
        on_device,
        mesh=mesh,
        in_specs=(
            P(("dp", "tensor"), None),
            P(),
            P("dp", "tensor"),
            P("dp", "tensor"),
            P("dp", None),
            P("dp", "tensor"),
            P(None, "tensor"),
            P("tensor"),
            P(),
            P(),
            P("tensor"),
            P("tensor"),
            P("tensor"),
            P("tensor"),
            P("tensor", "dp"),
            P(("dp", "tensor"), None),
        ),
        out_specs=(
            P(("dp", "tensor"), None),
            P(("dp", "tensor"), None),
            P(),
            P("dp", "tensor"),
            P("dp", "tensor"),
            P("dp", None),
            P("dp", "tensor"),
            P(None, "tensor"),
            P("tensor"),
            P(),
            P(),
            P("tensor"),
            P("tensor"),
            P("tensor"),
            P("tensor"),
            P("tensor", "dp"),
        ),
        check_vma=False,
    )
```

```python
import functools

import jax
import jax.numpy as jnp
from jax import lax
from jax.experimental import pallas as pl
from jax.experimental.pallas import tpu as pltpu
from jax.sharding import PartitionSpec as P

DI = 3072
epsilon = 1e-05
HEAD_DIM = 64
STATE = 128
CONV = 4
SEQ = 1024
SPAN = 256
CHUNK = 128
LANES = 128
NEVER = -1e30
f32 = jnp.float32
bf16 = jnp.bfloat16
highest = lax.Precision.HIGHEST


def dot(first, second, first_dim=1, second_dim=0, precision=None):
    return lax.dot_general(
        first,
        second,
        (((first_dim,), (second_dim,)), ((), ())),
        precision=precision,
        preferred_element_type=f32,
    )


def sigmoid(values):
    return 0.5 * jnp.tanh(0.5 * values) + 0.5


def places(dim):
    return lax.broadcasted_iota(jnp.int32, (CHUNK, LANES), dim)


def decays(step_raw, heads_ref):
    raw = step_raw + heads_ref[0:1]
    small = jnp.exp(-jnp.abs(raw))
    log_one = jnp.where(small < 1e-3, small - 0.5 * small * small, jnp.log(1.0 + small))
    steps = jnp.maximum(raw, 0.0) + log_one
    upto = (places(0) >= places(1)).astype(f32)
    summed = dot(upto, steps * heads_ref[1:2], precision=highest)
    return steps, sigmoid(raw), summed, summed - jnp.log(steps)


def pair_of(first, second):
    return jnp.concatenate([first, second], axis=0)


def forward_kernel(raw_ref, taps_ref, heads_ref, skip_ref, scanned_ref, pre_ref, states_ref, state, before):
    chunk = pl.program_id(0)
    channels = skip_ref.shape[1]
    width = channels + 2 * STATE

    @pl.when(chunk % (SEQ // CHUNK) == 0)
    def _():
        state[...] = jnp.zeros_like(state)
        before[...] = jnp.zeros_like(before)

    raw = raw_ref[:, :width]
    extended = jnp.concatenate([before[...], raw], axis=0)
    pre = taps_ref[CONV : CONV + 1] + taps_ref[CONV - 1 : CONV] * raw
    for tap in range(CONV - 1):
        start = 8 - (CONV - 1) + tap
        pre = pre + taps_ref[tap : tap + 1] * extended[start : start + CHUNK]
    before[...] = raw[CHUNK - 8 :]
    pre_ref[...] = pre
    act = (pre * sigmoid(pre)).astype(bf16)
    writes = act[:, channels : channels + STATE]
    reads = act[:, channels + STATE :]
    _, _, summed, shifted = decays(raw_ref[:, width:], heads_ref)
    summed_t, shifted_t = summed.T, shifted.T
    tail_t = jnp.exp(summed_t[:, CHUNK - 1 :] - shifted_t)
    scores = dot(reads, writes, 1, 1)
    writes_t = writes.astype(f32).T
    causal = places(0) >= places(1)
    left = places(1) < HEAD_DIM
    states_ref[...] = state[...].astype(bf16)
    for pair in range(channels // LANES):
        cols = slice(pair * LANES, (pair + 1) * LANES)
        values = act[:, cols].astype(f32)
        both = pair_of(jnp.where(left, values, 0.0), jnp.where(left, 0.0, values)).astype(bf16)
        mixes, tails, grown = [], [], []
        for head in (2 * pair, 2 * pair + 1):
            here = jnp.broadcast_to(summed[:, head : head + 1], (CHUNK, LANES))
            decay = jnp.exp(jnp.where(causal, here - shifted_t[head : head + 1], NEVER))
            mixes.append((scores * decay).astype(bf16))
            tails.append((writes_t * tail_t[head : head + 1]).astype(bf16))
            grown.append(here)
        stacked = pair_of(jnp.concatenate(mixes, axis=1), jnp.concatenate(tails, axis=1))
        out = dot(stacked, both)
        entering = state[:, cols]
        factor = jnp.exp(jnp.where(left, grown[0], grown[1]))
        across = dot(reads, entering.astype(bf16)) * factor
        scanned_ref[:, cols] = out[:CHUNK] + across + values * skip_ref[:, cols]
        state[:, cols] = entering * factor[CHUNK - 1 :] + out[CHUNK:]


def backward_kernel(part, n_deps, *refs):
    raw_ref, pre_ref, grad_ref, states_ref, taps_ref, heads_ref, skip_ref = refs[:7]
    held, refs = refs[7 : 7 + (5 if part else 0)], refs[7 + (5 if part else 0) + n_deps :]
    low_ref, sums_ref, head_sums_ref, carry, after, wide = refs
    step = pl.program_id(0)
    channels = skip_ref.shape[1]
    width = channels + 2 * STATE

    @pl.when(step == 0)
    def _():
        if part:
            for ref, source in zip((sums_ref, head_sums_ref, carry, after), held[1:], strict=True):
                ref[...] = source[...]
        else:
            sums_ref[...] = jnp.zeros_like(sums_ref)
            head_sums_ref[...] = jnp.zeros_like(head_sums_ref)

    @pl.when((step + part * pl.num_programs(0)) % (SEQ // CHUNK) == 0)
    def _():
        carry[...] = jnp.zeros_like(carry)
        after[...] = jnp.zeros_like(after)

    pre = pre_ref[...]
    gate = sigmoid(pre)
    act = (pre * gate).astype(bf16)
    writes = act[:, channels : channels + STATE]
    reads = act[:, channels + STATE :]
    steps, slopes, summed, shifted = decays(raw_ref[:, width:], heads_ref)
    summed_t = summed.T
    scores_t = dot(writes, reads, 1, 1)
    causal = places(0) <= places(1)
    earlier = places(0) < places(1)
    suffix = (places(0) >= places(1)).astype(bf16)
    left = places(1) < HEAD_DIM
    score_grads = jnp.zeros((CHUNK, LANES), f32)
    spans, inner_grads = [], []
    for pair in range(channels // LANES):
        cols = slice(pair * LANES, (pair + 1) * LANES)
        values = act[:, cols].astype(f32)
        both = pair_of(jnp.where(left, values, 0.0), jnp.where(left, 0.0, values)).astype(bf16)
        grad_low = grad_ref[:, cols]
        grad = grad_low.astype(f32)
        grad_both = pair_of(jnp.where(left, grad, 0.0), jnp.where(left, 0.0, grad)).astype(bf16)
        products = dot(both, grad_low, 1, 1)
        mixes, crossing, grown, tails = [], [], [], []
        for place, head in enumerate((2 * pair, 2 * pair + 1)):
            here = jnp.broadcast_to(shifted[:, head : head + 1], (CHUNK, LANES))
            decay = jnp.exp(jnp.where(causal, summed_t[head : head + 1] - here, NEVER))
            product = products[place * CHUNK : (place + 1) * CHUNK]
            score_grads = score_grads + decay * product
            mix = scores_t * decay
            mixes.append(mix.astype(bf16))
            crossing.append((mix * product).astype(bf16))
            level = jnp.broadcast_to(summed[:, head : head + 1], (CHUNK, LANES))
            grown.append(level)
            tails.append(level[CHUNK - 1 :] - here)
        sums = dot(pair_of(*crossing), suffix)
        for place in range(2):
            part = jnp.where(earlier, sums[place * CHUNK : (place + 1) * CHUNK], 0.0)
            spans.append(jnp.sum(part, axis=0, keepdims=True))
        within = dot(jnp.concatenate(mixes, axis=1), grad_both)
        factor = jnp.exp(jnp.where(left, grown[0], grown[1]))
        tail = jnp.exp(jnp.where(left, tails[0], tails[1]))
        leaving = carry[:, cols]
        entering = states_ref[:, cols]
        later = tail * dot(writes, leaving.astype(bf16))
        both_grads = within + later
        inner_grads.append(both_grads + skip_ref[:, cols] * grad)
        spread = factor * grad
        spread_low = spread.astype(bf16)
        wide[0:CHUNK, cols] = spread_low
        wide[CHUNK : 2 * CHUNK, cols] = (tail * values).astype(bf16)
        wide[2 * CHUNK : 3 * CHUNK, cols] = (spread * dot(reads, entering)).astype(bf16)
        wide[3 * CHUNK : 4 * CHUNK, cols] = (values * later).astype(bf16)
        wide[4 * CHUNK : 5 * CHUNK, cols] = (values * both_grads).astype(bf16)
        held = jnp.sum(entering.astype(f32) * leaving, axis=0, keepdims=True) * factor[CHUNK - 1 :]
        sums_ref[CONV + 1 : CONV + 2, cols] += jnp.sum(grad * values, axis=0, keepdims=True)
        sums_ref[CONV + 2 : CONV + 3, cols] = held
    reads_t = reads.astype(f32).T.astype(bf16)
    score_low = score_grads.astype(bf16)
    spread_all = wide[0:CHUNK, :]
    read_grads = dot(score_low, writes, 0, 0) + dot(spread_all, states_ref[...], 1, 1)
    write_grads = dot(score_low, reads) + dot(wide[CHUNK : 2 * CHUNK, :], carry[...].astype(bf16), 1, 1)
    last = jnp.exp(summed[CHUNK - 1 :])
    of_head = (
        lax.broadcasted_iota(jnp.int32, (channels, LANES), 0) // HEAD_DIM
        == lax.broadcasted_iota(jnp.int32, (channels, LANES), 1)
    )
    reduced = dot(wide[2 * CHUNK : 5 * CHUNK, :], of_head.astype(bf16))
    held_rows = jnp.broadcast_to(sums_ref[CONV + 2 : CONV + 3, :channels], (8, channels))
    held_heads = dot(held_rows, of_head.astype(f32), precision=highest)[0:1]
    lasts = dot(jnp.broadcast_to(last, (8, LANES)), of_head.astype(f32), 1, 1, precision=highest)[0:1]
    carry[...] = carry[...] * lasts + dot(reads_t, spread_all)
    across_sums, later_sums, both_sums = reduced[:CHUNK], reduced[CHUNK : 2 * CHUNK], reduced[2 * CHUNK :]
    span_rows = jnp.concatenate(spans + [jnp.zeros((LANES - len(spans), LANES), f32)], axis=0)
    log_grads = (
        dot((places(0) <= places(1)).astype(f32), across_sums, precision=highest)
        + dot((places(0) > places(1)).astype(f32), later_sums, precision=highest)
        + span_rows.T
        + held_heads
    )
    ratio = jnp.where(steps > 1e-30, slopes / steps, 1.0)
    step_grads = both_sums * ratio + heads_ref[1:2] * log_grads * slopes
    head_sums_ref[0:1] += jnp.sum(step_grads, axis=0, keepdims=True)
    head_sums_ref[1:2] += jnp.sum(log_grads * steps, axis=0, keepdims=True)

    raw = raw_ref[:, :width]
    act_grads = jnp.concatenate(inner_grads + [write_grads, read_grads], axis=1)
    pre_grads = act_grads * (gate * (1.0 + pre * (1.0 - gate)))
    extended = jnp.concatenate([pre_grads, after[...]], axis=0)
    after[...] = pre_grads[:8]
    sums_ref[CONV : CONV + 1] += jnp.sum(pre_grads, axis=0, keepdims=True)
    raw_grads = taps_ref[CONV - 1 : CONV] * pre_grads
    sums_ref[CONV - 1 : CONV] += jnp.sum(raw * pre_grads, axis=0, keepdims=True)
    for tap in range(CONV - 1):
        moved = extended[CONV - 1 - tap : CONV - 1 - tap + CHUNK]
        raw_grads = raw_grads + taps_ref[tap : tap + 1] * moved
        sums_ref[tap : tap + 1] += jnp.sum(raw * moved, axis=0, keepdims=True)
    low_ref[:, :width] = raw_grads.astype(bf16)
    low_ref[:, width:] = step_grads.astype(bf16)


def stay(values):
    return pltpu.with_memory_space_constraint(values, pltpu.HBM)


def scan_forward(raw, taps, heads, skip):
    tokens, full = raw.shape
    channels = skip.shape[1]
    width = channels + 2 * STATE
    count = tokens // CHUNK
    by_chunk = lambda shape: pl.BlockSpec(shape, lambda s: (s, 0))
    whole = lambda v: pl.BlockSpec(v.shape, lambda s: (0, 0))
    return pl.pallas_call(
        forward_kernel,
        grid=(count,),
        in_specs=[by_chunk((CHUNK, full)), whole(taps), whole(heads), whole(skip)],
        out_specs=[
            by_chunk((CHUNK, channels)),
            by_chunk((CHUNK, width)),
            by_chunk((STATE, channels)),
        ],
        scratch_shapes=[pltpu.VMEM((STATE, channels), f32), pltpu.VMEM((8, width), f32)],
        out_shape=[
            jax.ShapeDtypeStruct((tokens, channels), f32),
            pltpu.HBM((tokens, width), f32),
            pltpu.HBM((count * STATE, channels), bf16),
        ],
        compiler_params=pltpu.CompilerParams(vmem_limit_bytes=20 << 20),
        cost_estimate=cost(9),
        name="scan_forward",
    )(raw, taps, heads, skip)


def scan_backward(part, raw, pre, grad, states, taps, heads, skip, held, earlier):
    tokens, full = raw.shape
    channels = skip.shape[1]
    width = channels + 2 * STATE
    count = tokens // CHUNK
    half = count // 2
    last = count - 1 - part * half
    by_chunk = lambda shape: pl.BlockSpec(shape, lambda s: (last - s, 0))
    whole = lambda shape: pl.BlockSpec(shape, lambda s: (0, 0))
    anywhere = pl.BlockSpec(memory_space=pl.ANY)
    kept = [(8, width), (8, LANES), (STATE, channels), (8, width)]
    held = list(held) if part else []
    return pl.pallas_call(
        functools.partial(backward_kernel, part, len(earlier)),
        grid=(half,),
        in_specs=[
            by_chunk((CHUNK, full)),
            by_chunk((CHUNK, width)),
            by_chunk((CHUNK, channels)),
            by_chunk((STATE, channels)),
            whole(taps.shape),
            whole(heads.shape),
            whole(skip.shape),
        ]
        + ([anywhere] + [whole(shape) for shape in kept] if part else [])
        + [anywhere] * len(earlier),
        out_specs=[by_chunk((CHUNK, full))] + [whole(shape) for shape in kept],
        scratch_shapes=[pltpu.VMEM((5 * CHUNK, channels), bf16)],
        out_shape=[jax.ShapeDtypeStruct((tokens, full), bf16)]
        + [jax.ShapeDtypeStruct(shape, f32) for shape in kept],
        input_output_aliases={7: 0} if part else {},
        compiler_params=pltpu.CompilerParams(vmem_limit_bytes=20 << 20),
        cost_estimate=cost(12),
        name=f"scan_backward_{part}",
    )(stay(raw), stay(pre), grad, stay(states), taps, heads, skip, *held, *earlier)


BLOCK = 256


def cost(microseconds):
    return pl.CostEstimate(flops=0, bytes_accessed=int(microseconds * 3.5e6), transcendentals=0)


LIMIT = 24 << 20


def column_sums(values, count):
    rows = [
        jnp.sum(values[i * LANES : (i + 1) * LANES].T, axis=0, keepdims=True)
        for i in range(count // LANES)
    ]
    return jnp.concatenate(rows, axis=0)


def fold(values):
    total = values[:, :LANES]
    for start in range(LANES, values.shape[1], LANES):
        total = total + values[:, start : start + LANES]
    return total


def shard_rows(place, index, chips, height):
    core, chip = index // chips, index % chips
    return pl.multiple_of(((place[0] ^ chip) * 2 + (place[1] ^ core)) * height, height)


def row_start(place, start):
    if isinstance(start, int):
        return pl.multiple_of((start // BLOCK ^ place[2]) * BLOCK + start % BLOCK, LANES)
    return pl.multiple_of((start // BLOCK ^ place[2]) * BLOCK, BLOCK)


def product_kernel(layout, chips, epilogue, place, *refs):
    heights, keep_rows, n_extra, n_out = layout
    n_rows, n_full = len(heights), 2 * chips
    row_refs, refs = refs[:n_rows], refs[n_rows:]
    full_refs, refs = refs[:n_full], refs[n_full:]
    extra, refs = refs[:n_extra], refs[n_extra:]
    outs, refs = refs[:n_out], refs[n_out:]
    full_out, refs = refs[0], refs[1:]
    if keep_rows:
        rows_out, refs = refs[0], refs[1:]
    rows, full, sems, back = refs
    step = pl.program_id(0)
    starts = [sum(heights[:i]) for i in range(n_rows)]
    shard = full.shape[0] // n_full
    row_copies = [
        pltpu.make_async_copy(
            row_refs[i], rows.at[pl.ds(row_start(place, starts[i]), heights[i])], sems.at[i]
        )
        for i in range(n_rows)
    ]
    full_copies = [
        pltpu.make_async_copy(
            full_refs[i], full.at[pl.ds(shard_rows(place, i, chips, shard), shard)], sems.at[n_rows + i]
        )
        for i in range(n_full)
    ]
    backs = [pltpu.make_async_copy(full, full_out, back.at[0])]

    @pl.when(step == 0)
    def _():
        for copy in full_copies + row_copies:
            copy.start()
        for copy in full_copies:
            copy.wait()
        backs[0].start()

    for i in range(n_rows):

        @pl.when(step == starts[i] // BLOCK)
        def _(i=i):
            row_copies[i].wait()

    if keep_rows:
        backs.append(pltpu.make_async_copy(rows, rows_out, back.at[1]))

        @pl.when(step == starts[-1] // BLOCK)
        def _():
            backs[1].start()

    block = rows[pl.ds(row_start(place, step * BLOCK), BLOCK), :]
    epilogue(step, lambda cols: dot(block, full[:, cols]), extra, outs)

    @pl.when(step == pl.num_programs(0) - 1)
    def _():
        for copy in backs:
            copy.wait()


def product(place, row_pieces, full_pieces, epilogue, extra, outs, keep_rows, name):
    chips = len(full_pieces) // 2
    heights = tuple(piece.shape[0] for piece in row_pieces)
    tokens, depth = sum(heights), row_pieces[0].shape[1]
    columns = full_pieces[0].shape[1]
    anywhere = pl.BlockSpec(memory_space=pl.ANY)
    by_block = lambda cols: pl.BlockSpec((BLOCK, cols), lambda s, p: (s ^ p[2], 0))
    whole = lambda shape: pl.BlockSpec(shape, lambda s, p: (0, 0))
    out_specs, out_shape = [], []
    for cols, dtype in outs:
        shape = (tokens // LANES, LANES) if cols is None else (tokens, cols)
        out_specs.append(whole(shape) if cols is None else by_block(cols))
        out_shape.append(jax.ShapeDtypeStruct(shape, dtype))
    out_specs.append(anywhere)
    out_shape.append(jax.ShapeDtypeStruct((depth, columns), bf16))
    if keep_rows:
        out_specs.append(anywhere)
        out_shape.append(jax.ShapeDtypeStruct((tokens, depth), bf16))
    layout = (heights, keep_rows, len(extra), len(outs))
    return pl.pallas_call(
        functools.partial(product_kernel, layout, chips, epilogue),
        grid_spec=pltpu.PrefetchScalarGridSpec(
            num_scalar_prefetch=1,
            grid=(tokens // BLOCK,),
            in_specs=[anywhere] * (len(row_pieces) + len(full_pieces))
            + [by_block(v.shape[1]) if by else whole(v.shape) for v, by in extra],
            out_specs=out_specs,
            scratch_shapes=[
                pltpu.VMEM((tokens, depth), bf16),
                pltpu.VMEM((depth, columns), bf16),
                pltpu.SemaphoreType.DMA((len(row_pieces) + len(full_pieces),)),
                pltpu.SemaphoreType.DMA((2,)),
            ],
        ),
        out_shape=out_shape,
        compiler_params=pltpu.CompilerParams(vmem_limit_bytes=(56 << 20) if keep_rows else LIMIT),
        cost_estimate=cost(8),
        name=name,
    )(place, *row_pieces, *full_pieces, *[v for v, _ in extra])


def slices(columns):
    return [slice(start, min(start + 256, columns)) for start in range(0, columns, 256)]


def raw_epilogue(step, multiply, extra, outs):
    (raw,) = outs
    for cols in slices(raw.shape[1]):
        raw[:, cols] = multiply(cols)


def gate_epilogue(step, multiply, extra, outs):
    (scanned,) = extra
    gate, gated, sums = outs
    total = jnp.zeros((BLOCK, LANES), f32)
    for cols in slices(gate.shape[1]):
        value = multiply(cols)
        gate[:, cols] = value
        product = scanned[:, cols] * (value * sigmoid(value))
        gated[:, cols] = product
        total = total + fold(product * product)
    sums[pl.ds(step * (BLOCK // LANES), BLOCK // LANES), :] = column_sums(total, BLOCK)


def out_epilogue(step, multiply, extra, outs):
    gated, gain = extra
    grad, sums = outs
    total = jnp.zeros((BLOCK, LANES), f32)
    for cols in slices(grad.shape[1]):
        value = multiply(cols)
        grad[:, cols] = value
        total = total + fold(value * gain[:, cols] * gated[:, cols])
    sums[pl.ds(step * (BLOCK // LANES), BLOCK // LANES), :] = column_sums(total, BLOCK)


def grads_kernel(place, rows, low, *refs):
    keep, give, acc = refs[-3:]
    shard = keep.shape[1]
    for cols in slices(low.shape[1]):
        acc[:, cols] = dot(rows[...], low[:, cols], 0, 0)
    keep[0] = acc[pl.ds(pl.multiple_of(place[1] * shard, shard), shard), :]
    give[0] = acc[pl.ds(pl.multiple_of((1 - place[1]) * shard, shard), shard), :].astype(bf16)


def weight_grads(place, chips, rows, low, name, earlier=()):
    tokens, depth = rows.shape
    columns = low.shape[1]
    shard = depth // (2 * chips)
    if depth // chips % LANES:
        whole = dot(rows, low, 0, 0).reshape(chips, 2, shard, columns)
        whole = jnp.take(whole, jnp.arange(chips) ^ place[0], axis=0)
        return jnp.take(whole, place[1], axis=1), jnp.take(whole, 1 - place[1], axis=1).astype(bf16)
    out = pl.BlockSpec((1, shard, columns), lambda k, p: (k, 0, 0))
    return pl.pallas_call(
        grads_kernel,
        grid_spec=pltpu.PrefetchScalarGridSpec(
            num_scalar_prefetch=1,
            grid=(chips,),
            in_specs=[
                pl.BlockSpec((tokens, depth // chips), lambda k, p: (0, k ^ p[0])),
                pl.BlockSpec((tokens, columns), lambda k, p: (0, 0)),
            ]
            + [pl.BlockSpec(memory_space=pl.ANY)] * len(earlier),
            out_specs=[out, out],
            scratch_shapes=[pltpu.VMEM((depth // chips, columns), f32)],
        ),
        out_shape=[
            jax.ShapeDtypeStruct((chips, shard, columns), f32),
            jax.ShapeDtypeStruct((chips, shard, columns), bf16),
        ],
        compiler_params=pltpu.CompilerParams(vmem_limit_bytes=LIMIT),
        cost_estimate=cost(6),
        name=name,
    )(place, rows, low, *earlier)


def back_kernel(count, with_rows, place, *refs):
    lows, fulls, refs = refs[:count], refs[count : 2 * count], refs[2 * count :]
    rows, out, sums = (refs[0], refs[-2], refs[-1]) if with_rows else (None, refs[-1], None)
    if with_rows:

        @pl.when(pl.program_id(0) == 0)
        def _():
            sums[...] = jnp.zeros_like(sums)

    for cols in slices(out.shape[1]):
        value = dot(lows[0][...], fulls[0][cols, :], 1, 1)
        for low, full in zip(lows[1:], fulls[1:], strict=True):
            value = value + dot(low[...], full[cols, :], 1, 1)
        out[:, cols] = value.astype(out.dtype)
        if with_rows:
            sums[0:1, cols] += jnp.sum(value * rows[:, cols].astype(f32), axis=0, keepdims=True)


def back(place, lows, fulls, rows, first, count, dtype, name, earlier):
    depth = fulls[0].shape[0]
    by_block = lambda cols: pl.BlockSpec((BLOCK, cols), lambda s, p: ((s + first) ^ p[2], 0))
    whole = lambda shape: pl.BlockSpec(shape, lambda s, p: (0, 0))
    extra = [] if rows is None else [rows]
    out = pl.pallas_call(
        functools.partial(back_kernel, len(lows), rows is not None),
        grid_spec=pltpu.PrefetchScalarGridSpec(
            num_scalar_prefetch=1,
            grid=(count,),
            in_specs=[by_block(v.shape[1]) for v in lows]
            + [whole(v.shape) for v in fulls]
            + [by_block(depth) for _ in extra]
            + [pl.BlockSpec(memory_space=pl.ANY)] * len(earlier),
            out_specs=[pl.BlockSpec((BLOCK, depth), lambda s, p: (s, 0))] + [whole((8, depth)) for _ in extra],
        ),
        out_shape=[jax.ShapeDtypeStruct((count * BLOCK, depth), dtype)]
        + [jax.ShapeDtypeStruct((8, depth), f32) for _ in extra],
        compiler_params=pltpu.CompilerParams(vmem_limit_bytes=LIMIT),
        cost_estimate=cost(2 * count),
        name=name,
    )(place, *lows, *fulls, *extra, *earlier)
    return out[0], out[1] if extra else None


def columns_of(row):
    return jnp.broadcast_to(row, (LANES, LANES)).T


def low_kernel(gated, squares, gain, out):
    for part in range(BLOCK // LANES):
        rows = slice(part * LANES, (part + 1) * LANES)
        row = squares[pl.ds(pl.program_id(0) * (BLOCK // LANES) + part, 1), :]
        ratio = columns_of(lax.rsqrt(row / DI + epsilon))
        for start in range(0, out.shape[1], LANES):
            cols = slice(start, start + LANES)
            out[rows, cols] = (gain[:, cols] * (gated[rows, cols] * ratio)).astype(bf16)


def low_rows(gated, squares, gain):
    tokens, columns = gated.shape
    return pl.pallas_call(
        low_kernel,
        grid=(tokens // BLOCK,),
        in_specs=[
            pl.BlockSpec((BLOCK, columns), lambda s: (s, 0)),
            pl.BlockSpec(squares.shape, lambda s: (0, 0)),
            pl.BlockSpec(gain.shape, lambda s: (0, 0)),
        ],
        out_specs=pl.BlockSpec((BLOCK, columns), lambda s: (s, 0)),
        out_shape=jax.ShapeDtypeStruct((tokens, columns), bf16),
        cost_estimate=cost(4),
        name="out_normed",
    )(gated, squares, gain)


def gating_kernel(grad_out, gated, scanned, gate, squares, dots, gain, gate_back, scan_grad, gain_grad):
    step = pl.program_id(0)

    @pl.when(step == 0)
    def _():
        gain_grad[...] = jnp.zeros_like(gain_grad)

    for part in range(BLOCK // LANES):
        rows = slice(part * LANES, (part + 1) * LANES)
        place = pl.ds(step * (BLOCK // LANES) + part, 1)
        ratio_row = lax.rsqrt(squares[place, :] / DI + epsilon)
        ratio = columns_of(ratio_row)
        pull = columns_of(ratio_row * ratio_row * ratio_row / DI * dots[place, :])
        for start in range(0, gate.shape[1], LANES):
            cols = slice(start, start + LANES)
            out, held, value = grad_out[rows, cols], gated[rows, cols], gate[rows, cols]
            scaled = out * ratio
            gain_grad[0:1, cols] += jnp.sum(scaled * held, axis=0, keepdims=True)
            grad = gain[:, cols] * scaled - held * pull
            slope = sigmoid(value)
            scan_grad[rows, cols] = (grad * (value * slope)).astype(bf16)
            gate_grad = grad * scanned[rows, cols] * (slope * (1.0 + value * (1.0 - slope)))
            gate_back[rows, cols] = gate_grad.astype(bf16)


def gating(grad_out, gated, scanned, gate, squares, dots, gain):
    tokens, columns = gated.shape
    block = pl.BlockSpec((BLOCK, columns), lambda s: (s, 0))
    whole = lambda v: pl.BlockSpec(v.shape, lambda s: (0, 0))
    return pl.pallas_call(
        gating_kernel,
        grid=(tokens // BLOCK,),
        in_specs=[block] * 4 + [whole(squares), whole(dots), whole(gain)],
        out_specs=[block, block, pl.BlockSpec((8, columns), lambda s: (0, 0))],
        out_shape=[
            jax.ShapeDtypeStruct((tokens, columns), bf16),
            jax.ShapeDtypeStruct((tokens, columns), bf16),
            jax.ShapeDtypeStruct((8, columns), f32),
        ],
        compiler_params=pltpu.CompilerParams(vmem_limit_bytes=LIMIT),
        cost_estimate=cost(3),
        name="gating",
    )(grad_out, gated, scanned, gate, squares, dots, gain)


def nothing(*refs):
    pass


def pinned(values, earlier):
    anywhere = pl.BlockSpec(memory_space=pl.ANY)
    held = pl.pallas_call(
        nothing,
        in_specs=[anywhere] * (len(values) + len(earlier)),
        out_specs=[anywhere] * len(values),
        out_shape=[jax.ShapeDtypeStruct(v.shape, v.dtype) for v in values],
        input_output_aliases={i: i for i in range(len(values))},
        name="pinned",
    )(*values, *earlier)
    return list(held)


def copy_kernel(source, *refs):
    refs[-1][...] = source[...]


def copied(value, earlier):
    whole = pl.BlockSpec(memory_space=pltpu.VMEM)
    return pl.pallas_call(
        copy_kernel,
        in_specs=[whole] + [pl.BlockSpec(memory_space=pl.ANY)] * len(earlier),
        out_specs=whole,
        out_shape=jax.ShapeDtypeStruct(value.shape, value.dtype),
        name="copied",
    )(value, *earlier)


def total_of(own, arrived):
    for value in arrived:
        own = own + value.astype(f32)
    return own


class Net:
    def __init__(self, dp, tensor):
        self.dp, self.tensor = dp, tensor
        self.chips = dp // 2
        self.rank = lax.axis_index("tensor")
        at = lax.axis_index("dp")
        self.place = jnp.stack([at // 2, at % 2, self.row_shift()]).astype(jnp.int32)

    def over_chips(self, values, k):
        return lax.ppermute(values, "dp", [(i, i ^ (2 * k)) for i in range(self.dp)])

    def over_core(self, values):
        return lax.ppermute(values, "dp", [(i, i ^ 1) for i in range(self.dp)])

    def over_tensor(self, values, k):
        return lax.ppermute(values, "tensor", [(i, i ^ k) for i in range(self.tensor)])

    def gather_chips(self, shard):
        return [shard] + [self.over_chips(shard, k) for k in range(1, self.chips)]

    def gather_cores(self, mine):
        return mine + [self.over_core(piece) for piece in mine]

    def gather_whole(self, shard, axis):
        return lax.all_gather(shard, axis, axis=0, tiled=True)

    def scatter_whole(self, values, axis):
        return lax.psum_scatter(values, axis, scatter_dimension=0, tiled=True).astype(f32)

    def scatter_pairs(self, keep, give):
        pairs = keep + self.over_core(give).astype(f32)
        return pairs[0], [pairs[k].astype(bf16) for k in range(1, self.chips)]

    def over_all_chips(self, others):
        return [self.over_chips(value, k + 1) for k, value in enumerate(others)]

    def row_shift(self):
        return self.rank if self.tensor == 4 else jnp.zeros_like(self.rank)

    def gather_tensor(self, shard):
        if self.tensor != 4:
            return [lax.all_gather(shard, "tensor", axis=0, tiled=True)]
        half = shard.shape[0] // 2
        one, two = self.over_tensor(shard, 1), self.over_tensor(shard, 2)
        return [shard, one, two, self.over_tensor(one[:half], 2), self.over_tensor(two[half:], 1)]

    def scatter_tensor(self, lows, fulls, rows, name, earlier):
        tokens = lows[0].shape[0]
        if self.tensor != 4:
            low, sums = back(self.place, lows, fulls, rows, 0, tokens // BLOCK, bf16, name, earlier)
            return lax.psum_scatter(low, "tensor", scatter_dimension=0, tiled=True).astype(f32), sums
        last, last_sums = back(self.place, lows, fulls, rows, 3, 1, bf16, name + "_last", earlier)
        half = BLOCK // 2
        to_one = self.over_tensor(last[:half], 2)
        to_two = self.over_tensor(last[half:], 1)
        rest, rest_sums = back(self.place, lows, fulls, rows, 0, 3, f32, name, [last])
        own, one, two = jnp.split(rest, 3)
        one = jnp.concatenate([one[:half] + to_one.astype(f32), one[half:]]).astype(bf16)
        two = jnp.concatenate([two[:half], two[half:] + to_two.astype(f32)]).astype(bf16)
        total = own + self.over_tensor(one, 1).astype(f32) + self.over_tensor(two, 2).astype(f32)
        return total, None if rows is None else last_sums + rest_sums

    def branch(self, low, full):
        place = self.place * jnp.array([1, 1, 0], jnp.int32)
        partial, _ = back(place, [low], [full], None, 0, low.shape[0] // BLOCK, bf16, "branch", [])
        return lax.psum_scatter(partial, "tensor", scatter_dimension=0, tiled=True).astype(f32)

    def sum_tensor(self, values):
        total = values
        for k in range(1, self.tensor):
            total = total + self.over_tensor(values, k)
        return total

    def sum_dp(self, values):
        pair = values + self.over_core(values)
        total = pair
        for k in range(1, self.chips):
            total = total + self.over_chips(pair, k)
        return total


def local(
    net_of,
    tokens,
    norm_gain,
    gate_proj,
    inner_proj,
    shared_proj,
    step_proj,
    conv_inner,
    conv_inner_bias,
    conv_shared,
    conv_shared_bias,
    step_bias,
    decay_log,
    skip_gain,
    out_gain,
    out_proj,
    cotangent,
):
    net = net_of()
    place, chips = net.place, net.chips
    straight = place * jnp.array([1, 1, 0], jnp.int32)
    channels = gate_proj.shape[1]
    heads = step_proj.shape[1]
    width = channels + 2 * STATE
    token_rows = tokens.astype(f32)
    inverse = lax.rsqrt(jnp.mean(token_rows * token_rows, axis=-1, keepdims=True) + epsilon)
    unit = token_rows * inverse
    normed_low = (unit * norm_gain).astype(bf16)
    padding = jnp.zeros((step_proj.shape[0], LANES - heads), bf16)
    scan_shard = jnp.concatenate([inner_proj, shared_proj, step_proj, padding], axis=1)
    scan_mine = net.gather_chips(scan_shard)
    row_pieces = net.gather_tensor(normed_low)
    scan_pieces = net.gather_cores(scan_mine)
    reached = scan_mine[1:]
    gate_mine = net.gather_chips(copied(gate_proj, reached + row_pieces[1:3]))
    cot_rows = net.gather_whole(copied(cotangent, reached + row_pieces), "tensor")

    taps = jnp.concatenate(
        [
            jnp.concatenate([conv_inner, conv_inner_bias[None]]),
            jnp.concatenate([conv_shared, conv_shared_bias[None]]),
        ],
        axis=1,
    )
    taps = jnp.pad(taps, ((0, 8 - CONV - 1), (0, 0)))
    rates = -jnp.exp(decay_log)
    head_rows = jnp.pad(jnp.stack([step_bias, rates]), ((0, 6), (0, LANES - heads)))
    skip_row = jnp.repeat(skip_gain, HEAD_DIM)[None]
    gain = out_gain[None]

    raw, scan_full, rows = product(
        place, row_pieces, scan_pieces, raw_epilogue, [], [(width + LANES, f32)], True, "project"
    )
    scanned, pre, states = scan_forward(raw, taps, head_rows, skip_row)
    gate_mine = pinned(gate_mine, [scanned])
    gate_pieces = net.gather_cores(gate_mine)
    outward_mine = net.gather_chips(copied(out_proj.T, gate_mine))
    gate, gated, squares, gate_full = product(
        straight,
        [rows],
        gate_pieces,
        gate_epilogue,
        [(scanned, True)],
        [(channels, f32), (channels, f32), (None, f32)],
        False,
        "gate",
    )
    squares = net.sum_tensor(squares)
    out_low = low_rows(gated, squares, gain)
    out_keep, out_give = weight_grads(place, chips, cot_rows, out_low, "grad_out_proj")
    outward_mine = pinned(outward_mine, [out_give])
    outward_pieces = net.gather_cores(outward_mine)
    grad_out, dots, outward_full = product(
        straight,
        [cot_rows],
        outward_pieces,
        out_epilogue,
        [(gated, True), (gain, False)],
        [(channels, f32), (None, f32)],
        False,
        "grad_out",
    )
    out_own, out_others = net.scatter_pairs(out_keep, out_give)
    out_others = pinned(out_others, outward_mine)
    out_arrived = net.over_all_chips(out_others)
    dots = net.sum_tensor(dots)
    branch = net.branch(out_low, outward_full)
    mixed = (token_rows + branch).astype(bf16)
    gate_back, scan_grad, gain_grad = gating(grad_out, gated, scanned, gate, squares, dots, gain)
    gate_keep, gate_give = weight_grads(place, chips, rows, gate_back, "grad_gate_proj")
    gate_own, gate_others = net.scatter_pairs(gate_keep, gate_give)
    carried = scan_backward(
        0, raw, pre, scan_grad, states, taps, head_rows, skip_row, None, gate_others
    )
    out_arrived = pinned(out_arrived, [carried[1]])
    grad_out_proj = total_of(out_own, out_arrived)
    gate_arrived = net.over_all_chips(pinned(gate_others, out_arrived))
    scan_back, sums, head_sums, _, _ = scan_backward(
        1, raw, pre, scan_grad, states, taps, head_rows, skip_row, carried, out_arrived
    )
    scan_keep, scan_give = weight_grads(
        place, chips, rows, scan_back, "grad_scan_proj", gate_arrived
    )
    scan_own, scan_others = net.scatter_pairs(scan_keep, scan_give)
    grad_gate_proj = total_of(gate_own, gate_arrived)
    scan_arrived = net.over_all_chips(scan_others)
    grad_scan_proj = total_of(scan_own, scan_arrived)
    grad_normed, norm_sums = net.scatter_tensor(
        [gate_back, scan_back], [gate_full, scan_full], rows, "grad_normed", [scan_give]
    )
    grad_out_proj = grad_out_proj.T
    grad_inner_proj = grad_scan_proj[:, :channels]
    grad_shared_proj = net.sum_tensor(grad_scan_proj[:, channels:width])
    grad_step_proj = grad_scan_proj[:, width : width + heads]
    grad_norm_gain = jnp.sum(norm_sums, axis=0) / norm_gain
    spread = grad_normed * norm_gain
    grad_tokens = (
        cotangent.astype(f32)
        + inverse * spread
        - unit * (inverse * jnp.mean(spread * unit, axis=-1, keepdims=True))
    )
    own = (
        sums[:CONV, :channels],
        sums[CONV, :channels],
        gain_grad[0],
        head_sums[0, :heads],
        head_sums[1, :heads] * rates,
        jnp.sum(sums[CONV + 1, :channels].reshape(heads, HEAD_DIM), axis=1),
    )
    common = (sums[:CONV, channels:], sums[CONV, channels:], grad_norm_gain)
    common_flat = net.sum_tensor(jnp.concatenate([v.reshape(-1) for v in common]))
    flat = net.sum_dp(jnp.concatenate([v.reshape(-1) for v in own] + [common_flat]))
    small = []
    start = 0
    for v in own + common:
        small.append(flat[start : start + v.size].reshape(v.shape))
        start += v.size
    (
        grad_conv_inner,
        grad_conv_inner_bias,
        grad_out_gain,
        grad_step_bias,
        grad_decay_log,
        grad_skip_gain,
        grad_conv_shared,
        grad_conv_shared_bias,
        grad_norm_gain,
    ) = small
    return (
        mixed,
        grad_tokens,
        grad_norm_gain,
        grad_gate_proj,
        grad_inner_proj,
        grad_shared_proj,
        grad_step_proj,
        grad_conv_inner,
        grad_conv_inner_bias,
        grad_conv_shared,
        grad_conv_shared_bias,
        grad_step_bias,
        grad_decay_log,
        grad_skip_gain,
        grad_out_gain,
        grad_out_proj,
    )


def solution(mesh):
    dp, tensor = mesh.shape["dp"], mesh.shape["tensor"]

    def on_device(*args):
        return local(lambda: Net(dp, tensor), *args)

    return jax.shard_map(
        on_device,
        mesh=mesh,
        in_specs=(
            P(("dp", "tensor"), None),
            P(),
            P("dp", "tensor"),
            P("dp", "tensor"),
            P("dp", None),
            P("dp", "tensor"),
            P(None, "tensor"),
            P("tensor"),
            P(),
            P(),
            P("tensor"),
            P("tensor"),
            P("tensor"),
            P("tensor"),
            P("tensor", "dp"),
            P(("dp", "tensor"), None),
        ),
        out_specs=(
            P(("dp", "tensor"), None),
            P(("dp", "tensor"), None),
            P(),
            P("dp", "tensor"),
            P("dp", "tensor"),
            P("dp", None),
            P("dp", "tensor"),
            P(None, "tensor"),
            P("tensor"),
            P(),
            P(),
            P("tensor"),
            P("tensor"),
            P("tensor"),
            P("tensor"),
            P("tensor", "dp"),
        ),
        check_vma=False,
    )
```

```python
import functools

import jax
import jax.numpy as jnp
from jax import lax
from jax.experimental import pallas as pl
from jax.experimental.pallas import tpu as pltpu
from jax.sharding import PartitionSpec as P

DI = 3072
epsilon = 1e-05
HEAD_DIM = 64
STATE = 128
CONV = 4
SEQ = 1024
SPAN = 256
CHUNK = 128
LANES = 128
NEVER = -1e30
NEAR = jax.ShapeDtypeStruct
f32 = jnp.float32
bf16 = jnp.bfloat16
highest = lax.Precision.HIGHEST


def dot(first, second, first_dim=1, second_dim=0, precision=None):
    return lax.dot_general(
        first,
        second,
        (((first_dim,), (second_dim,)), ((), ())),
        precision=precision,
        preferred_element_type=f32,
    )


def sigmoid(values):
    return 0.5 * jnp.tanh(0.5 * values) + 0.5


def places(dim):
    return lax.broadcasted_iota(jnp.int32, (CHUNK, LANES), dim)


def decays(step_raw, heads_ref):
    raw = step_raw + heads_ref[0:1]
    small = jnp.exp(-jnp.abs(raw))
    log_one = jnp.where(small < 1e-3, small - 0.5 * small * small, jnp.log(1.0 + small))
    steps = jnp.maximum(raw, 0.0) + log_one
    upto = (places(0) >= places(1)).astype(f32)
    summed = dot(upto, steps * heads_ref[1:2], precision=highest)
    return steps, sigmoid(raw), summed, summed - jnp.log(steps)


def pair_of(first, second):
    return jnp.concatenate([first, second], axis=0)


def forward_kernel(raw_ref, taps_ref, heads_ref, skip_ref, *refs):
    scanned_ref, pre_ref, states_ref, state, before = refs[-5:]
    chunk = pl.program_id(0)
    channels = skip_ref.shape[1]
    width = channels + 2 * STATE

    @pl.when(chunk % (SEQ // CHUNK) == 0)
    def _():
        state[...] = jnp.zeros_like(state)
        before[...] = jnp.zeros_like(before)

    raw = raw_ref[:, :width]
    extended = jnp.concatenate([before[...], raw], axis=0)
    pre = taps_ref[CONV : CONV + 1] + taps_ref[CONV - 1 : CONV] * raw
    for tap in range(CONV - 1):
        start = 8 - (CONV - 1) + tap
        pre = pre + taps_ref[tap : tap + 1] * extended[start : start + CHUNK]
    before[...] = raw[CHUNK - 8 :]
    pre_ref[...] = pre
    act = (pre * sigmoid(pre)).astype(bf16)
    writes = act[:, channels : channels + STATE]
    reads = act[:, channels + STATE :]
    _, _, summed, shifted = decays(raw_ref[:, width:], heads_ref)
    summed_t, shifted_t = summed.T, shifted.T
    tail_t = jnp.exp(summed_t[:, CHUNK - 1 :] - shifted_t)
    scores = dot(reads, writes, 1, 1)
    writes_t = writes.astype(f32).T
    causal = places(0) >= places(1)
    left = places(1) < HEAD_DIM
    states_ref[...] = state[...].astype(bf16)
    for pair in range(channels // LANES):
        cols = slice(pair * LANES, (pair + 1) * LANES)
        values = act[:, cols].astype(f32)
        both = pair_of(jnp.where(left, values, 0.0), jnp.where(left, 0.0, values)).astype(bf16)
        mixes, tails, grown = [], [], []
        for head in (2 * pair, 2 * pair + 1):
            here = jnp.broadcast_to(summed[:, head : head + 1], (CHUNK, LANES))
            decay = jnp.exp(jnp.where(causal, here - shifted_t[head : head + 1], NEVER))
            mixes.append((scores * decay).astype(bf16))
            tails.append((writes_t * tail_t[head : head + 1]).astype(bf16))
            grown.append(here)
        stacked = pair_of(jnp.concatenate(mixes, axis=1), jnp.concatenate(tails, axis=1))
        out = dot(stacked, both)
        entering = state[:, cols]
        factor = jnp.exp(jnp.where(left, grown[0], grown[1]))
        across = dot(reads, entering.astype(bf16)) * factor
        scanned_ref[:, cols] = out[:CHUNK] + across + values * skip_ref[:, cols]
        state[:, cols] = entering * factor[CHUNK - 1 :] + out[CHUNK:]


def backward_kernel(part, n_deps, *refs):
    raw_ref, pre_ref, grad_ref, states_ref, taps_ref, heads_ref, skip_ref = refs[:7]
    n_held = 5 if part else 0
    held, refs = refs[7 : 7 + n_held], refs[7 + n_held + n_deps :]
    low_ref, sums_ref, head_sums_ref, carry, after, wide = refs
    step = pl.program_id(0)
    channels = skip_ref.shape[1]
    width = channels + 2 * STATE

    @pl.when(step == 0)
    def _():
        if part:
            for ref, source in zip((sums_ref, head_sums_ref, carry, after), held[1:], strict=True):
                ref[...] = source[...]
        else:
            sums_ref[...] = jnp.zeros_like(sums_ref)
            head_sums_ref[...] = jnp.zeros_like(head_sums_ref)

    @pl.when((step + part * pl.num_programs(0)) % (SEQ // CHUNK) == 0)
    def _():
        carry[...] = jnp.zeros_like(carry)
        after[...] = jnp.zeros_like(after)

    pre = pre_ref[...]
    gate = sigmoid(pre)
    act = (pre * gate).astype(bf16)
    writes = act[:, channels : channels + STATE]
    reads = act[:, channels + STATE :]
    steps, slopes, summed, shifted = decays(raw_ref[:, width:], heads_ref)
    summed_t = summed.T
    scores_t = dot(writes, reads, 1, 1)
    causal = places(0) <= places(1)
    earlier = places(0) < places(1)
    suffix = (places(0) >= places(1)).astype(bf16)
    left = places(1) < HEAD_DIM
    score_grads = jnp.zeros((CHUNK, LANES), f32)
    spans, inner_grads = [], []
    for pair in range(channels // LANES):
        cols = slice(pair * LANES, (pair + 1) * LANES)
        values = act[:, cols].astype(f32)
        both = pair_of(jnp.where(left, values, 0.0), jnp.where(left, 0.0, values)).astype(bf16)
        grad_low = grad_ref[:, cols]
        grad = grad_low.astype(f32)
        grad_both = pair_of(jnp.where(left, grad, 0.0), jnp.where(left, 0.0, grad)).astype(bf16)
        products = dot(both, grad_low, 1, 1)
        mixes, crossing, grown, tails = [], [], [], []
        for place, head in enumerate((2 * pair, 2 * pair + 1)):
            here = jnp.broadcast_to(shifted[:, head : head + 1], (CHUNK, LANES))
            decay = jnp.exp(jnp.where(causal, summed_t[head : head + 1] - here, NEVER))
            product = products[place * CHUNK : (place + 1) * CHUNK]
            score_grads = score_grads + decay * product
            mix = scores_t * decay
            mixes.append(mix.astype(bf16))
            crossing.append((mix * product).astype(bf16))
            level = jnp.broadcast_to(summed[:, head : head + 1], (CHUNK, LANES))
            grown.append(level)
            tails.append(level[CHUNK - 1 :] - here)
        sums = dot(pair_of(*crossing), suffix)
        for place in range(2):
            piece = jnp.where(earlier, sums[place * CHUNK : (place + 1) * CHUNK], 0.0)
            spans.append(jnp.sum(piece, axis=0, keepdims=True))
        within = dot(jnp.concatenate(mixes, axis=1), grad_both)
        factor = jnp.exp(jnp.where(left, grown[0], grown[1]))
        tail = jnp.exp(jnp.where(left, tails[0], tails[1]))
        leaving = carry[:, cols]
        entering = states_ref[:, cols]
        later = tail * dot(writes, leaving.astype(bf16))
        both_grads = within + later
        inner_grads.append(both_grads + skip_ref[:, cols] * grad)
        spread = factor * grad
        spread_low = spread.astype(bf16)
        wide[0:CHUNK, cols] = spread_low
        wide[CHUNK : 2 * CHUNK, cols] = (tail * values).astype(bf16)
        wide[2 * CHUNK : 3 * CHUNK, cols] = (spread * dot(reads, entering)).astype(bf16)
        wide[3 * CHUNK : 4 * CHUNK, cols] = (values * later).astype(bf16)
        wide[4 * CHUNK : 5 * CHUNK, cols] = (values * both_grads).astype(bf16)
        held = jnp.sum(entering.astype(f32) * leaving, axis=0, keepdims=True) * factor[CHUNK - 1 :]
        sums_ref[CONV + 1 : CONV + 2, cols] += jnp.sum(grad * values, axis=0, keepdims=True)
        sums_ref[CONV + 2 : CONV + 3, cols] = held
    reads_t = reads.astype(f32).T.astype(bf16)
    score_low = score_grads.astype(bf16)
    spread_all = wide[0:CHUNK, :]
    read_grads = dot(score_low, writes, 0, 0) + dot(spread_all, states_ref[...], 1, 1)
    write_grads = dot(score_low, reads) + dot(wide[CHUNK : 2 * CHUNK, :], carry[...].astype(bf16), 1, 1)
    last = jnp.exp(summed[CHUNK - 1 :])
    of_head = (
        lax.broadcasted_iota(jnp.int32, (channels, LANES), 0) // HEAD_DIM
        == lax.broadcasted_iota(jnp.int32, (channels, LANES), 1)
    )
    reduced = dot(wide[2 * CHUNK : 5 * CHUNK, :], of_head.astype(bf16))
    held_rows = jnp.broadcast_to(sums_ref[CONV + 2 : CONV + 3, :channels], (8, channels))
    held_heads = dot(held_rows, of_head.astype(f32), precision=highest)[0:1]
    lasts = dot(jnp.broadcast_to(last, (8, LANES)), of_head.astype(f32), 1, 1, precision=highest)[0:1]
    carry[...] = carry[...] * lasts + dot(reads_t, spread_all)
    across_sums, later_sums, both_sums = reduced[:CHUNK], reduced[CHUNK : 2 * CHUNK], reduced[2 * CHUNK :]
    span_rows = jnp.concatenate(spans + [jnp.zeros((LANES - len(spans), LANES), f32)], axis=0)
    log_grads = (
        dot((places(0) <= places(1)).astype(f32), across_sums, precision=highest)
        + dot((places(0) > places(1)).astype(f32), later_sums, precision=highest)
        + span_rows.T
        + held_heads
    )
    ratio = jnp.where(steps > 1e-30, slopes / steps, 1.0)
    step_grads = both_sums * ratio + heads_ref[1:2] * log_grads * slopes
    head_sums_ref[0:1] += jnp.sum(step_grads, axis=0, keepdims=True)
    head_sums_ref[1:2] += jnp.sum(log_grads * steps, axis=0, keepdims=True)

    @pl.when(part * pl.num_programs(0) + step == 2 * pl.num_programs(0) - 1)
    def _():
        skip_rows = jnp.broadcast_to(sums_ref[CONV + 1 : CONV + 2, :channels], (8, channels))
        head_sums_ref[2:3] = dot(skip_rows, of_head.astype(f32), precision=highest)[0:1]

    raw = raw_ref[:, :width]
    act_grads = jnp.concatenate(inner_grads + [write_grads, read_grads], axis=1)
    pre_grads = act_grads * (gate * (1.0 + pre * (1.0 - gate)))
    extended = jnp.concatenate([pre_grads, after[...]], axis=0)
    after[...] = pre_grads[:8]
    sums_ref[CONV : CONV + 1] += jnp.sum(pre_grads, axis=0, keepdims=True)
    raw_grads = taps_ref[CONV - 1 : CONV] * pre_grads
    sums_ref[CONV - 1 : CONV] += jnp.sum(raw * pre_grads, axis=0, keepdims=True)
    for tap in range(CONV - 1):
        moved = extended[CONV - 1 - tap : CONV - 1 - tap + CHUNK]
        raw_grads = raw_grads + taps_ref[tap : tap + 1] * moved
        sums_ref[tap : tap + 1] += jnp.sum(raw * moved, axis=0, keepdims=True)
    low_ref[:, :width] = raw_grads.astype(bf16)
    low_ref[:, width:] = step_grads.astype(bf16)


def stay(values):
    return pltpu.with_memory_space_constraint(values, pltpu.HBM)


def scan_forward(raw, taps, heads, skip, earlier):
    tokens, full = raw.shape
    channels = skip.shape[1]
    width = channels + 2 * STATE
    count = tokens // CHUNK
    by_chunk = lambda shape: pl.BlockSpec(shape, lambda s: (s, 0))
    whole = lambda v: pl.BlockSpec(v.shape, lambda s: (0, 0))
    return pl.pallas_call(
        forward_kernel,
        grid=(count,),
        in_specs=[by_chunk((CHUNK, full)), whole(taps), whole(heads), whole(skip)]
        + [pl.BlockSpec(memory_space=pl.ANY)] * len(earlier),
        out_specs=[
            by_chunk((CHUNK, channels)),
            by_chunk((CHUNK, width)),
            by_chunk((STATE, channels)),
        ],
        scratch_shapes=[pltpu.VMEM((STATE, channels), f32), pltpu.VMEM((8, width), f32)],
        out_shape=[
            pltpu.HBM((tokens, channels), f32),
            pltpu.HBM((tokens, width), f32),
            pltpu.HBM((count * STATE, channels), bf16),
        ],
        compiler_params=pltpu.CompilerParams(vmem_limit_bytes=20 << 20),
        name="scan_forward",
    )(stay(raw), taps, heads, skip, *earlier)


def scan_backward(part, raw, pre, grad, states, taps, heads, skip, held, earlier):
    tokens, full = raw.shape
    channels = skip.shape[1]
    width = channels + 2 * STATE
    count = tokens // CHUNK
    half = count // 2
    last = count - 1 - part * half
    by_chunk = lambda shape: pl.BlockSpec(shape, lambda s: (last - s, 0))
    whole = lambda shape: pl.BlockSpec(shape, lambda s: (0, 0))
    kept = [(8, width), (8, LANES), (STATE, channels), (8, width)]
    free = pl.BlockSpec(memory_space=pl.ANY)
    held = list(held) if part else []
    return pl.pallas_call(
        functools.partial(backward_kernel, part, len(earlier)),
        grid=(half,),
        in_specs=[
            by_chunk((CHUNK, full)),
            by_chunk((CHUNK, width)),
            by_chunk((CHUNK, channels)),
            by_chunk((STATE, channels)),
            whole(taps.shape),
            whole(heads.shape),
            whole(skip.shape),
        ]
        + ([free] + [whole(shape) for shape in kept] if part else [])
        + [free] * len(earlier),
        out_specs=[by_chunk((CHUNK, full))] + [whole(shape) for shape in kept],
        scratch_shapes=[pltpu.VMEM((5 * CHUNK, channels), bf16)],
        out_shape=[pltpu.HBM((tokens, full), bf16)] + [pltpu.HBM(shape, f32) for shape in kept],
        input_output_aliases={7: 0} if part else {},
        compiler_params=pltpu.CompilerParams(vmem_limit_bytes=20 << 20),
        name=f"scan_backward_{part}",
    )(stay(raw), stay(pre), stay(grad), stay(states), taps, heads, skip, *[stay(v) for v in held], *earlier)


BLOCK = 256
LIMIT = 24 << 20
SMALL = 16
anywhere = pl.BlockSpec(memory_space=pl.ANY)
in_vmem = pl.BlockSpec(memory_space=pltpu.VMEM)


def column_sums(values, count):
    rows = [
        jnp.sum(values[i * LANES : (i + 1) * LANES].T, axis=0, keepdims=True)
        for i in range(count // LANES)
    ]
    return jnp.concatenate(rows, axis=0)


def fold(values):
    total = values[:, :LANES]
    for start in range(LANES, values.shape[1], LANES):
        total = total + values[:, start : start + LANES]
    return total


def shard_rows(place, index, chips, height):
    core, chip = index // chips, index % chips
    return pl.multiple_of(((place[0] ^ chip) * 2 + (place[1] ^ core)) * height, height)


def row_start(place, start):
    if isinstance(start, int):
        return pl.multiple_of((start // BLOCK ^ place[2]) * BLOCK + start % BLOCK, LANES)
    return pl.multiple_of((start // BLOCK ^ place[2]) * BLOCK, BLOCK)


def product_kernel(layout, chips, epilogue, place, *refs):
    heights, keep_rows, n_extra, n_deps, n_out = layout
    n_rows, n_full = len(heights), 2 * chips
    row_refs, refs = refs[:n_rows], refs[n_rows:]
    full_refs, refs = refs[:n_full], refs[n_full:]
    extra, refs = refs[:n_extra], refs[n_extra + n_deps :]
    outs, refs = refs[:n_out], refs[n_out:]
    full_out, refs = refs[0], refs[1:]
    if keep_rows:
        rows_out, refs = refs[0], refs[1:]
    rows, full, sems, back = refs
    step = pl.program_id(0)
    starts = [sum(heights[:i]) for i in range(n_rows)]
    shard = full.shape[0] // n_full
    row_copies = [
        pltpu.make_async_copy(
            row_refs[i], rows.at[pl.ds(row_start(place, starts[i]), heights[i])], sems.at[i]
        )
        for i in range(n_rows)
    ]
    full_copies = [
        pltpu.make_async_copy(
            full_refs[i], full.at[pl.ds(shard_rows(place, i, chips, shard), shard)], sems.at[n_rows + i]
        )
        for i in range(n_full)
    ]
    backs = [pltpu.make_async_copy(full, full_out, back.at[0])]

    @pl.when(step == 0)
    def _():
        for copy in full_copies + row_copies:
            copy.start()
        for copy in full_copies:
            copy.wait()
        backs[0].start()

    for i in range(n_rows):

        @pl.when(step == starts[i] // BLOCK)
        def _(i=i):
            row_copies[i].wait()

    if keep_rows:
        backs.append(pltpu.make_async_copy(rows, rows_out, back.at[1]))

        @pl.when(step == starts[-1] // BLOCK)
        def _():
            backs[1].start()

    block = rows[pl.ds(row_start(place, step * BLOCK), BLOCK), :]
    epilogue(step ^ place[2], block, full, extra, outs)

    @pl.when(step == pl.num_programs(0) - 1)
    def _():
        for copy in backs:
            copy.wait()


def product(place, row_pieces, full_pieces, epilogue, extra, outs, name, earlier=()):
    chips = len(full_pieces) // 2
    heights = tuple(piece.shape[0] for piece in row_pieces)
    tokens, depth = sum(heights), row_pieces[0].shape[1]
    columns = full_pieces[0].shape[1]
    by_block = lambda cols: pl.BlockSpec((BLOCK, cols), lambda s, p: (s ^ p[2], 0))
    whole = lambda shape: pl.BlockSpec(shape, lambda s, p: (0, 0))
    out_specs, out_shape = [], []
    for cols, dtype in outs:
        if cols is None:
            out_specs.append(whole((dtype * tokens // LANES, LANES)))
            out_shape.append(jax.ShapeDtypeStruct((dtype * tokens // LANES, LANES), f32))
        else:
            out_specs.append(by_block(cols))
            out_shape.append((pltpu.HBM if name == "project" else NEAR)((tokens, cols), dtype))
    out_specs += [anywhere, anywhere]
    out_shape += [pltpu.HBM((depth, columns), bf16), pltpu.HBM((tokens, depth), bf16)]
    layout = (heights, True, len(extra), len(earlier), len(outs))
    return pl.pallas_call(
        functools.partial(product_kernel, layout, chips, epilogue),
        grid_spec=pltpu.PrefetchScalarGridSpec(
            num_scalar_prefetch=1,
            grid=(tokens // BLOCK,),
            in_specs=[anywhere] * (len(row_pieces) + len(full_pieces))
            + [by_block(v.shape[1]) if by else whole(v.shape) for v, by in extra]
            + [anywhere] * len(earlier),
            out_specs=out_specs,
            scratch_shapes=[
                pltpu.VMEM((tokens, depth), bf16),
                pltpu.VMEM((depth, columns), bf16),
                pltpu.SemaphoreType.DMA((len(row_pieces) + len(full_pieces),)),
                pltpu.SemaphoreType.DMA((2,)),
            ],
        ),
        out_shape=out_shape,
        compiler_params=pltpu.CompilerParams(vmem_limit_bytes=LIMIT),
        name=name,
    )(place, *[stay(v) for v in row_pieces + full_pieces], *[v for v, _ in extra], *earlier)


def slices(columns):
    return [slice(start, min(start + 256, columns)) for start in range(0, columns, 256)]


def raw_epilogue(index, block, full, extra, outs):
    (raw,) = outs
    for cols in slices(raw.shape[1]):
        raw[:, cols] = dot(block, full[:, cols])


def mix_epilogue(index, block, full, extra, outs):
    rows, scanned, gain = extra
    gate, gated, grad, sums = outs
    channels = gate.shape[1]
    squares = jnp.zeros((BLOCK, LANES), f32)
    dots = jnp.zeros((BLOCK, LANES), f32)
    for cols in slices(channels):
        value = dot(rows[...], full[:, cols])
        out = dot(block, full[:, channels + cols.start : channels + cols.stop])
        gate[:, cols] = value
        grad[:, cols] = out
        product = scanned[:, cols] * (value * sigmoid(value))
        gated[:, cols] = product
        squares = squares + fold(product * product)
        dots = dots + fold(out * gain[:, cols] * product)
    per = BLOCK // LANES
    half = sums.shape[0] // 2
    sums[pl.ds(index * per, per), :] = column_sums(squares, BLOCK)
    sums[pl.ds(half + index * per, per), :] = column_sums(dots, BLOCK)


def shard_kernel(gate_proj, out_proj, *refs):
    out = refs[-1]
    channels, height = out_proj.shape
    out[:, :channels] = gate_proj[...]
    place = [lax.broadcasted_iota(jnp.int32, (height, height), dim) for dim in range(2)]
    same = (place[0] == place[1]).astype(bf16)
    out[:, channels:] = dot(same, out_proj[...], 1, 1).astype(bf16)


def joint_shard(gate_proj, out_proj, earlier):
    return pl.pallas_call(
        shard_kernel,
        in_specs=[in_vmem] * 2 + [anywhere] * len(earlier),
        out_specs=in_vmem,
        out_shape=jax.ShapeDtypeStruct((gate_proj.shape[0], 2 * gate_proj.shape[1]), bf16),
        name="joint_shard",
    )(gate_proj, out_proj, *earlier)


def columns_of(row):
    return jnp.broadcast_to(row, (LANES, LANES)).T


def gating_kernel(grad_out, gated, scanned, gate, sums, gain, out_low, gate_back, scan_grad, gain_grad):
    step = pl.program_id(0)
    half = sums.shape[0] // 2

    @pl.when(step == 0)
    def _():
        gain_grad[...] = jnp.zeros_like(gain_grad)

    for part in range(BLOCK // LANES):
        rows = slice(part * LANES, (part + 1) * LANES)
        index = step * (BLOCK // LANES) + part
        ratio_row = lax.rsqrt(sums[pl.ds(index, 1), :] / DI + epsilon)
        dots = sums[pl.ds(half + index, 1), :]
        ratio = columns_of(ratio_row)
        pull = columns_of(ratio_row * ratio_row * ratio_row / DI * dots)
        for start in range(0, gate.shape[1], LANES):
            cols = slice(start, start + LANES)
            held, value = gated[rows, cols], gate[rows, cols]
            scaled = grad_out[rows, cols] * ratio
            out_low[rows, cols] = (gain[:, cols] * (held * ratio)).astype(bf16)
            gain_grad[0:1, cols] += jnp.sum(scaled * held, axis=0, keepdims=True)
            grad = gain[:, cols] * scaled - held * pull
            slope = sigmoid(value)
            scan_grad[rows, cols] = (grad * (value * slope)).astype(bf16)
            gate_grad = grad * scanned[rows, cols] * (slope * (1.0 + value * (1.0 - slope)))
            gate_back[rows, cols] = gate_grad.astype(bf16)


def gating(grad_out, gated, scanned, gate, sums, gain):
    tokens, columns = gated.shape
    block = pl.BlockSpec((BLOCK, columns), lambda s: (s, 0))
    whole = lambda v: pl.BlockSpec(v.shape, lambda s: (0, 0))
    return pl.pallas_call(
        gating_kernel,
        grid=(tokens // BLOCK,),
        in_specs=[block] * 4 + [whole(sums), whole(gain)],
        out_specs=[block] * 3 + [pl.BlockSpec((8, columns), lambda s: (0, 0))],
        out_shape=[NEAR((tokens, columns), bf16)] * 3 + [jax.ShapeDtypeStruct((8, columns), f32)],
        compiler_params=pltpu.CompilerParams(vmem_limit_bytes=LIMIT),
        name="gating",
    )(grad_out, gated, stay(scanned), gate, sums, gain)


def grads_kernel(n_rows, place, *refs):
    rows, lows = refs[:n_rows], refs[n_rows : 2 * n_rows]
    keep, give, acc = refs[-3:]
    wide = acc.shape[0]
    shard = wide // 2
    start = 0
    for row, low in zip(rows, lows, strict=True):
        for cols in slices(low.shape[1]):
            acc[:, start + cols.start : start + cols.stop] = dot(row[...], low[:, cols], 0, 0)
        start += low.shape[1]
    mine, other = (pl.multiple_of(core * shard, shard) for core in (place[1], 1 - place[1]))
    keep[0, :shard] = acc[pl.ds(mine, shard), :].astype(bf16)
    give[0, :shard] = acc[pl.ds(other, shard), :].astype(bf16)


def fill_small(small, sums, gain_grad, norm_grad, head_sums):
    rest = norm_grad.shape[1] - small.shape[1]
    small[...] = jnp.zeros_like(small)
    small[0:8, : sums.shape[1]] = sums[...]
    small[8:9, : gain_grad.shape[1]] = gain_grad[0:1, :]
    small[9:10, :] = norm_grad[0:1, : small.shape[1]]
    small[10:11, :rest] = norm_grad[0:1, small.shape[1] :]
    small[11:14, :LANES] = head_sums[0:3, :]


def small_kernel(n_rows, place, *refs):
    keep, give, small = refs[-4], refs[-3], refs[-1]
    grads_kernel(n_rows, place, *refs[:-1])
    fill_small(small, *refs[2 * n_rows : 2 * n_rows + 4])
    low = small[...].astype(bf16)
    shard = keep.shape[1] - SMALL
    keep[0, shard:] = low
    give[0, shard:] = low


def whole_grads_kernel(chips, n_rows, n_small, place, *refs):
    rows, lows = refs[:n_rows], refs[n_rows : 2 * n_rows]
    keep, give, acc, small = refs[-4:]
    depth = acc.shape[0]
    shard = depth // (2 * chips)
    start = 0
    for row, low in zip(rows, lows, strict=True):
        cols = slice(start, start + low.shape[1])
        for lanes in slices(depth):
            acc[lanes, cols] = dot(row[:, lanes], low[...], 0, 0)
        start = cols.stop
    for k in range(chips):
        for out, core in ((keep, place[1]), (give, 1 - place[1])):
            at = pl.multiple_of(((place[0] ^ k) * 2 + core) * shard, shard)
            out[k, :shard] = acc[pl.ds(at, shard), :].astype(bf16)
    if n_small:
        fill_small(small, *refs[2 * n_rows : 2 * n_rows + n_small])
        for k in range(chips):
            keep[k, shard:] = small[...].astype(bf16)
            give[k, shard:] = small[...].astype(bf16)


def weight_grads(place, chips, rows, lows, small, name, earlier=()):
    tokens, depth = rows[0].shape
    columns = sum(v.shape[1] for v in lows)
    wide = depth // chips
    shard = wide // 2
    height = shard + (SMALL if small else 0)
    if wide % LANES:
        return pl.pallas_call(
            functools.partial(whole_grads_kernel, chips, len(rows), len(small)),
            in_specs=[pl.BlockSpec(memory_space=pltpu.SMEM)]
            + [in_vmem] * (2 * len(rows) + len(small))
            + [anywhere] * len(earlier),
            out_specs=[in_vmem] * 2,
            out_shape=[jax.ShapeDtypeStruct((chips, height, columns), bf16)] * 2,
            scratch_shapes=[pltpu.VMEM((depth, columns), f32), pltpu.VMEM((SMALL, columns), f32)],
            compiler_params=pltpu.CompilerParams(vmem_limit_bytes=2 * LIMIT),
            name=name,
        )(place, *rows, *lows, *small, *earlier)
    out = pl.BlockSpec((1, height, columns), lambda k, p: (k, 0, 0))
    whole = lambda v: pl.BlockSpec(v.shape, lambda k, p: (0, 0))
    return pl.pallas_call(
        functools.partial(small_kernel if small else grads_kernel, len(rows)),
        grid_spec=pltpu.PrefetchScalarGridSpec(
            num_scalar_prefetch=1,
            grid=(chips,),
            in_specs=[pl.BlockSpec((tokens, wide), lambda k, p: (0, k ^ p[0]))] * len(rows)
            + [whole(v) for v in lows]
            + [whole(v) for v in small]
            + [anywhere] * len(earlier),
            out_specs=[out, out],
            scratch_shapes=[pltpu.VMEM((wide, columns), f32)]
            + ([pltpu.VMEM((SMALL, columns), f32)] if small else []),
        ),
        out_shape=[jax.ShapeDtypeStruct((chips, height, columns), bf16)] * 2,
        compiler_params=pltpu.CompilerParams(vmem_limit_bytes=LIMIT),
        name=name,
    )(place, *[stay(v) for v in rows], *lows, *small, *earlier)


def pairs_kernel(chips, *refs):
    keep, come, own, others = refs[0], refs[1], refs[-chips], refs[1 - chips :]
    own[...] = keep[0].astype(f32) + come[0].astype(f32)
    for k in range(1, chips):
        others[k - 1][...] = (keep[k].astype(f32) + come[k].astype(f32)).astype(bf16)


def pairs(keep, come, earlier=()):
    chips, rows, columns = keep.shape
    out = pl.pallas_call(
        functools.partial(pairs_kernel, chips),
        in_specs=[in_vmem, in_vmem] + [anywhere] * len(earlier),
        out_specs=[in_vmem] * chips,
        out_shape=[pltpu.HBM((rows, columns), f32)] + [pltpu.HBM((rows, columns), bf16)] * (chips - 1),
        compiler_params=pltpu.CompilerParams(vmem_limit_bytes=LIMIT),
        name="pairs",
    )(keep, come, *earlier)
    return out[0], list(out[1:])


def back_kernel(count, with_rows, place, *refs):
    lows, fulls, refs = refs[:count], refs[count : 2 * count], refs[2 * count :]
    rows, out, sums = (refs[0], refs[-2], refs[-1]) if with_rows else (None, refs[-1], None)
    if with_rows:

        @pl.when(pl.program_id(0) == 0)
        def _():
            sums[...] = jnp.zeros_like(sums)

    for cols in slices(out.shape[1]):
        value = dot(lows[0][...], fulls[0][cols, :], 1, 1)
        for low, full in zip(lows[1:], fulls[1:], strict=True):
            value = value + dot(low[...], full[cols, :], 1, 1)
        out[:, cols] = value.astype(bf16)
        if with_rows:
            sums[0:1, cols] += jnp.sum(value * rows[:, cols].astype(f32), axis=0, keepdims=True)


def back(place, lows, fulls, rows, name, earlier=()):
    tokens, depth = lows[0].shape[0], fulls[0][0].shape[0]
    by_block = lambda cols: pl.BlockSpec((BLOCK, cols), lambda s, p: (s ^ p[2], 0))
    whole = lambda shape: pl.BlockSpec(shape, lambda s, p: (0, 0))
    columns = lambda cols, i: pl.BlockSpec((depth, cols), lambda s, p: (0, i))
    extra = [] if rows is None else [stay(rows)]
    out = pl.pallas_call(
        functools.partial(back_kernel, len(lows), rows is not None),
        grid_spec=pltpu.PrefetchScalarGridSpec(
            num_scalar_prefetch=1,
            grid=(tokens // BLOCK,),
            in_specs=[by_block(v.shape[1]) for v in lows]
            + [columns(v.shape[1], i) for v, (_, i) in zip(lows, fulls, strict=True)]
            + [by_block(depth) for _ in extra]
            + [anywhere] * len(earlier),
            out_specs=[pl.BlockSpec((BLOCK, depth), lambda s, p: (s, 0))] + [whole((8, depth)) for _ in extra],
        ),
        out_shape=[jax.ShapeDtypeStruct((tokens, depth), bf16)]
        + [jax.ShapeDtypeStruct((8, depth), f32) for _ in extra],
        compiler_params=pltpu.CompilerParams(vmem_limit_bytes=LIMIT),
        name=name,
    )(place, *lows, *[stay(v) for v, _ in fulls], *extra, *earlier)
    return out[0], out[1] if extra else None


def add_up(parts, rows, cols):
    value = parts[0][rows, cols].astype(f32)
    for part in parts[1:]:
        value = value + part[rows, cols].astype(f32)
    return value


def collect_kernel(count, n_deps, *refs):
    parts = refs[:count]
    inner, step, taps, bias, gain, heads, common, rest = refs[count + n_deps :]
    shard, channels = inner.shape
    full = parts[0].shape[1]
    own = slice(0, shard)
    for start in range(0, channels, 256):
        cols = slice(start, min(start + 256, channels))
        inner[:, cols] = add_up(parts, own, cols)
    step[...] = add_up(parts, own, slice(full - LANES, full))
    shared = slice(channels, channels + 2 * STATE)
    common[0:shard] = add_up(parts, own, shared).astype(bf16)
    small = add_up(parts, slice(shard, shard + SMALL), slice(0, full))
    taps[...] = small[0:CONV, :channels]
    bias[...] = small[CONV : CONV + 1, :channels]
    gain[...] = small[8:9, :channels]
    heads[...] = jnp.zeros_like(heads)
    heads[0:3] = small[11:14, :LANES]
    rest[...] = jnp.zeros_like(rest)
    rest[0:8] = small[0:8, shared]
    for piece in range(12):
        row, start = divmod(piece * LANES, full)
        target = slice(piece % 2 * LANES, (piece % 2 + 1) * LANES)
        rest[8 + piece // 2 : 9 + piece // 2, target] = small[9 + row : 10 + row, start : start + LANES]
    common[shard:] = rest[...].astype(bf16)


def collect(parts, channels, earlier):
    rows = parts[0].shape[0]
    shapes = [
        (rows - SMALL, channels), (rows - SMALL, LANES), (CONV, channels), (1, channels), (1, channels), (8, LANES)
    ]
    return pl.pallas_call(
        functools.partial(collect_kernel, len(parts), len(earlier)),
        in_specs=[in_vmem] * len(parts) + [anywhere] * len(earlier),
        out_specs=[in_vmem] * 7,
        out_shape=[jax.ShapeDtypeStruct(shape, f32) for shape in shapes]
        + [jax.ShapeDtypeStruct((rows, 2 * STATE), bf16)],
        scratch_shapes=[pltpu.VMEM((SMALL, 2 * STATE), f32)],
        compiler_params=pltpu.CompilerParams(vmem_limit_bytes=LIMIT),
        name="collect",
    )(*parts, *earlier)


def finish_kernel(count, *refs):
    parts, norm_gain, (shared, taps, bias, norm) = refs[:count], refs[count], refs[count + 1 :]
    shard = shared.shape[0]
    every = slice(0, 2 * STATE)
    shared[...] = add_up(parts, slice(0, shard), every)
    small = add_up(parts, slice(shard, shard + SMALL), every)
    taps[...] = small[0:CONV]
    bias[...] = small[CONV : CONV + 1]
    for row in range(6):
        cols = slice(row * 2 * STATE, (row + 1) * 2 * STATE)
        norm[:, cols] = small[8 + row : 9 + row] / norm_gain[:, cols]


def finish(parts, norm_gain):
    rows = parts[0].shape[0]
    shapes = [(rows - SMALL, 2 * STATE), (CONV, 2 * STATE), (1, 2 * STATE), norm_gain.shape]
    return pl.pallas_call(
        functools.partial(finish_kernel, len(parts)),
        in_specs=[in_vmem] * (len(parts) + 1),
        out_specs=[in_vmem] * 4,
        out_shape=[jax.ShapeDtypeStruct(shape, f32) for shape in shapes],
        name="finish",
    )(*parts, norm_gain)


def nothing(*refs):
    pass


def pinned(values, earlier):
    anywhere = pl.BlockSpec(memory_space=pl.ANY)
    held = pl.pallas_call(
        nothing,
        in_specs=[anywhere] * (len(values) + len(earlier)),
        out_specs=[anywhere] * len(values),
        out_shape=[jax.ShapeDtypeStruct(v.shape, v.dtype) for v in values],
        input_output_aliases={i: i for i in range(len(values))},
        name="pinned",
    )(*values, *earlier)
    return list(held)


def copy_kernel(source, *refs):
    refs[-1][...] = source[...]


def copied(value, earlier):
    whole = pl.BlockSpec(memory_space=pltpu.VMEM)
    return pl.pallas_call(
        copy_kernel,
        in_specs=[whole] + [pl.BlockSpec(memory_space=pl.ANY)] * len(earlier),
        out_specs=whole,
        out_shape=jax.ShapeDtypeStruct(value.shape, value.dtype),
        name="copied",
    )(value, *earlier)


def total_of(own, arrived):
    for value in arrived:
        own = own + value.astype(f32)
    return own


class Net:
    def __init__(self, dp, tensor):
        self.dp, self.tensor = dp, tensor
        self.chips = dp // 2
        rank = lax.axis_index("tensor")
        at = lax.axis_index("dp")
        shift = rank if tensor == 4 else jnp.zeros_like(rank)
        self.place = jnp.stack([at // 2, at % 2, shift]).astype(jnp.int32)

    def over_chips(self, values, k):
        return lax.ppermute(values, "dp", [(i, i ^ (2 * k)) for i in range(self.dp)])

    def over_core(self, values):
        return lax.ppermute(values, "dp", [(i, i ^ 1) for i in range(self.dp)])

    def over_tensor(self, values, k):
        return lax.ppermute(values, "tensor", [(i, i ^ k) for i in range(self.tensor)])

    def between(self, values, pairs):
        return lax.ppermute(values, "dp", [(2 * a + c, 2 * b + c) for a, b in pairs for c in range(2)])

    def gather_near(self, shard):
        if self.chips != 4:
            return [shard] + [self.over_chips(shard, k) for k in range(1, self.chips)]
        return [shard, self.over_chips(shard, 1), self.over_chips(shard, 2)]

    def gather_far(self, near, earlier):
        if self.chips != 4:
            return pinned(near, earlier) if earlier else near
        near = pinned(near, earlier)
        middle = self.between(near[0], [(1, 2), (2, 1)])
        return near + [middle + self.between(near[2], [(1, 0), (2, 3)])]

    def gather_cores(self, mine):
        return mine + [self.over_core(piece) for piece in mine]

    def scatter_far(self, others):
        if self.chips != 4:
            return []
        return [self.between(others[2], [(0, 1), (3, 2)]), self.between(others[2], [(1, 2), (2, 1)])]

    def scatter_join(self, others, came):
        if self.chips != 4:
            return others
        return [others[0], (others[1].astype(f32) + came[0].astype(f32)).astype(bf16)]

    def scatter_near(self, joined, came):
        return came[1:] + [self.over_chips(value, k + 1) for k, value in enumerate(joined)]

    def gather_first(self, shard):
        if self.tensor != 4:
            return [lax.all_gather(shard, "tensor", axis=0, tiled=True)]
        return [shard, self.over_tensor(shard, 1), self.over_tensor(shard, 2)]

    def gather_last(self, pieces, earlier):
        if self.tensor != 4:
            return pieces
        half = BLOCK // 2
        halves = [pieces[1][:half], pieces[2][half:]]
        if earlier:
            halves = pinned(halves, earlier)
        return pieces + [self.over_tensor(halves[0], 2), self.over_tensor(halves[1], 1)]

    def scatter_first(self, rows, earlier):
        if self.tensor != 4:
            return []
        half = BLOCK // 2
        halves = [rows[3 * BLOCK : 3 * BLOCK + half], rows[3 * BLOCK + half :]]
        if earlier:
            halves = pinned(halves, earlier)
        return [self.over_tensor(halves[0], 2), self.over_tensor(halves[1], 1)]

    def scatter_blocks(self, rows, came):
        if self.tensor != 4:
            return [rows]
        half = BLOCK // 2
        own, one, two = rows[:BLOCK], rows[BLOCK : 2 * BLOCK], rows[2 * BLOCK : 3 * BLOCK]
        one = jnp.concatenate([(one[:half].astype(f32) + came[0].astype(f32)).astype(bf16), one[half:]])
        two = jnp.concatenate([two[:half], (two[half:].astype(f32) + came[1].astype(f32)).astype(bf16)])
        return [own, one, two]

    def scatter_last(self, blocks, earlier):
        if self.tensor != 4:
            return [lax.psum_scatter(blocks[0], "tensor", scatter_dimension=0, tiled=True)]
        came = [self.over_tensor(blocks[k], k) for k in (1, 2)]
        return [blocks[0]] + (pinned(came, earlier) if earlier else came)

    def spread_tensor(self, values):
        return [values] + [self.over_tensor(values, k) for k in range(1, self.tensor)]

    def sum_tensor(self, values):
        k = 1
        while k < self.tensor:
            values = values + self.over_tensor(values, k)
            k *= 2
        return values


def local(
    net_of,
    tokens,
    norm_gain,
    gate_proj,
    inner_proj,
    shared_proj,
    step_proj,
    conv_inner,
    conv_inner_bias,
    conv_shared,
    conv_shared_bias,
    step_bias,
    decay_log,
    skip_gain,
    out_gain,
    out_proj,
    cotangent,
):
    net = net_of()
    place, chips = net.place, net.chips
    channels = gate_proj.shape[1]
    heads = step_proj.shape[1]
    width = channels + 2 * STATE
    token_rows = tokens.astype(f32)
    inverse = lax.rsqrt(jnp.mean(token_rows * token_rows, axis=-1, keepdims=True) + epsilon)
    unit = token_rows * inverse
    normed_low = (unit * norm_gain).astype(bf16)
    padding = jnp.zeros((step_proj.shape[0], LANES - heads), bf16)
    scan_shard = jnp.concatenate([inner_proj, shared_proj, step_proj, padding], axis=1)
    scan_mine = net.gather_far(net.gather_near(scan_shard), [])
    row_pieces = net.gather_first(normed_low)
    reached = scan_mine[1:]
    joint = joint_shard(gate_proj, out_proj, row_pieces[1:2])
    row_pieces = net.gather_last(row_pieces, [])
    scan_pieces = net.gather_cores(pinned(scan_mine, row_pieces[3:]) if row_pieces[3:] else scan_mine)
    cot_pieces = net.gather_first(copied(cotangent, row_pieces[3:] + scan_pieces[chips:]))
    joint_mine = net.gather_near(pinned([joint], reached)[0])

    taps = jnp.concatenate(
        [
            jnp.concatenate([conv_inner, conv_inner_bias[None]]),
            jnp.concatenate([conv_shared, conv_shared_bias[None]]),
        ],
        axis=1,
    )
    taps = jnp.pad(taps, ((0, 8 - CONV - 1), (0, 0)))
    rates = -jnp.exp(decay_log)
    head_rows = jnp.pad(jnp.stack([step_bias, rates]), ((0, 6), (0, LANES - heads)))
    skip_row = jnp.repeat(skip_gain, HEAD_DIM)[None]
    gain = out_gain[None]

    raw, scan_full, rows = product(
        place,
        row_pieces,
        scan_pieces,
        raw_epilogue,
        [],
        [(width + LANES, f32)],
        "project",
    )
    scanned, pre, states = scan_forward(raw, taps, head_rows, skip_row, [])
    cot_pieces = net.gather_last(cot_pieces, [scanned])
    joint_mine = net.gather_far(joint_mine, [scanned])
    gate, gated, grad_out, token_sums, joint_full, cot_rows = product(
        place,
        cot_pieces,
        net.gather_cores(pinned(joint_mine, cot_pieces[3:])),
        mix_epilogue,
        [(stay(rows), True), (stay(scanned), True), (gain, False)],
        [(channels, f32), (channels, f32), (channels, f32), (None, 2)],
        "mix",
    )
    token_sums = net.sum_tensor(token_sums)
    out_low, gate_back, scan_grad, gain_grad = gating(grad_out, gated, scanned, gate, token_sums, gain)
    keep, give = weight_grads(
        place, chips, [rows, cot_rows], [gate_back, out_low], [], "grad_joint_proj"
    )
    joint_come = net.over_core(give)
    branch, _ = back(place, [out_low], [(joint_full, 1)], None, "branch", [give])
    joint_own, joint_others = pairs(keep, joint_come, [branch])
    came = net.scatter_far(joint_others)
    branch_came = net.scatter_first(branch, joint_others[:1])
    held = scan_backward(
        0, raw, pre, scan_grad, states, taps, head_rows, skip_row, None, joint_others[:1]
    )
    if came:
        *came, one, two = pinned(came + branch_came, [held[1]])
        branch_came = [one, two]
    joint_arrived = net.scatter_near(net.scatter_join(joint_others, came), came)
    branch_parts = net.scatter_last(net.scatter_blocks(branch, branch_came), [])
    scan_back, sums, head_sums, _, _ = scan_backward(
        1, raw, pre, scan_grad, states, taps, head_rows, skip_row, held, came
    )
    norm_rows, norm_sums = back(
        place, [gate_back, stay(scan_back)], [(joint_full, 0), (scan_full, 0)], rows, "grad_normed"
    )
    keep, give = weight_grads(
        place,
        chips,
        [rows],
        [stay(scan_back)],
        [sums, gain_grad, norm_sums, head_sums],
        "grad_scan_proj",
        joint_arrived + branch_parts[1:],
    )
    norm_came = net.scatter_first(norm_rows, joint_arrived)
    scan_own, scan_others = pairs(keep, net.over_core(give))
    norm_came = pinned(norm_came, scan_others[:1]) if norm_came else norm_came
    came = net.scatter_far(scan_others)
    joined = net.scatter_join(scan_others, came)
    scan_arrived = net.scatter_near(joined, came)
    norm_parts = net.scatter_last(net.scatter_blocks(norm_rows, norm_came), joined[1:])
    grad_normed = total_of(norm_parts[0].astype(f32), norm_parts[1:])
    mixed = total_of(token_rows, branch_parts).astype(bf16)
    joint_total = total_of(joint_own, joint_arrived)
    grad_gate_proj, grad_out_proj = joint_total[:, :channels], joint_total[:, channels:].T
    spread = grad_normed * norm_gain
    grad_tokens = (
        cotangent.astype(f32)
        + inverse * spread
        - unit * (inverse * jnp.mean(spread * unit, axis=-1, keepdims=True))
    )
    grad_inner_proj, step_part, grad_conv_inner, inner_bias, gain_part, head_part, common = collect(
        [scan_own] + scan_arrived, channels, []
    )
    grad_shared_proj, grad_conv_shared, shared_bias, norm_part = finish(
        net.spread_tensor(common), norm_gain[None]
    )
    return (
        mixed,
        grad_tokens,
        norm_part[0],
        grad_gate_proj,
        grad_inner_proj,
        grad_shared_proj,
        step_part[:, :heads],
        grad_conv_inner,
        inner_bias[0],
        grad_conv_shared,
        shared_bias[0],
        head_part[0, :heads],
        head_part[1, :heads] * rates,
        head_part[2, :heads],
        gain_part[0],
        grad_out_proj,
    )


def solution(mesh):
    dp, tensor = mesh.shape["dp"], mesh.shape["tensor"]

    def on_device(*args):
        return local(lambda: Net(dp, tensor), *args)

    return jax.shard_map(
        on_device,
        mesh=mesh,
        in_specs=(
            P(("dp", "tensor"), None),
            P(),
            P("dp", "tensor"),
            P("dp", "tensor"),
            P("dp", None),
            P("dp", "tensor"),
            P(None, "tensor"),
            P("tensor"),
            P(),
            P(),
            P("tensor"),
            P("tensor"),
            P("tensor"),
            P("tensor"),
            P("tensor", "dp"),
            P(("dp", "tensor"), None),
        ),
        out_specs=(
            P(("dp", "tensor"), None),
            P(("dp", "tensor"), None),
            P(),
            P("dp", "tensor"),
            P("dp", "tensor"),
            P("dp", None),
            P("dp", "tensor"),
            P(None, "tensor"),
            P("tensor"),
            P(),
            P(),
            P("tensor"),
            P("tensor"),
            P("tensor"),
            P("tensor"),
            P("tensor", "dp"),
        ),
        check_vma=False,
    )
```

```python
import functools

import jax
import jax.numpy as jnp
from jax import lax
from jax.experimental import pallas as pl
from jax.experimental.pallas import tpu as pltpu
from jax.sharding import PartitionSpec as P

DI = 3072
epsilon = 1e-05
HEAD_DIM = 64
STATE = 128
CONV = 4
SEQ = 1024
SPAN = 256
CHUNK = 128
LANES = 128
NEVER = -1e30
NEAR = jax.ShapeDtypeStruct
f32 = jnp.float32
bf16 = jnp.bfloat16
highest = lax.Precision.HIGHEST


def dot(first, second, first_dim=1, second_dim=0, precision=None):
    return lax.dot_general(
        first,
        second,
        (((first_dim,), (second_dim,)), ((), ())),
        precision=precision,
        preferred_element_type=f32,
    )


def sigmoid(values):
    return 0.5 * jnp.tanh(0.5 * values) + 0.5


def places(dim):
    return lax.broadcasted_iota(jnp.int32, (CHUNK, LANES), dim)


def exact_dot(ones, values, parts):
    split = []
    for _ in range(parts):
        split.append(values.astype(bf16))
        values = values - split[-1].astype(f32)
    result = dot(ones, jnp.concatenate(split, axis=1))
    return sum(result[:, i * LANES : (i + 1) * LANES] for i in range(parts))


def decays(step_raw, heads_ref):
    raw = step_raw + heads_ref[0:1]
    small = jnp.exp(-jnp.abs(raw))
    log_one = jnp.where(small < 1e-3, small - 0.5 * small * small, jnp.log(1.0 + small))
    steps = jnp.maximum(raw, 0.0) + log_one
    summed = exact_dot((places(0) >= places(1)).astype(bf16), steps * heads_ref[1:2], 3)
    return steps, sigmoid(raw), summed, summed - jnp.log(steps)


def pair_of(first, second):
    return jnp.concatenate([first, second], axis=0)


def forward_kernel(raw_ref, taps_ref, heads_ref, skip_ref, *refs):
    scanned_ref, pre_ref, states_ref, state, before = refs[-5:]
    chunk = pl.program_id(0)
    channels = skip_ref.shape[1]
    width = channels + 2 * STATE

    @pl.when(chunk % (SEQ // CHUNK) == 0)
    def _():
        state[...] = jnp.zeros_like(state)
        before[...] = jnp.zeros_like(before)

    raw = raw_ref[:, :width]
    extended = jnp.concatenate([before[...], raw], axis=0)
    pre = taps_ref[CONV : CONV + 1] + taps_ref[CONV - 1 : CONV] * raw
    for tap in range(CONV - 1):
        start = 8 - (CONV - 1) + tap
        pre = pre + taps_ref[tap : tap + 1] * extended[start : start + CHUNK]
    before[...] = raw[CHUNK - 8 :]
    pre_ref[...] = pre
    act = (pre * sigmoid(pre)).astype(bf16)
    writes = act[:, channels : channels + STATE]
    reads = act[:, channels + STATE :]
    _, _, summed, shifted = decays(raw_ref[:, width:], heads_ref)
    summed_t, shifted_t = summed.T, shifted.T
    tail_t = jnp.exp(summed_t[:, CHUNK - 1 :] - shifted_t)
    scores = dot(reads, writes, 1, 1)
    writes_t = writes.astype(f32).T
    causal = places(0) >= places(1)
    left = places(1) < HEAD_DIM
    states_ref[...] = state[...].astype(bf16)
    for pair in range(channels // LANES):
        cols = slice(pair * LANES, (pair + 1) * LANES)
        values = act[:, cols].astype(f32)
        both = pair_of(jnp.where(left, values, 0.0), jnp.where(left, 0.0, values)).astype(bf16)
        mixes, tails, grown = [], [], []
        for head in (2 * pair, 2 * pair + 1):
            here = jnp.broadcast_to(summed[:, head : head + 1], (CHUNK, LANES))
            decay = jnp.exp(jnp.where(causal, here - shifted_t[head : head + 1], NEVER))
            mixes.append((scores * decay).astype(bf16))
            tails.append((writes_t * tail_t[head : head + 1]).astype(bf16))
            grown.append(here)
        stacked = pair_of(jnp.concatenate(mixes, axis=1), jnp.concatenate(tails, axis=1))
        out = dot(stacked, both)
        entering = state[:, cols]
        factor = jnp.exp(jnp.where(left, grown[0], grown[1]))
        across = dot(reads, entering.astype(bf16)) * factor
        scanned_ref[:, cols] = out[:CHUNK] + across + values * skip_ref[:, cols]
        state[:, cols] = entering * factor[CHUNK - 1 :] + out[CHUNK:]


def backward_kernel(part, n_deps, *refs):
    raw_ref, pre_ref, grad_ref, states_ref, taps_ref, heads_ref, skip_ref = refs[:7]
    n_held = 5 if part else 0
    held, refs = refs[7 : 7 + n_held], refs[7 + n_held + n_deps :]
    low_ref, sums_ref, head_sums_ref, carry, after, wide = refs
    step = pl.program_id(0)
    channels = skip_ref.shape[1]
    width = channels + 2 * STATE

    @pl.when(step == 0)
    def _():
        if part:
            for ref, source in zip((sums_ref, head_sums_ref, carry, after), held[1:], strict=True):
                ref[...] = source[...]
        else:
            sums_ref[...] = jnp.zeros_like(sums_ref)
            head_sums_ref[...] = jnp.zeros_like(head_sums_ref)

    @pl.when((step + part * pl.num_programs(0)) % (SEQ // CHUNK) == 0)
    def _():
        carry[...] = jnp.zeros_like(carry)
        after[...] = jnp.zeros_like(after)

    pre = pre_ref[...]
    gate = sigmoid(pre)
    act = (pre * gate).astype(bf16)
    writes = act[:, channels : channels + STATE]
    reads = act[:, channels + STATE :]
    steps, slopes, summed, shifted = decays(raw_ref[:, width:], heads_ref)
    summed_t = summed.T
    scores_t = dot(writes, reads, 1, 1)
    causal = places(0) <= places(1)
    earlier = places(0) < places(1)
    suffix = (places(0) >= places(1)).astype(bf16)
    left = places(1) < HEAD_DIM
    score_grads = jnp.zeros((CHUNK, LANES), f32)
    spans, inner_grads, lasts = [], [], []
    for pair in range(channels // LANES):
        cols = slice(pair * LANES, (pair + 1) * LANES)
        values = act[:, cols].astype(f32)
        both = pair_of(jnp.where(left, values, 0.0), jnp.where(left, 0.0, values)).astype(bf16)
        grad_low = grad_ref[:, cols]
        grad = grad_low.astype(f32)
        grad_both = pair_of(jnp.where(left, grad, 0.0), jnp.where(left, 0.0, grad)).astype(bf16)
        products = dot(both, grad_low, 1, 1)
        mixes, crossing, grown, tails = [], [], [], []
        for place, head in enumerate((2 * pair, 2 * pair + 1)):
            here = jnp.broadcast_to(shifted[:, head : head + 1], (CHUNK, LANES))
            decay = jnp.exp(jnp.where(causal, summed_t[head : head + 1] - here, NEVER))
            product = products[place * CHUNK : (place + 1) * CHUNK]
            score_grads = score_grads + decay * product
            mix = scores_t * decay
            mixes.append(mix.astype(bf16))
            crossing.append((mix * product).astype(bf16))
            level = jnp.broadcast_to(summed[:, head : head + 1], (CHUNK, LANES))
            grown.append(level)
            tails.append(level[CHUNK - 1 :] - here)
        sums = dot(pair_of(*crossing), suffix)
        for place in range(2):
            piece = jnp.where(earlier, sums[place * CHUNK : (place + 1) * CHUNK], 0.0)
            spans.append(jnp.sum(piece, axis=0, keepdims=True))
        within = dot(jnp.concatenate(mixes, axis=1), grad_both)
        factor = jnp.exp(jnp.where(left, grown[0], grown[1]))
        tail = jnp.exp(jnp.where(left, tails[0], tails[1]))
        leaving = carry[:, cols]
        entering = states_ref[:, cols]
        later = tail * dot(writes, leaving.astype(bf16))
        both_grads = within + later
        inner_grads.append(both_grads + skip_ref[:, cols] * grad)
        spread = factor * grad
        spread_low = spread.astype(bf16)
        wide[0:CHUNK, cols] = spread_low
        wide[CHUNK : 2 * CHUNK, cols] = (tail * values).astype(bf16)
        wide[2 * CHUNK : 3 * CHUNK, cols] = (spread * dot(reads, entering)).astype(bf16)
        wide[3 * CHUNK : 4 * CHUNK, cols] = (values * later).astype(bf16)
        wide[4 * CHUNK : 5 * CHUNK, cols] = (values * both_grads).astype(bf16)
        held = jnp.sum(entering.astype(f32) * leaving, axis=0, keepdims=True) * factor[CHUNK - 1 :]
        sums_ref[CONV + 1 : CONV + 2, cols] += jnp.sum(grad * values, axis=0, keepdims=True)
        wide[5 * CHUNK :, cols] = jnp.broadcast_to(held, (16, LANES)).astype(bf16)
        lasts.append(factor[CHUNK - 1 :])
    reads_t = reads.astype(f32).T.astype(bf16)
    score_low = score_grads.astype(bf16)
    spread_all = wide[0:CHUNK, :]
    read_grads = dot(score_low, writes, 0, 0) + dot(spread_all, states_ref[...], 1, 1)
    write_grads = dot(score_low, reads) + dot(wide[CHUNK : 2 * CHUNK, :], carry[...].astype(bf16), 1, 1)
    of_head = (
        lax.broadcasted_iota(jnp.int32, (channels, LANES), 0) // HEAD_DIM
        == lax.broadcasted_iota(jnp.int32, (channels, LANES), 1)
    )
    reduced = dot(wide[2 * CHUNK :, :], of_head.astype(bf16))
    carry[...] = carry[...] * jnp.concatenate(lasts, axis=1) + dot(reads_t, spread_all)
    both_sums = reduced[2 * CHUNK : 3 * CHUNK]
    held_heads = reduced[3 * CHUNK : 3 * CHUNK + 1]
    span_rows = jnp.concatenate(spans + [jnp.zeros((LANES - len(spans), LANES), f32)], axis=0)
    upto = [places(0) <= places(1), places(0) > places(1)]
    upto = jnp.concatenate([v.astype(bf16) for v in upto], axis=1)
    log_grads = exact_dot(upto, reduced[: 2 * CHUNK], 2) + span_rows.T + held_heads
    ratio = jnp.where(steps > 1e-30, slopes / steps, 1.0)
    step_grads = both_sums * ratio + heads_ref[1:2] * log_grads * slopes
    head_sums_ref[0:1] += jnp.sum(step_grads, axis=0, keepdims=True)
    head_sums_ref[1:2] += jnp.sum(log_grads * steps, axis=0, keepdims=True)

    @pl.when(part * pl.num_programs(0) + step == 2 * pl.num_programs(0) - 1)
    def _():
        skip_rows = jnp.broadcast_to(sums_ref[CONV + 1 : CONV + 2, :channels], (8, channels))
        head_sums_ref[2:3] = dot(skip_rows, of_head.astype(f32), precision=highest)[0:1]

    raw = raw_ref[:, :width]
    act_grads = jnp.concatenate(inner_grads + [write_grads, read_grads], axis=1)
    pre_grads = act_grads * (gate * (1.0 + pre * (1.0 - gate)))
    extended = jnp.concatenate([pre_grads, after[...]], axis=0)
    after[...] = pre_grads[:8]
    sums_ref[CONV : CONV + 1] += jnp.sum(pre_grads, axis=0, keepdims=True)
    raw_grads = taps_ref[CONV - 1 : CONV] * pre_grads
    sums_ref[CONV - 1 : CONV] += jnp.sum(raw * pre_grads, axis=0, keepdims=True)
    for tap in range(CONV - 1):
        moved = extended[CONV - 1 - tap : CONV - 1 - tap + CHUNK]
        raw_grads = raw_grads + taps_ref[tap : tap + 1] * moved
        sums_ref[tap : tap + 1] += jnp.sum(raw * moved, axis=0, keepdims=True)
    low_ref[:, :width] = raw_grads.astype(bf16)
    low_ref[:, width:] = step_grads.astype(bf16)


def stay(values):
    return pltpu.with_memory_space_constraint(values, pltpu.HBM)


def scan_forward(raw, taps, heads, skip, earlier):
    tokens, full = raw.shape
    channels = skip.shape[1]
    width = channels + 2 * STATE
    count = tokens // CHUNK
    by_chunk = lambda shape: pl.BlockSpec(shape, lambda s: (s, 0))
    whole = lambda v: pl.BlockSpec(v.shape, lambda s: (0, 0))
    return pl.pallas_call(
        forward_kernel,
        grid=(count,),
        in_specs=[by_chunk((CHUNK, full)), whole(taps), whole(heads), whole(skip)]
        + [pl.BlockSpec(memory_space=pl.ANY)] * len(earlier),
        out_specs=[
            by_chunk((CHUNK, channels)),
            by_chunk((CHUNK, width)),
            by_chunk((STATE, channels)),
        ],
        scratch_shapes=[pltpu.VMEM((STATE, channels), f32), pltpu.VMEM((8, width), f32)],
        out_shape=[
            pltpu.HBM((tokens, channels), f32),
            pltpu.HBM((tokens, width), f32),
            pltpu.HBM((count * STATE, channels), bf16),
        ],
        compiler_params=pltpu.CompilerParams(vmem_limit_bytes=12 << 20),
        name="scan_forward",
    )(stay(raw), taps, heads, skip, *earlier)


def scan_backward(part, raw, pre, grad, states, taps, heads, skip, held, earlier):
    tokens, full = raw.shape
    channels = skip.shape[1]
    width = channels + 2 * STATE
    count = tokens // CHUNK
    half = count // 2
    last = count - 1 - part * half
    by_chunk = lambda shape: pl.BlockSpec(shape, lambda s: (last - s, 0))
    whole = lambda shape: pl.BlockSpec(shape, lambda s: (0, 0))
    kept = [(8, width), (8, LANES), (STATE, channels), (8, width)]
    free = pl.BlockSpec(memory_space=pl.ANY)
    held = list(held) if part else []
    return pl.pallas_call(
        functools.partial(backward_kernel, part, len(earlier)),
        grid=(half,),
        in_specs=[
            by_chunk((CHUNK, full)),
            by_chunk((CHUNK, width)),
            by_chunk((CHUNK, channels)),
            by_chunk((STATE, channels)),
            whole(taps.shape),
            whole(heads.shape),
            whole(skip.shape),
        ]
        + ([free] + [whole(shape) for shape in kept] if part else [])
        + [free] * len(earlier),
        out_specs=[by_chunk((CHUNK, full))] + [whole(shape) for shape in kept],
        scratch_shapes=[pltpu.VMEM((5 * CHUNK + 16, channels), bf16)],
        out_shape=[pltpu.HBM((tokens, full), bf16)] + [pltpu.HBM(shape, f32) for shape in kept],
        input_output_aliases={7: 0} if part else {},
        compiler_params=pltpu.CompilerParams(vmem_limit_bytes=12 << 20),
        name=f"scan_backward_{part}",
    )(stay(raw), stay(pre), stay(grad), stay(states), taps, heads, skip, *[stay(v) for v in held], *earlier)


BLOCK = 256
LIMIT = 16 << 20
SMALL_LIMIT = 12 << 20
SMALL = 16
anywhere = pl.BlockSpec(memory_space=pl.ANY)
in_vmem = pl.BlockSpec(memory_space=pltpu.VMEM)


def column_sums(values, count):
    rows = [
        jnp.sum(values[i * LANES : (i + 1) * LANES].T, axis=0, keepdims=True)
        for i in range(count // LANES)
    ]
    return jnp.concatenate(rows, axis=0)


def fold(values):
    total = values[:, :LANES]
    for start in range(LANES, values.shape[1], LANES):
        total = total + values[:, start : start + LANES]
    return total


def shard_rows(place, index, chips, height):
    core, chip = index // chips, index % chips
    return pl.multiple_of(((place[0] ^ chip) * 2 + (place[1] ^ core)) * height, height)


def row_start(place, start):
    if isinstance(start, int):
        return pl.multiple_of((start // BLOCK ^ place[2]) * BLOCK + start % BLOCK, LANES)
    return pl.multiple_of((start // BLOCK ^ place[2]) * BLOCK, BLOCK)


def product_kernel(heights, chips, epilogue, n_extra, n_deps, n_out, place, *refs):
    n_rows, n_full = len(heights), 2 * chips
    row_refs, refs = refs[:n_rows], refs[n_rows:]
    full_refs, refs = refs[:n_full], refs[n_full:]
    extra, refs = refs[:n_extra], refs[n_extra + n_deps :]
    outs, (full, rows, sems) = refs[:n_out], refs[n_out:]
    step = pl.program_id(0)
    starts = [sum(heights[:i]) for i in range(n_rows)]
    shard = full.shape[0] // n_full
    row_copies = [
        pltpu.make_async_copy(
            row_refs[i], rows.at[pl.ds(row_start(place, starts[i]), heights[i])], sems.at[i]
        )
        for i in range(n_rows)
    ]
    full_copies = [
        pltpu.make_async_copy(
            full_refs[i], full.at[pl.ds(shard_rows(place, i, chips, shard), shard)], sems.at[n_rows + i]
        )
        for i in range(n_full)
    ]

    @pl.when(step == 0)
    def _():
        for copy in full_copies + row_copies:
            copy.start()
        for copy in full_copies:
            copy.wait()

    for i in range(n_rows):

        @pl.when(step == starts[i] // BLOCK)
        def _(i=i):
            row_copies[i].wait()

    block = rows[pl.ds(row_start(place, step * BLOCK), BLOCK), :]
    epilogue(step ^ place[2], block, full, extra, outs)


def product(place, row_pieces, full_pieces, epilogue, extra, outs, name, earlier=()):
    chips = len(full_pieces) // 2
    heights = tuple(piece.shape[0] for piece in row_pieces)
    tokens, depth = sum(heights), row_pieces[0].shape[1]
    columns = full_pieces[0].shape[1]
    by_block = lambda cols: pl.BlockSpec((BLOCK, cols), lambda s, p: (s ^ p[2], 0))
    out_specs, out_shape = [], []
    for cols, dtype in outs:
        if cols is None:
            shape = (dtype * tokens // LANES, LANES)
            out_specs.append(pl.BlockSpec(shape, lambda s, p: (0, 0)))
            out_shape.append(jax.ShapeDtypeStruct(shape, f32))
        else:
            out_specs.append(by_block(cols))
            out_shape.append((pltpu.HBM if name == "project" else NEAR)((tokens, cols), dtype))
    return pl.pallas_call(
        functools.partial(product_kernel, heights, chips, epilogue, len(extra), len(earlier), len(outs)),
        grid_spec=pltpu.PrefetchScalarGridSpec(
            num_scalar_prefetch=1,
            grid=(tokens // BLOCK,),
            in_specs=[anywhere] * (len(row_pieces) + len(full_pieces))
            + [by_block(v.shape[1]) if by else in_vmem for v, by in extra]
            + [anywhere] * len(earlier),
            out_specs=out_specs + [in_vmem, in_vmem],
            scratch_shapes=[pltpu.SemaphoreType.DMA((len(row_pieces) + len(full_pieces),))],
        ),
        out_shape=out_shape + [pltpu.VMEM((depth, columns), bf16), pltpu.VMEM((tokens, depth), bf16)],
        compiler_params=pltpu.CompilerParams(vmem_limit_bytes=LIMIT),
        name=name,
    )(place, *[stay(v) for v in row_pieces + full_pieces], *[v for v, _ in extra], *earlier)


def slices(columns):
    return [slice(start, min(start + 256, columns)) for start in range(0, columns, 256)]


def raw_epilogue(index, block, full, extra, outs):
    (raw,) = outs
    for cols in slices(raw.shape[1]):
        raw[:, cols] = dot(block, full[:, cols])


def mix_epilogue(index, block, full, extra, outs):
    rows, scanned, gain = extra
    gate, gated, grad, sums = outs
    channels = gate.shape[1]
    squares = jnp.zeros((BLOCK, LANES), f32)
    dots = jnp.zeros((BLOCK, LANES), f32)
    here = pl.ds(pl.multiple_of(index * BLOCK, BLOCK), BLOCK)
    for cols in slices(channels):
        value = dot(rows[here, :], full[:, cols])
        out = dot(block, full[:, channels + cols.start : channels + cols.stop])
        gate[:, cols] = value
        grad[:, cols] = out
        product = scanned[:, cols] * (value * sigmoid(value))
        gated[:, cols] = product
        squares = squares + fold(product * product)
        dots = dots + fold(out * gain[:, cols] * product)
    per = BLOCK // LANES
    half = sums.shape[0] // 2
    sums[pl.ds(index * per, per), :] = column_sums(squares, BLOCK)
    sums[pl.ds(half + index * per, per), :] = column_sums(dots, BLOCK)


def shard_kernel(gate_proj, out_proj, *refs):
    out = refs[-1]
    channels, height = out_proj.shape
    out[:, :channels] = gate_proj[...]
    place = [lax.broadcasted_iota(jnp.int32, (height, height), dim) for dim in range(2)]
    same = (place[0] == place[1]).astype(bf16)
    out[:, channels:] = dot(same, out_proj[...], 1, 1).astype(bf16)


def joint_shard(gate_proj, out_proj, earlier):
    return pl.pallas_call(
        shard_kernel,
        in_specs=[in_vmem] * 2 + [anywhere] * len(earlier),
        out_specs=in_vmem,
        out_shape=jax.ShapeDtypeStruct((gate_proj.shape[0], 2 * gate_proj.shape[1]), bf16),
        name="joint_shard",
    )(gate_proj, out_proj, *earlier)


def columns_of(row):
    return jnp.broadcast_to(row, (LANES, LANES)).T


def gating_kernel(grad_out, gated, gate, sums, gain, scanned, out_low, gate_back, scan_grad, gain_grad):
    step = pl.program_id(0)
    half = sums.shape[0] // 2

    @pl.when(step == 0)
    def _():
        gain_grad[...] = jnp.zeros_like(gain_grad)

    for part in range(BLOCK // LANES):
        rows = slice(part * LANES, (part + 1) * LANES)
        index = step * (BLOCK // LANES) + part
        here = pl.ds(pl.multiple_of(index * LANES, LANES), LANES)
        ratio_row = lax.rsqrt(sums[pl.ds(index, 1), :] / DI + epsilon)
        dots = sums[pl.ds(half + index, 1), :]
        ratio = columns_of(ratio_row)
        pull = columns_of(ratio_row * ratio_row * ratio_row / DI * dots)
        for start in range(0, gate.shape[1], LANES):
            cols = slice(start, start + LANES)
            held, value = gated[here, cols], gate[here, cols]
            scaled = grad_out[here, cols] * ratio
            out_low[rows, cols] = (gain[:, cols] * (held * ratio)).astype(bf16)
            gain_grad[0:1, cols] += jnp.sum(scaled * held, axis=0, keepdims=True)
            grad = gain[:, cols] * scaled - held * pull
            slope = sigmoid(value)
            scan_grad[rows, cols] = (grad * (value * slope)).astype(bf16)
            gate_grad = grad * scanned[rows, cols] * (slope * (1.0 + value * (1.0 - slope)))
            gate_back[rows, cols] = gate_grad.astype(bf16)


def gating(grad_out, gated, scanned, gate, sums, gain):
    tokens, columns = gated.shape
    block = pl.BlockSpec((BLOCK, columns), lambda s: (s, 0))
    return pl.pallas_call(
        gating_kernel,
        grid=(tokens // BLOCK,),
        in_specs=[in_vmem] * 5 + [block],
        out_specs=[block] * 3 + [pl.BlockSpec((8, columns), lambda s: (0, 0))],
        out_shape=[NEAR((tokens, columns), bf16)] * 2
        + [pltpu.HBM((tokens, columns), bf16)] + [jax.ShapeDtypeStruct((8, columns), f32)],
        compiler_params=pltpu.CompilerParams(vmem_limit_bytes=SMALL_LIMIT),
        name="gating",
    )(grad_out, gated, gate, sums, gain, stay(scanned))


def grads_kernel(n_rows, wide, place, *refs):
    rows, lows = refs[:n_rows], refs[n_rows : 2 * n_rows]
    keep, give = refs[-2:]
    shard = wide // 2
    first = place[1] == 0
    lanes = pl.ds(pl.multiple_of((pl.program_id(0) ^ place[0]) * wide, LANES), wide)
    start = 0
    for row, low in zip(rows, lows, strict=True):
        for cols in slices(low.shape[1]):
            value = dot(row[:, lanes], low[:, cols], 0, 0)
            one, two = value[:shard], value[shard:]
            out = slice(start + cols.start, start + cols.stop)
            keep[0, :shard, out] = jnp.where(first, one, two).astype(bf16)
            give[0, :shard, out] = jnp.where(first, two, one).astype(bf16)
        start += low.shape[1]


def fill_small(small, sums, gain_grad, norm_grad, head_sums):
    rest = norm_grad.shape[1] - small.shape[1]
    small[...] = jnp.zeros_like(small)
    small[0:8, : sums.shape[1]] = sums[...]
    small[8:9, : gain_grad.shape[1]] = gain_grad[0:1, :]
    small[9:10, :] = norm_grad[0:1, : small.shape[1]]
    small[10:11, :rest] = norm_grad[0:1, small.shape[1] :]
    small[11:14, :LANES] = head_sums[0:3, :]


def small_kernel(n_rows, wide, place, *refs):
    keep, give, small = refs[-3:]
    grads_kernel(n_rows, wide, place, *refs[:-1])
    fill_small(small, *refs[2 * n_rows : 2 * n_rows + 4])
    low = small[...].astype(bf16)
    shard = keep.shape[1] - SMALL
    keep[0, shard:] = low
    give[0, shard:] = low


def whole_grads_kernel(chips, n_rows, n_small, place, *refs):
    rows, lows = refs[:n_rows], refs[n_rows : 2 * n_rows]
    keep, give, acc, small = refs[-4:]
    depth = acc.shape[0]
    shard = depth // (2 * chips)
    start = 0
    for row, low in zip(rows, lows, strict=True):
        cols = slice(start, start + low.shape[1])
        for lanes in slices(depth):
            acc[lanes, cols] = dot(row[:, lanes], low[...], 0, 0)
        start = cols.stop
    for k in range(chips):
        for out, core in ((keep, place[1]), (give, 1 - place[1])):
            at = pl.multiple_of(((place[0] ^ k) * 2 + core) * shard, shard)
            out[k, :shard] = acc[pl.ds(at, shard), :].astype(bf16)
    if n_small:
        fill_small(small, *refs[2 * n_rows : 2 * n_rows + n_small])
        for k in range(chips):
            keep[k, shard:] = small[...].astype(bf16)
            give[k, shard:] = small[...].astype(bf16)


def weight_grads(place, chips, rows, lows, small, name, earlier=()):
    tokens, depth = rows[0].shape
    columns = sum(v.shape[1] for v in lows)
    wide = depth // chips
    shard = wide // 2
    height = shard + (SMALL if small else 0)
    if wide % LANES:
        return pl.pallas_call(
            functools.partial(whole_grads_kernel, chips, len(rows), len(small)),
            in_specs=[pl.BlockSpec(memory_space=pltpu.SMEM)]
            + [in_vmem] * (2 * len(rows) + len(small))
            + [anywhere] * len(earlier),
            out_specs=[in_vmem] * 2,
            out_shape=[jax.ShapeDtypeStruct((chips, height, columns), bf16)] * 2,
            scratch_shapes=[pltpu.VMEM((depth, columns), f32), pltpu.VMEM((SMALL, columns), f32)],
            compiler_params=pltpu.CompilerParams(vmem_limit_bytes=2 * LIMIT),
            name=name,
        )(place, *rows, *lows, *small, *earlier)
    out = pl.BlockSpec((1, height, columns), lambda k, p: (k, 0, 0))
    return pl.pallas_call(
        functools.partial(small_kernel if small else grads_kernel, len(rows), wide),
        grid_spec=pltpu.PrefetchScalarGridSpec(
            num_scalar_prefetch=1,
            grid=(chips,),
            in_specs=[in_vmem] * (2 * len(rows) + len(small))
            + [anywhere] * len(earlier),
            out_specs=[out, out],
            scratch_shapes=[pltpu.VMEM((SMALL, columns), f32)] if small else [],
        ),
        out_shape=[jax.ShapeDtypeStruct((chips, height, columns), bf16)] * 2,
        compiler_params=pltpu.CompilerParams(vmem_limit_bytes=SMALL_LIMIT),
        name=name,
    )(place, *rows, *lows, *small, *earlier)


def pairs_kernel(chips, *refs):
    keep, come, own, others = refs[0], refs[1], refs[-chips], refs[1 - chips :]
    own[...] = keep[0].astype(f32) + come[0].astype(f32)
    for k in range(1, chips):
        others[k - 1][...] = (keep[k].astype(f32) + come[k].astype(f32)).astype(bf16)


def pairs(keep, come, earlier=()):
    chips, rows, columns = keep.shape
    out = pl.pallas_call(
        functools.partial(pairs_kernel, chips),
        in_specs=[in_vmem, in_vmem] + [anywhere] * len(earlier),
        out_specs=[in_vmem] * chips,
        out_shape=[pltpu.HBM((rows, columns), f32)] + [pltpu.HBM((rows, columns), bf16)] * (chips - 1),
        compiler_params=pltpu.CompilerParams(vmem_limit_bytes=SMALL_LIMIT),
        name="pairs",
    )(keep, come, *earlier)
    return out[0], list(out[1:])


def back_kernel(parts, with_rows, place, *refs):
    count = len(parts)
    lows, fulls, refs = refs[:count], refs[count : 2 * count], refs[2 * count :]
    rows, out, sums = (refs[0], refs[-2], refs[-1]) if with_rows else (None, refs[-1], None)
    step = pl.program_id(0)
    if with_rows:

        @pl.when(step == 0)
        def _():
            sums[...] = jnp.zeros_like(sums)

    here = pl.ds(pl.multiple_of((step ^ place[2]) * BLOCK, BLOCK), BLOCK)
    for cols in slices(out.shape[1]):
        value = 0.0
        for low, full, part in zip(lows, fulls, parts, strict=True):
            wide = low.shape[1]
            value = value + dot(low[...], full[cols, part * wide : (part + 1) * wide], 1, 1)
        out[:, cols] = value.astype(bf16)
        if with_rows:
            sums[0:1, cols] += jnp.sum(value * rows[here, cols].astype(f32), axis=0, keepdims=True)


def back(place, lows, fulls, rows, name, earlier=()):
    tokens, depth = lows[0].shape[0], fulls[0][0].shape[0]
    by_block = lambda cols: pl.BlockSpec((BLOCK, cols), lambda s, p: (s ^ p[2], 0))
    extra = [] if rows is None else [rows]
    out = pl.pallas_call(
        functools.partial(back_kernel, tuple(part for _, part in fulls), rows is not None),
        grid_spec=pltpu.PrefetchScalarGridSpec(
            num_scalar_prefetch=1,
            grid=(tokens // BLOCK,),
            in_specs=[by_block(v.shape[1]) for v in lows]
            + [in_vmem] * (len(fulls) + len(extra))
            + [anywhere] * len(earlier),
            out_specs=[pl.BlockSpec((BLOCK, depth), lambda s, p: (s, 0))]
            + [pl.BlockSpec((8, depth), lambda s, p: (0, 0)) for _ in extra],
        ),
        out_shape=[jax.ShapeDtypeStruct((tokens, depth), bf16)]
        + [jax.ShapeDtypeStruct((8, depth), f32) for _ in extra],
        compiler_params=pltpu.CompilerParams(vmem_limit_bytes=SMALL_LIMIT),
        name=name,
    )(place, *lows, *[v for v, _ in fulls], *extra, *earlier)
    return out[0], out[1] if extra else None


def add_up(parts, rows, cols):
    value = parts[0][rows, cols].astype(f32)
    for part in parts[1:]:
        value = value + part[rows, cols].astype(f32)
    return value


def collect_kernel(count, n_deps, *refs):
    parts = refs[:count]
    inner, step, taps, bias, gain, heads, common, rest = refs[count + n_deps :]
    shard, channels = inner.shape
    full = parts[0].shape[1]
    own = slice(0, shard)
    for start in range(0, channels, 256):
        cols = slice(start, min(start + 256, channels))
        inner[:, cols] = add_up(parts, own, cols)
    step[...] = add_up(parts, own, slice(full - LANES, full))
    shared = slice(channels, channels + 2 * STATE)
    common[0:shard] = add_up(parts, own, shared).astype(bf16)
    small = add_up(parts, slice(shard, shard + SMALL), slice(0, full))
    taps[...] = small[0:CONV, :channels]
    bias[...] = small[CONV : CONV + 1, :channels]
    gain[...] = small[8:9, :channels]
    heads[...] = jnp.zeros_like(heads)
    heads[0:3] = small[11:14, :LANES]
    rest[...] = jnp.zeros_like(rest)
    rest[0:8] = small[0:8, shared]
    for piece in range(12):
        row, start = divmod(piece * LANES, full)
        target = slice(piece % 2 * LANES, (piece % 2 + 1) * LANES)
        rest[8 + piece // 2 : 9 + piece // 2, target] = small[9 + row : 10 + row, start : start + LANES]
    common[shard:] = rest[...].astype(bf16)


def collect(parts, channels, earlier):
    rows = parts[0].shape[0]
    shapes = [
        (rows - SMALL, channels), (rows - SMALL, LANES), (CONV, channels), (1, channels), (1, channels), (8, LANES)
    ]
    return pl.pallas_call(
        functools.partial(collect_kernel, len(parts), len(earlier)),
        in_specs=[in_vmem] * len(parts) + [anywhere] * len(earlier),
        out_specs=[in_vmem] * 7,
        out_shape=[jax.ShapeDtypeStruct(shape, f32) for shape in shapes]
        + [jax.ShapeDtypeStruct((rows, 2 * STATE), bf16)],
        scratch_shapes=[pltpu.VMEM((SMALL, 2 * STATE), f32)],
        compiler_params=pltpu.CompilerParams(vmem_limit_bytes=SMALL_LIMIT),
        name="collect",
    )(*parts, *earlier)


def finish_kernel(count, *refs):
    parts, norm_gain, (shared, taps, bias, norm) = refs[:count], refs[count], refs[count + 1 :]
    shard = shared.shape[0]
    every = slice(0, 2 * STATE)
    shared[...] = add_up(parts, slice(0, shard), every)
    small = add_up(parts, slice(shard, shard + SMALL), every)
    taps[...] = small[0:CONV]
    bias[...] = small[CONV : CONV + 1]
    for row in range(6):
        cols = slice(row * 2 * STATE, (row + 1) * 2 * STATE)
        norm[:, cols] = small[8 + row : 9 + row] / norm_gain[:, cols]


def finish(parts, norm_gain):
    rows = parts[0].shape[0]
    shapes = [(rows - SMALL, 2 * STATE), (CONV, 2 * STATE), (1, 2 * STATE), norm_gain.shape]
    return pl.pallas_call(
        functools.partial(finish_kernel, len(parts)),
        in_specs=[in_vmem] * (len(parts) + 1),
        out_specs=[in_vmem] * 4,
        out_shape=[jax.ShapeDtypeStruct(shape, f32) for shape in shapes],
        name="finish",
    )(*parts, norm_gain)


def nothing(*refs):
    pass


def pinned(values, earlier):
    anywhere = pl.BlockSpec(memory_space=pl.ANY)
    held = pl.pallas_call(
        nothing,
        in_specs=[anywhere] * (len(values) + len(earlier)),
        out_specs=[anywhere] * len(values),
        out_shape=[jax.ShapeDtypeStruct(v.shape, v.dtype) for v in values],
        input_output_aliases={i: i for i in range(len(values))},
        name="pinned",
    )(*values, *earlier)
    return list(held)


def copy_kernel(source, *refs):
    refs[-1][...] = source[...]


def copied(value, earlier):
    whole = pl.BlockSpec(memory_space=pltpu.VMEM)
    return pl.pallas_call(
        copy_kernel,
        in_specs=[whole] + [pl.BlockSpec(memory_space=pl.ANY)] * len(earlier),
        out_specs=whole,
        out_shape=jax.ShapeDtypeStruct(value.shape, value.dtype),
        name="copied",
    )(value, *earlier)


def total_of(own, arrived):
    for value in arrived:
        own = own + value.astype(f32)
    return own


class Net:
    def __init__(self, dp, tensor):
        self.dp, self.tensor = dp, tensor
        self.chips = dp // 2
        rank = lax.axis_index("tensor")
        at = lax.axis_index("dp")
        shift = rank if tensor == 4 else jnp.zeros_like(rank)
        self.place = jnp.stack([at // 2, at % 2, shift]).astype(jnp.int32)

    def over_chips(self, values, k):
        return lax.ppermute(values, "dp", [(i, i ^ (2 * k)) for i in range(self.dp)])

    def over_core(self, values):
        return lax.ppermute(values, "dp", [(i, i ^ 1) for i in range(self.dp)])

    def over_tensor(self, values, k):
        return lax.ppermute(values, "tensor", [(i, i ^ k) for i in range(self.tensor)])

    def between(self, values, pairs):
        return lax.ppermute(values, "dp", [(2 * a + c, 2 * b + c) for a, b in pairs for c in range(2)])

    def gather_near(self, shard):
        if self.chips != 4:
            return [shard] + [self.over_chips(shard, k) for k in range(1, self.chips)]
        return [shard, self.over_chips(shard, 1), self.over_chips(shard, 2)]

    def gather_far(self, near, earlier):
        if self.chips != 4:
            return pinned(near, earlier) if earlier else near
        near = pinned(near, earlier)
        middle = self.between(near[0], [(1, 2), (2, 1)])
        return near + [middle + self.between(near[2], [(1, 0), (2, 3)])]

    def gather_cores(self, mine, earlier, early):
        first = pinned(mine[:-1], early)
        last = pinned(mine[-1:], earlier)
        return first + last + [self.over_core(piece) for piece in first + last]

    def scatter_far(self, others):
        if self.chips != 4:
            return []
        return [self.between(others[2], [(0, 1), (3, 2)]), self.between(others[2], [(1, 2), (2, 1)])]

    def scatter_join(self, others, came):
        if self.chips != 4:
            return others
        one, two = pinned(others[:2], came)
        return [one, (two.astype(f32) + came[0].astype(f32)).astype(bf16)]

    def scatter_near(self, joined, came):
        return came[1:] + [self.over_chips(value, k + 1) for k, value in enumerate(joined)]

    def gather_first(self, shard):
        if self.tensor != 4:
            return [lax.all_gather(shard, "tensor", axis=0, tiled=True)]
        return [shard, self.over_tensor(shard, 1), self.over_tensor(shard, 2)]

    def gather_last(self, pieces, earlier):
        if self.tensor != 4:
            return pieces
        half = BLOCK // 2
        halves = [pieces[1][:half], pieces[2][half:]]
        if earlier:
            halves = pinned(halves, earlier)
        return pieces + [self.over_tensor(halves[0], 2), self.over_tensor(halves[1], 1)]

    def scatter_first(self, rows, earlier):
        if self.tensor != 4:
            return []
        half = BLOCK // 2
        halves = [rows[3 * BLOCK : 3 * BLOCK + half], rows[3 * BLOCK + half :]]
        if earlier:
            halves = pinned(halves, earlier)
        return [self.over_tensor(halves[0], 2), self.over_tensor(halves[1], 1)]

    def scatter_blocks(self, rows, came):
        if self.tensor != 4:
            return [rows]
        half = BLOCK // 2
        own, one, two = rows[:BLOCK], rows[BLOCK : 2 * BLOCK], rows[2 * BLOCK : 3 * BLOCK]
        one = jnp.concatenate([(one[:half].astype(f32) + came[0].astype(f32)).astype(bf16), one[half:]])
        two = jnp.concatenate([two[:half], (two[half:].astype(f32) + came[1].astype(f32)).astype(bf16)])
        return [own, one, two]

    def scatter_last(self, blocks, earlier):
        if self.tensor != 4:
            return [lax.psum_scatter(blocks[0], "tensor", scatter_dimension=0, tiled=True)]
        came = [self.over_tensor(blocks[k], k) for k in (1, 2)]
        return [blocks[0]] + (pinned(came, earlier) if earlier else came)

    def spread_tensor(self, values):
        return [values] + [self.over_tensor(values, k) for k in range(1, self.tensor)]

    def sum_tensor(self, values):
        return sum(self.spread_tensor(values)[1:], values)


def local(
    net_of,
    tokens,
    norm_gain,
    gate_proj,
    inner_proj,
    shared_proj,
    step_proj,
    conv_inner,
    conv_inner_bias,
    conv_shared,
    conv_shared_bias,
    step_bias,
    decay_log,
    skip_gain,
    out_gain,
    out_proj,
    cotangent,
):
    net = net_of()
    place, chips = net.place, net.chips
    channels = gate_proj.shape[1]
    heads = step_proj.shape[1]
    width = channels + 2 * STATE
    token_rows = tokens.astype(f32)
    inverse = lax.rsqrt(jnp.mean(token_rows * token_rows, axis=-1, keepdims=True) + epsilon)
    unit = token_rows * inverse
    normed_low = (unit * norm_gain).astype(bf16)
    padding = jnp.zeros((step_proj.shape[0], LANES - heads), bf16)
    scan_shard = jnp.concatenate([inner_proj, shared_proj, step_proj, padding], axis=1)
    scan_mine = net.gather_far(net.gather_near(scan_shard), [])
    row_pieces = net.gather_first(normed_low)
    reached = scan_mine[1:]
    cot_copy = copied(cotangent, row_pieces[1:2])
    joint = joint_shard(gate_proj, out_proj, [cot_copy])
    row_pieces = net.gather_last(row_pieces, [])
    scan_pieces = net.gather_cores(scan_mine, row_pieces[3:], [])
    cot_pieces = net.gather_first(pinned([cot_copy], row_pieces[3:] + scan_pieces[chips:])[0])
    joint_mine = net.gather_near(pinned([joint], reached)[0])

    taps = jnp.concatenate(
        [
            jnp.concatenate([conv_inner, conv_inner_bias[None]]),
            jnp.concatenate([conv_shared, conv_shared_bias[None]]),
        ],
        axis=1,
    )
    taps = jnp.pad(taps, ((0, 8 - CONV - 1), (0, 0)))
    rates = -jnp.exp(decay_log)
    head_rows = jnp.pad(jnp.stack([step_bias, rates]), ((0, 6), (0, LANES - heads)))
    skip_row = jnp.repeat(skip_gain, HEAD_DIM)[None]
    gain = out_gain[None]

    raw, scan_full, rows = product(
        place,
        row_pieces,
        scan_pieces,
        raw_epilogue,
        [],
        [(width + LANES, f32)],
        "project",
    )
    scanned, pre, states = scan_forward(raw, taps, head_rows, skip_row, [])
    cot_pieces = net.gather_last(cot_pieces, [scanned])
    joint_mine = net.gather_far(joint_mine, [scanned])
    gate, gated, grad_out, token_sums, joint_full, cot_rows = product(
        place,
        cot_pieces,
        net.gather_cores(joint_mine, cot_pieces[3:], []),
        mix_epilogue,
        [(rows, False), (stay(scanned), True), (gain, False)],
        [(channels, f32), (channels, f32), (channels, f32), (None, 2)],
        "mix",
    )
    token_sums = net.sum_tensor(token_sums)
    out_low, gate_back, scan_grad, gain_grad = gating(grad_out, gated, scanned, gate, token_sums, gain)
    keep, give = weight_grads(
        place, chips, [rows, cot_rows], [gate_back, out_low], [], "grad_joint_proj"
    )
    joint_come = net.over_core(give)
    branch, _ = back(place, [out_low], [(joint_full, 1)], None, "branch", [give])
    joint_own, joint_others = pairs(keep, joint_come, [branch])
    came = net.scatter_far(joint_others)
    branch_came = net.scatter_first(branch, joint_others[:1])
    held = scan_backward(
        0, raw, pre, scan_grad, states, taps, head_rows, skip_row, None, joint_others[:1]
    )
    if came:
        *came, one, two = pinned(came + branch_came, [held[1]])
        branch_came = [one, two]
    joint_arrived = net.scatter_near(net.scatter_join(joint_others, came), came)
    branch_parts = net.scatter_last(net.scatter_blocks(branch, branch_came), [])
    scan_back, sums, head_sums, _, _ = scan_backward(
        1, raw, pre, scan_grad, states, taps, head_rows, skip_row, held, came
    )
    norm_rows, norm_sums = back(
        place, [gate_back, stay(scan_back)], [(joint_full, 0), (scan_full, 0)], rows, "grad_normed"
    )
    keep, give = weight_grads(
        place,
        chips,
        [rows],
        [stay(scan_back)],
        [sums, gain_grad, norm_sums, head_sums],
        "grad_scan_proj",
        joint_arrived + branch_parts[1:],
    )
    norm_came = net.scatter_first(norm_rows, joint_arrived)
    scan_own, scan_others = pairs(keep, net.over_core(give))
    came = net.scatter_far(scan_others)
    came = pinned(came, []) if came else came
    norm_came = pinned(norm_came, scan_others[:1]) if norm_came else norm_came
    joined = net.scatter_join(scan_others, came)
    *joint_arrived, = pinned(joint_arrived, joined[1:2])
    scan_arrived = net.scatter_near(joined, came)
    norm_parts = net.scatter_last(net.scatter_blocks(norm_rows, norm_came), joined[1:])
    grad_normed = total_of(norm_parts[0].astype(f32), norm_parts[1:])
    mixed = total_of(token_rows, branch_parts).astype(bf16)
    joint_total = total_of(joint_own, joint_arrived)
    grad_gate_proj, grad_out_proj = joint_total[:, :channels], joint_total[:, channels:].T
    spread = grad_normed * norm_gain
    grad_tokens = (
        cotangent.astype(f32)
        + inverse * spread
        - unit * (inverse * jnp.mean(spread * unit, axis=-1, keepdims=True))
    )
    grad_inner_proj, step_part, grad_conv_inner, inner_bias, gain_part, head_part, common = collect(
        [scan_own] + scan_arrived, channels, []
    )
    grad_shared_proj, grad_conv_shared, shared_bias, norm_part = finish(
        net.spread_tensor(common), norm_gain[None]
    )
    return (
        mixed,
        grad_tokens,
        norm_part.reshape(-1),
        grad_gate_proj,
        grad_inner_proj,
        grad_shared_proj,
        step_part[:, :heads],
        grad_conv_inner,
        inner_bias.reshape(-1),
        grad_conv_shared,
        shared_bias.reshape(-1),
        head_part[0, :heads],
        head_part[1, :heads] * rates,
        head_part[2, :heads],
        gain_part.reshape(-1),
        grad_out_proj,
    )


def solution(mesh):
    dp, tensor = mesh.shape["dp"], mesh.shape["tensor"]

    def on_device(*args):
        return local(lambda: Net(dp, tensor), *args)

    return jax.shard_map(
        on_device,
        mesh=mesh,
        in_specs=(
            P(("dp", "tensor"), None),
            P(),
            P("dp", "tensor"),
            P("dp", "tensor"),
            P("dp", None),
            P("dp", "tensor"),
            P(None, "tensor"),
            P("tensor"),
            P(),
            P(),
            P("tensor"),
            P("tensor"),
            P("tensor"),
            P("tensor"),
            P("tensor", "dp"),
            P(("dp", "tensor"), None),
        ),
        out_specs=(
            P(("dp", "tensor"), None),
            P(("dp", "tensor"), None),
            P(),
            P("dp", "tensor"),
            P("dp", "tensor"),
            P("dp", None),
            P("dp", "tensor"),
            P(None, "tensor"),
            P("tensor"),
            P(),
            P(),
            P("tensor"),
            P("tensor"),
            P("tensor"),
            P("tensor"),
            P("tensor", "dp"),
        ),
        check_vma=False,
    )
```

```python
import functools

import jax
import jax.numpy as jnp
from jax import lax
from jax.experimental import pallas as pl
from jax.experimental.pallas import tpu as pltpu
from jax.sharding import PartitionSpec as P

DI = 3072
epsilon = 1e-05
HEAD_DIM = 64
STATE = 128
CONV = 4
SEQ = 1024
SPAN = 256
CHUNK = 128
LANES = 128
NEVER = -1e30
NEAR = jax.ShapeDtypeStruct
f32 = jnp.float32
bf16 = jnp.bfloat16
highest = lax.Precision.HIGHEST


def dot(first, second, first_dim=1, second_dim=0, precision=None):
    return lax.dot_general(
        first,
        second,
        (((first_dim,), (second_dim,)), ((), ())),
        precision=precision,
        preferred_element_type=f32,
    )


def sigmoid(values):
    return 0.5 * jnp.tanh(0.5 * values) + 0.5


def places(dim):
    return lax.broadcasted_iota(jnp.int32, (CHUNK, LANES), dim)


def exact_dot(ones, values, parts):
    split = []
    for _ in range(parts):
        split.append(values.astype(bf16))
        values = values - split[-1].astype(f32)
    result = dot(ones, jnp.concatenate(split, axis=1))
    return sum(result[:, i * LANES : (i + 1) * LANES] for i in range(parts))


def decays(step_raw, heads_ref):
    raw = step_raw + heads_ref[0:1]
    small = jnp.exp(-jnp.abs(raw))
    log_one = jnp.where(small < 1e-3, small - 0.5 * small * small, jnp.log(1.0 + small))
    steps = jnp.maximum(raw, 0.0) + log_one
    summed = exact_dot((places(0) >= places(1)).astype(bf16), steps * heads_ref[1:2], 3)
    return steps, sigmoid(raw), summed, summed - jnp.log(steps)


def pair_of(first, second):
    return jnp.concatenate([first, second], axis=0)


def forward_kernel(raw_ref, taps_ref, heads_ref, skip_ref, *refs):
    scanned_ref, pre_ref, states_ref, state, before = refs[-5:]
    chunk = pl.program_id(0)
    channels = skip_ref.shape[1]
    width = channels + 2 * STATE

    @pl.when(chunk % (SEQ // CHUNK) == 0)
    def _():
        state[...] = jnp.zeros_like(state)
        before[...] = jnp.zeros_like(before)

    raw = raw_ref[:, :width]
    extended = jnp.concatenate([before[...], raw], axis=0)
    pre = taps_ref[CONV : CONV + 1] + taps_ref[CONV - 1 : CONV] * raw
    for tap in range(CONV - 1):
        start = 8 - (CONV - 1) + tap
        pre = pre + taps_ref[tap : tap + 1] * extended[start : start + CHUNK]
    before[...] = raw[CHUNK - 8 :]
    pre_ref[...] = pre
    act = (pre * sigmoid(pre)).astype(bf16)
    writes = act[:, channels : channels + STATE]
    reads = act[:, channels + STATE :]
    _, _, summed, shifted = decays(raw_ref[:, width:], heads_ref)
    summed_t, shifted_t = summed.T, shifted.T
    tail_t = jnp.exp(summed_t[:, CHUNK - 1 :] - shifted_t)
    scores = dot(reads, writes, 1, 1)
    writes_t = writes.astype(f32).T
    causal = places(0) >= places(1)
    left = places(1) < HEAD_DIM
    states_ref[...] = state[...].astype(bf16)
    for pair in range(channels // LANES):
        cols = slice(pair * LANES, (pair + 1) * LANES)
        values = act[:, cols].astype(f32)
        both = pair_of(jnp.where(left, values, 0.0), jnp.where(left, 0.0, values)).astype(bf16)
        mixes, tails, grown = [], [], []
        for head in (2 * pair, 2 * pair + 1):
            here = jnp.broadcast_to(summed[:, head : head + 1], (CHUNK, LANES))
            decay = jnp.exp(jnp.where(causal, here - shifted_t[head : head + 1], NEVER))
            mixes.append((scores * decay).astype(bf16))
            tails.append((writes_t * tail_t[head : head + 1]).astype(bf16))
            grown.append(here)
        stacked = pair_of(jnp.concatenate(mixes, axis=1), jnp.concatenate(tails, axis=1))
        out = dot(stacked, both)
        entering = state[:, cols]
        factor = jnp.exp(jnp.where(left, grown[0], grown[1]))
        across = dot(reads, entering.astype(bf16)) * factor
        scanned_ref[:, cols] = out[:CHUNK] + across + values * skip_ref[:, cols]
        state[:, cols] = entering * factor[CHUNK - 1 :] + out[CHUNK:]


def backward_kernel(part, n_deps, *refs):
    raw_ref, pre_ref, grad_ref, states_ref, taps_ref, heads_ref, skip_ref = refs[:7]
    n_held = 5 if part else 0
    held, refs = refs[7 : 7 + n_held], refs[7 + n_held + n_deps :]
    low_ref, sums_ref, head_sums_ref, carry, after, wide = refs
    step = pl.program_id(0)
    channels = skip_ref.shape[1]
    width = channels + 2 * STATE

    @pl.when(step == 0)
    def _():
        if part:
            for ref, source in zip((sums_ref, head_sums_ref, carry, after), held[1:], strict=True):
                ref[...] = source[...]
        else:
            sums_ref[...] = jnp.zeros_like(sums_ref)
            head_sums_ref[...] = jnp.zeros_like(head_sums_ref)

    @pl.when((step + part * pl.num_programs(0)) % (SEQ // CHUNK) == 0)
    def _():
        carry[...] = jnp.zeros_like(carry)
        after[...] = jnp.zeros_like(after)

    pre = pre_ref[...]
    gate = sigmoid(pre)
    act = (pre * gate).astype(bf16)
    writes = act[:, channels : channels + STATE]
    reads = act[:, channels + STATE :]
    steps, slopes, summed, shifted = decays(raw_ref[:, width:], heads_ref)
    summed_t = summed.T
    scores_t = dot(writes, reads, 1, 1)
    causal = places(0) <= places(1)
    earlier = places(0) < places(1)
    suffix = (places(0) >= places(1)).astype(bf16)
    left = places(1) < HEAD_DIM
    score_grads = jnp.zeros((CHUNK, LANES), f32)
    spans, inner_grads, lasts = [], [], []
    for pair in range(channels // LANES):
        cols = slice(pair * LANES, (pair + 1) * LANES)
        values = act[:, cols].astype(f32)
        both = pair_of(jnp.where(left, values, 0.0), jnp.where(left, 0.0, values)).astype(bf16)
        grad_low = grad_ref[:, cols]
        grad = grad_low.astype(f32)
        grad_both = pair_of(jnp.where(left, grad, 0.0), jnp.where(left, 0.0, grad)).astype(bf16)
        products = dot(both, grad_low, 1, 1)
        mixes, crossing, grown, tails = [], [], [], []
        for place, head in enumerate((2 * pair, 2 * pair + 1)):
            here = jnp.broadcast_to(shifted[:, head : head + 1], (CHUNK, LANES))
            decay = jnp.exp(jnp.where(causal, summed_t[head : head + 1] - here, NEVER))
            product = products[place * CHUNK : (place + 1) * CHUNK]
            score_grads = score_grads + decay * product
            mix = scores_t * decay
            mixes.append(mix.astype(bf16))
            crossing.append((mix * product).astype(bf16))
            level = jnp.broadcast_to(summed[:, head : head + 1], (CHUNK, LANES))
            grown.append(level)
            tails.append(level[CHUNK - 1 :] - here)
        sums = dot(pair_of(*crossing), suffix)
        for place in range(2):
            piece = jnp.where(earlier, sums[place * CHUNK : (place + 1) * CHUNK], 0.0)
            spans.append(jnp.sum(piece, axis=0, keepdims=True))
        within = dot(jnp.concatenate(mixes, axis=1), grad_both)
        factor = jnp.exp(jnp.where(left, grown[0], grown[1]))
        tail = jnp.exp(jnp.where(left, tails[0], tails[1]))
        leaving = carry[:, cols]
        entering = states_ref[:, cols]
        later = tail * dot(writes, leaving.astype(bf16))
        both_grads = within + later
        inner_grads.append(both_grads + skip_ref[:, cols] * grad)
        spread = factor * grad
        spread_low = spread.astype(bf16)
        wide[0:CHUNK, cols] = spread_low
        wide[CHUNK : 2 * CHUNK, cols] = (tail * values).astype(bf16)
        wide[2 * CHUNK : 3 * CHUNK, cols] = (spread * dot(reads, entering)).astype(bf16)
        wide[3 * CHUNK : 4 * CHUNK, cols] = (values * later).astype(bf16)
        wide[4 * CHUNK : 5 * CHUNK, cols] = (values * both_grads).astype(bf16)
        held = jnp.sum(entering.astype(f32) * leaving, axis=0, keepdims=True) * factor[CHUNK - 1 :]
        sums_ref[CONV + 1 : CONV + 2, cols] += jnp.sum(grad * values, axis=0, keepdims=True)
        wide[5 * CHUNK :, cols] = jnp.broadcast_to(held, (16, LANES)).astype(bf16)
        lasts.append(factor[CHUNK - 1 :])
    reads_t = reads.astype(f32).T.astype(bf16)
    score_low = score_grads.astype(bf16)
    spread_all = wide[0:CHUNK, :]
    read_grads = dot(score_low, writes, 0, 0) + dot(spread_all, states_ref[...], 1, 1)
    write_grads = dot(score_low, reads) + dot(wide[CHUNK : 2 * CHUNK, :], carry[...].astype(bf16), 1, 1)
    of_head = (
        lax.broadcasted_iota(jnp.int32, (channels, LANES), 0) // HEAD_DIM
        == lax.broadcasted_iota(jnp.int32, (channels, LANES), 1)
    )
    reduced = dot(wide[2 * CHUNK :, :], of_head.astype(bf16))
    carry[...] = carry[...] * jnp.concatenate(lasts, axis=1) + dot(reads_t, spread_all)
    both_sums = reduced[2 * CHUNK : 3 * CHUNK]
    held_heads = reduced[3 * CHUNK : 3 * CHUNK + 1]
    span_rows = jnp.concatenate(spans + [jnp.zeros((LANES - len(spans), LANES), f32)], axis=0)
    upto = [places(0) <= places(1), places(0) > places(1)]
    upto = jnp.concatenate([v.astype(bf16) for v in upto], axis=1)
    log_grads = exact_dot(upto, reduced[: 2 * CHUNK], 2) + span_rows.T + held_heads
    ratio = jnp.where(steps > 1e-30, slopes / steps, 1.0)
    step_grads = both_sums * ratio + heads_ref[1:2] * log_grads * slopes
    head_sums_ref[0:1] += jnp.sum(step_grads, axis=0, keepdims=True)
    head_sums_ref[1:2] += jnp.sum(log_grads * steps, axis=0, keepdims=True)

    @pl.when(part * pl.num_programs(0) + step == 2 * pl.num_programs(0) - 1)
    def _():
        skip_rows = jnp.broadcast_to(sums_ref[CONV + 1 : CONV + 2, :channels], (8, channels))
        head_sums_ref[2:3] = dot(skip_rows, of_head.astype(f32), precision=highest)[0:1]

    raw = raw_ref[:, :width]
    act_grads = jnp.concatenate(inner_grads + [write_grads, read_grads], axis=1)
    pre_grads = act_grads * (gate * (1.0 + pre * (1.0 - gate)))
    extended = jnp.concatenate([pre_grads, after[...]], axis=0)
    after[...] = pre_grads[:8]
    sums_ref[CONV : CONV + 1] += jnp.sum(pre_grads, axis=0, keepdims=True)
    raw_grads = taps_ref[CONV - 1 : CONV] * pre_grads
    sums_ref[CONV - 1 : CONV] += jnp.sum(raw * pre_grads, axis=0, keepdims=True)
    for tap in range(CONV - 1):
        moved = extended[CONV - 1 - tap : CONV - 1 - tap + CHUNK]
        raw_grads = raw_grads + taps_ref[tap : tap + 1] * moved
        sums_ref[tap : tap + 1] += jnp.sum(raw * moved, axis=0, keepdims=True)
    low_ref[:, :width] = raw_grads.astype(bf16)
    low_ref[:, width:] = step_grads.astype(bf16)


def stay(values):
    return pltpu.with_memory_space_constraint(values, pltpu.HBM)


def scan_forward(raw, taps, heads, skip, earlier):
    tokens, full = raw.shape
    channels = skip.shape[1]
    width = channels + 2 * STATE
    count = tokens // CHUNK
    by_chunk = lambda shape: pl.BlockSpec(shape, lambda s: (s, 0))
    whole = lambda v: pl.BlockSpec(v.shape, lambda s: (0, 0))
    return pl.pallas_call(
        forward_kernel,
        grid=(count,),
        in_specs=[by_chunk((CHUNK, full)), whole(taps), whole(heads), whole(skip)]
        + [pl.BlockSpec(memory_space=pl.ANY)] * len(earlier),
        out_specs=[
            by_chunk((CHUNK, channels)),
            by_chunk((CHUNK, width)),
            by_chunk((STATE, channels)),
        ],
        scratch_shapes=[pltpu.VMEM((STATE, channels), f32), pltpu.VMEM((8, width), f32)],
        out_shape=[
            pltpu.HBM((tokens, channels), f32),
            pltpu.HBM((tokens, width), f32),
            pltpu.HBM((count * STATE, channels), bf16),
        ],
        compiler_params=pltpu.CompilerParams(vmem_limit_bytes=12 << 20),
        name="scan_forward",
    )(stay(raw), taps, heads, skip, *earlier)


def scan_backward(part, raw, pre, grad, states, taps, heads, skip, held, earlier):
    tokens, full = raw.shape
    channels = skip.shape[1]
    width = channels + 2 * STATE
    count = tokens // CHUNK
    half = count // 2
    last = count - 1 - part * half
    by_chunk = lambda shape: pl.BlockSpec(shape, lambda s: (last - s, 0))
    whole = lambda shape: pl.BlockSpec(shape, lambda s: (0, 0))
    kept = [(8, width), (8, LANES), (STATE, channels), (8, width)]
    free = pl.BlockSpec(memory_space=pl.ANY)
    held = list(held) if part else []
    return pl.pallas_call(
        functools.partial(backward_kernel, part, len(earlier)),
        grid=(half,),
        in_specs=[
            by_chunk((CHUNK, full)),
            by_chunk((CHUNK, width)),
            by_chunk((CHUNK, channels)),
            by_chunk((STATE, channels)),
            whole(taps.shape),
            whole(heads.shape),
            whole(skip.shape),
        ]
        + ([free] + [whole(shape) for shape in kept] if part else [])
        + [free] * len(earlier),
        out_specs=[by_chunk((CHUNK, full))] + [whole(shape) for shape in kept],
        scratch_shapes=[pltpu.VMEM((5 * CHUNK + 16, channels), bf16)],
        out_shape=[pltpu.HBM((tokens, full), bf16)] + [pltpu.HBM(shape, f32) for shape in kept],
        input_output_aliases={7: 0} if part else {},
        compiler_params=pltpu.CompilerParams(vmem_limit_bytes=12 << 20),
        name=f"scan_backward_{part}",
    )(stay(raw), stay(pre), stay(grad), stay(states), taps, heads, skip, *[stay(v) for v in held], *earlier)


BLOCK = 256
LIMIT = 16 << 20
SMALL_LIMIT = 12 << 20
SMALL = 16
anywhere = pl.BlockSpec(memory_space=pl.ANY)
in_vmem = pl.BlockSpec(memory_space=pltpu.VMEM)


def column_sums(values, count):
    rows = [
        jnp.sum(values[i * LANES : (i + 1) * LANES].T, axis=0, keepdims=True)
        for i in range(count // LANES)
    ]
    return jnp.concatenate(rows, axis=0)


def fold(values):
    total = values[:, :LANES]
    for start in range(LANES, values.shape[1], LANES):
        total = total + values[:, start : start + LANES]
    return total


def shard_rows(place, index, chips, height):
    core, chip = index // chips, index % chips
    return pl.multiple_of(((place[0] ^ chip) * 2 + (place[1] ^ core)) * height, height)


def row_start(place, start):
    if isinstance(start, int):
        return pl.multiple_of((start // BLOCK ^ place[2]) * BLOCK + start % BLOCK, LANES)
    return pl.multiple_of((start // BLOCK ^ place[2]) * BLOCK, BLOCK)


def product_kernel(heights, chips, epilogue, n_extra, n_deps, n_out, place, *refs):
    n_rows, n_full = len(heights), 2 * chips
    row_refs, refs = refs[:n_rows], refs[n_rows:]
    full_refs, refs = refs[:n_full], refs[n_full:]
    extra, refs = refs[:n_extra], refs[n_extra + n_deps :]
    outs, (full, rows, sems) = refs[:n_out], refs[n_out:]
    step = pl.program_id(0)
    starts = [sum(heights[:i]) for i in range(n_rows)]
    shard = full.shape[0] // n_full
    row_copies = [
        pltpu.make_async_copy(
            row_refs[i], rows.at[pl.ds(row_start(place, starts[i]), heights[i])], sems.at[i]
        )
        for i in range(n_rows)
    ]
    full_copies = [
        pltpu.make_async_copy(
            full_refs[i], full.at[pl.ds(shard_rows(place, i, chips, shard), shard)], sems.at[n_rows + i]
        )
        for i in range(n_full)
    ]

    @pl.when(step == 0)
    def _():
        for copy in full_copies + row_copies:
            copy.start()
        for copy in full_copies:
            copy.wait()

    for i in range(n_rows):

        @pl.when(step == starts[i] // BLOCK)
        def _(i=i):
            row_copies[i].wait()

    block = rows[pl.ds(row_start(place, step * BLOCK), BLOCK), :]
    epilogue(step ^ place[2], block, full, extra, outs)


def product(place, row_pieces, full_pieces, epilogue, extra, outs, name, earlier=()):
    chips = len(full_pieces) // 2
    heights = tuple(piece.shape[0] for piece in row_pieces)
    tokens, depth = sum(heights), row_pieces[0].shape[1]
    columns = full_pieces[0].shape[1]
    by_block = lambda cols: pl.BlockSpec((BLOCK, cols), lambda s, p: (s ^ p[2], 0))
    out_specs, out_shape = [], []
    for cols, dtype in outs:
        if cols is None:
            shape = (dtype * tokens // LANES, LANES)
            out_specs.append(pl.BlockSpec(shape, lambda s, p: (0, 0)))
            out_shape.append(jax.ShapeDtypeStruct(shape, f32))
        else:
            out_specs.append(by_block(cols))
            out_shape.append((pltpu.HBM if name == "project" else NEAR)((tokens, cols), dtype))
    return pl.pallas_call(
        functools.partial(product_kernel, heights, chips, epilogue, len(extra), len(earlier), len(outs)),
        grid_spec=pltpu.PrefetchScalarGridSpec(
            num_scalar_prefetch=1,
            grid=(tokens // BLOCK,),
            in_specs=[anywhere] * (len(row_pieces) + len(full_pieces))
            + [by_block(v.shape[1]) if by else in_vmem for v, by in extra]
            + [anywhere] * len(earlier),
            out_specs=out_specs + [in_vmem, in_vmem],
            scratch_shapes=[pltpu.SemaphoreType.DMA((len(row_pieces) + len(full_pieces),))],
        ),
        out_shape=out_shape + [pltpu.VMEM((depth, columns), bf16), pltpu.VMEM((tokens, depth), bf16)],
        compiler_params=pltpu.CompilerParams(vmem_limit_bytes=LIMIT),
        name=name,
    )(place, *[stay(v) for v in row_pieces + full_pieces], *[v for v, _ in extra], *earlier)


def slices(columns):
    return [slice(start, min(start + 256, columns)) for start in range(0, columns, 256)]


def raw_epilogue(index, block, full, extra, outs):
    (raw,) = outs
    for cols in slices(raw.shape[1]):
        raw[:, cols] = dot(block, full[:, cols])


def mix_epilogue(index, block, full, extra, outs):
    rows, scanned, gain = extra
    gate, gated, grad, sums = outs
    channels = gate.shape[1]
    squares = jnp.zeros((BLOCK, LANES), f32)
    dots = jnp.zeros((BLOCK, LANES), f32)
    here = pl.ds(pl.multiple_of(index * BLOCK, BLOCK), BLOCK)
    for cols in slices(channels):
        value = dot(rows[here, :], full[:, cols])
        out = dot(block, full[:, channels + cols.start : channels + cols.stop])
        gate[:, cols] = value
        grad[:, cols] = out
        product = scanned[:, cols] * (value * sigmoid(value))
        gated[:, cols] = product
        squares = squares + fold(product * product)
        dots = dots + fold(out * gain[:, cols] * product)
    per = BLOCK // LANES
    half = sums.shape[0] // 2
    sums[pl.ds(index * per, per), :] = column_sums(squares, BLOCK)
    sums[pl.ds(half + index * per, per), :] = column_sums(dots, BLOCK)


def shard_kernel(gate_proj, out_proj, *refs):
    out = refs[-1]
    channels, height = out_proj.shape
    out[:, :channels] = gate_proj[...]
    place = [lax.broadcasted_iota(jnp.int32, (height, height), dim) for dim in range(2)]
    same = (place[0] == place[1]).astype(bf16)
    out[:, channels:] = dot(same, out_proj[...], 1, 1).astype(bf16)


def joint_shard(gate_proj, out_proj, earlier):
    return pl.pallas_call(
        shard_kernel,
        in_specs=[in_vmem] * 2 + [anywhere] * len(earlier),
        out_specs=in_vmem,
        out_shape=jax.ShapeDtypeStruct((gate_proj.shape[0], 2 * gate_proj.shape[1]), bf16),
        name="joint_shard",
    )(gate_proj, out_proj, *earlier)


def columns_of(row):
    return jnp.broadcast_to(row, (LANES, LANES)).T


def gating_kernel(grad_out, gated, gate, sums, gain, scanned, out_low, gate_back, scan_grad, gain_grad):
    step = pl.program_id(0)
    half = sums.shape[0] // 2

    @pl.when(step == 0)
    def _():
        gain_grad[...] = jnp.zeros_like(gain_grad)

    for part in range(BLOCK // LANES):
        rows = slice(part * LANES, (part + 1) * LANES)
        index = step * (BLOCK // LANES) + part
        here = pl.ds(pl.multiple_of(index * LANES, LANES), LANES)
        ratio_row = lax.rsqrt(sums[pl.ds(index, 1), :] / DI + epsilon)
        dots = sums[pl.ds(half + index, 1), :]
        ratio = columns_of(ratio_row)
        pull = columns_of(ratio_row * ratio_row * ratio_row / DI * dots)
        for start in range(0, gate.shape[1], LANES):
            cols = slice(start, start + LANES)
            held, value = gated[here, cols], gate[here, cols]
            scaled = grad_out[here, cols] * ratio
            out_low[rows, cols] = (gain[:, cols] * (held * ratio)).astype(bf16)
            gain_grad[0:1, cols] += jnp.sum(scaled * held, axis=0, keepdims=True)
            grad = gain[:, cols] * scaled - held * pull
            slope = sigmoid(value)
            scan_grad[rows, cols] = (grad * (value * slope)).astype(bf16)
            gate_grad = grad * scanned[rows, cols] * (slope * (1.0 + value * (1.0 - slope)))
            gate_back[rows, cols] = gate_grad.astype(bf16)


def gating(grad_out, gated, scanned, gate, sums, gain):
    tokens, columns = gated.shape
    block = pl.BlockSpec((BLOCK, columns), lambda s: (s, 0))
    return pl.pallas_call(
        gating_kernel,
        grid=(tokens // BLOCK,),
        in_specs=[in_vmem] * 5 + [block],
        out_specs=[block] * 3 + [pl.BlockSpec((8, columns), lambda s: (0, 0))],
        out_shape=[NEAR((tokens, columns), bf16)] * 2
        + [pltpu.HBM((tokens, columns), bf16)] + [jax.ShapeDtypeStruct((8, columns), f32)],
        compiler_params=pltpu.CompilerParams(vmem_limit_bytes=SMALL_LIMIT),
        name="gating",
    )(grad_out, gated, gate, sums, gain, stay(scanned))


def grads_kernel(n_rows, wide, place, *refs):
    rows, lows = refs[:n_rows], refs[n_rows : 2 * n_rows]
    keep, give = refs[-2:]
    shard = wide // 2
    first = place[1] == 0
    lanes = pl.ds(pl.multiple_of((pl.program_id(0) ^ place[0]) * wide, LANES), wide)
    start = 0
    for row, low in zip(rows, lows, strict=True):
        for cols in slices(low.shape[1]):
            value = dot(row[:, lanes], low[:, cols], 0, 0)
            one, two = value[:shard], value[shard:]
            out = slice(start + cols.start, start + cols.stop)
            keep[0, :shard, out] = jnp.where(first, one, two).astype(bf16)
            give[0, :shard, out] = jnp.where(first, two, one).astype(bf16)
        start += low.shape[1]


def fill_small(small, sums, gain_grad, norm_grad, head_sums):
    rest = norm_grad.shape[1] - small.shape[1]
    small[...] = jnp.zeros_like(small)
    small[0:8, : sums.shape[1]] = sums[...]
    small[8:9, : gain_grad.shape[1]] = gain_grad[0:1, :]
    small[9:10, :] = norm_grad[0:1, : small.shape[1]]
    small[10:11, :rest] = norm_grad[0:1, small.shape[1] :]
    small[11:14, :LANES] = head_sums[0:3, :]


def small_kernel(n_rows, wide, place, *refs):
    keep, give, small = refs[-3:]
    grads_kernel(n_rows, wide, place, *refs[:-1])
    fill_small(small, *refs[2 * n_rows : 2 * n_rows + 4])
    low = small[...].astype(bf16)
    shard = keep.shape[1] - SMALL
    keep[0, shard:] = low
    give[0, shard:] = low


def whole_grads_kernel(chips, n_rows, n_small, place, *refs):
    rows, lows = refs[:n_rows], refs[n_rows : 2 * n_rows]
    keep, give, acc, small = refs[-4:]
    depth = acc.shape[0]
    shard = depth // (2 * chips)
    start = 0
    for row, low in zip(rows, lows, strict=True):
        cols = slice(start, start + low.shape[1])
        for lanes in slices(depth):
            acc[lanes, cols] = dot(row[:, lanes], low[...], 0, 0)
        start = cols.stop
    for k in range(chips):
        for out, core in ((keep, place[1]), (give, 1 - place[1])):
            at = pl.multiple_of(((place[0] ^ k) * 2 + core) * shard, shard)
            out[k, :shard] = acc[pl.ds(at, shard), :].astype(bf16)
    if n_small:
        fill_small(small, *refs[2 * n_rows : 2 * n_rows + n_small])
        for k in range(chips):
            keep[k, shard:] = small[...].astype(bf16)
            give[k, shard:] = small[...].astype(bf16)


def weight_grads(place, chips, rows, lows, small, name, earlier=()):
    tokens, depth = rows[0].shape
    columns = sum(v.shape[1] for v in lows)
    wide = depth // chips
    shard = wide // 2
    height = shard + (SMALL if small else 0)
    if wide % LANES:
        return pl.pallas_call(
            functools.partial(whole_grads_kernel, chips, len(rows), len(small)),
            in_specs=[pl.BlockSpec(memory_space=pltpu.SMEM)]
            + [in_vmem] * (2 * len(rows) + len(small))
            + [anywhere] * len(earlier),
            out_specs=[in_vmem] * 2,
            out_shape=[jax.ShapeDtypeStruct((chips, height, columns), bf16)] * 2,
            scratch_shapes=[pltpu.VMEM((depth, columns), f32), pltpu.VMEM((SMALL, columns), f32)],
            compiler_params=pltpu.CompilerParams(vmem_limit_bytes=2 * LIMIT),
            name=name,
        )(place, *rows, *lows, *small, *earlier)
    out = pl.BlockSpec((1, height, columns), lambda k, p: (k, 0, 0))
    return pl.pallas_call(
        functools.partial(small_kernel if small else grads_kernel, len(rows), wide),
        grid_spec=pltpu.PrefetchScalarGridSpec(
            num_scalar_prefetch=1,
            grid=(chips,),
            in_specs=[in_vmem] * (2 * len(rows) + len(small))
            + [anywhere] * len(earlier),
            out_specs=[out, out],
            scratch_shapes=[pltpu.VMEM((SMALL, columns), f32)] if small else [],
        ),
        out_shape=[(pltpu.HBM if small else NEAR)((chips, height, columns), bf16)] * 2,
        compiler_params=pltpu.CompilerParams(vmem_limit_bytes=SMALL_LIMIT),
        name=name,
    )(place, *rows, *lows, *small, *earlier)


def pairs_kernel(chips, streamed, keep, come, *refs):
    if streamed:
        refs, (kept, arrived, sems) = refs[:-3], refs[-3:]
        copies = []
        for k in range(chips):
            for i, (source, target) in enumerate(((keep, kept), (come, arrived))):
                copies.append(pltpu.make_async_copy(source.at[k], target.at[k], sems.at[2 * k + i]))
        for copy in copies:
            copy.start()
        keep, come = kept, arrived
    for k, out in enumerate(refs[-chips:]):
        if streamed:
            copies[2 * k].wait()
            copies[2 * k + 1].wait()
        out[...] = (keep[k].astype(f32) + come[k].astype(f32)).astype(out.dtype)


def pairs(keep, come, streamed, earlier=()):
    chips, rows, columns = keep.shape
    scratch = [pltpu.VMEM(keep.shape, bf16)] * 2 + [pltpu.SemaphoreType.DMA((2 * chips,))]
    out = pl.pallas_call(
        functools.partial(pairs_kernel, chips, streamed),
        in_specs=[anywhere if streamed else in_vmem] * 2 + [anywhere] * len(earlier),
        out_specs=[in_vmem] * chips,
        out_shape=[pltpu.HBM((rows, columns), f32)] + [pltpu.HBM((rows, columns), bf16)] * (chips - 1),
        scratch_shapes=scratch if streamed else [],
        compiler_params=pltpu.CompilerParams(vmem_limit_bytes=SMALL_LIMIT),
        name="pairs",
    )(keep, come, *earlier)
    return out[0], list(out[1:])


def back_kernel(parts, with_rows, place, *refs):
    count = len(parts)
    lows, fulls, refs = refs[:count], refs[count : 2 * count], refs[2 * count :]
    rows, out, sums = (refs[0], refs[-2], refs[-1]) if with_rows else (None, refs[-1], None)
    step = pl.program_id(0)
    if with_rows:

        @pl.when(step == 0)
        def _():
            sums[...] = jnp.zeros_like(sums)

    here = pl.ds(pl.multiple_of((step ^ place[2]) * BLOCK, BLOCK), BLOCK)
    for cols in slices(out.shape[1]):
        value = 0.0
        for low, full, part in zip(lows, fulls, parts, strict=True):
            wide = low.shape[1]
            value = value + dot(low[...], full[cols, part * wide : (part + 1) * wide], 1, 1)
        out[:, cols] = value.astype(bf16)
        if with_rows:
            sums[0:1, cols] += jnp.sum(value * rows[here, cols].astype(f32), axis=0, keepdims=True)


def back(place, lows, fulls, rows, name, earlier=()):
    tokens, depth = lows[0].shape[0], fulls[0][0].shape[0]
    by_block = lambda cols: pl.BlockSpec((BLOCK, cols), lambda s, p: (s ^ p[2], 0))
    extra = [] if rows is None else [rows]
    out = pl.pallas_call(
        functools.partial(back_kernel, tuple(part for _, part in fulls), rows is not None),
        grid_spec=pltpu.PrefetchScalarGridSpec(
            num_scalar_prefetch=1,
            grid=(tokens // BLOCK,),
            in_specs=[by_block(v.shape[1]) for v in lows]
            + [in_vmem] * (len(fulls) + len(extra))
            + [anywhere] * len(earlier),
            out_specs=[pl.BlockSpec((BLOCK, depth), lambda s, p: (s, 0))]
            + [pl.BlockSpec((8, depth), lambda s, p: (0, 0)) for _ in extra],
        ),
        out_shape=[jax.ShapeDtypeStruct((tokens, depth), bf16)]
        + [jax.ShapeDtypeStruct((8, depth), f32) for _ in extra],
        compiler_params=pltpu.CompilerParams(vmem_limit_bytes=SMALL_LIMIT),
        name=name,
    )(place, *lows, *[v for v, _ in fulls], *extra, *earlier)
    return out[0], out[1] if extra else None


def add_up(parts, rows, cols):
    value = parts[0][rows, cols].astype(f32)
    for part in parts[1:]:
        value = value + part[rows, cols].astype(f32)
    return value


def collect_kernel(count, n_deps, *refs):
    parts = refs[:count]
    inner, step, taps, bias, gain, heads, common, rest = refs[count + n_deps :]
    shard, channels = inner.shape
    full = parts[0].shape[1]
    own = slice(0, shard)
    for start in range(0, channels, 256):
        cols = slice(start, min(start + 256, channels))
        inner[:, cols] = add_up(parts, own, cols)
    step[...] = add_up(parts, own, slice(full - LANES, full))
    shared = slice(channels, channels + 2 * STATE)
    common[0:shard] = add_up(parts, own, shared).astype(bf16)
    small = add_up(parts, slice(shard, shard + SMALL), slice(0, full))
    taps[...] = small[0:CONV, :channels]
    bias[...] = small[CONV : CONV + 1, :channels]
    gain[...] = small[8:9, :channels]
    heads[...] = jnp.zeros_like(heads)
    heads[0:3] = small[11:14, :LANES]
    rest[...] = jnp.zeros_like(rest)
    rest[0:8] = small[0:8, shared]
    for piece in range(12):
        row, start = divmod(piece * LANES, full)
        target = slice(piece % 2 * LANES, (piece % 2 + 1) * LANES)
        rest[8 + piece // 2 : 9 + piece // 2, target] = small[9 + row : 10 + row, start : start + LANES]
    common[shard:] = rest[...].astype(bf16)


def collect(parts, channels, earlier):
    rows = parts[0].shape[0]
    shapes = [
        (rows - SMALL, channels), (rows - SMALL, LANES), (CONV, channels), (1, channels), (1, channels), (8, LANES)
    ]
    return pl.pallas_call(
        functools.partial(collect_kernel, len(parts), len(earlier)),
        in_specs=[in_vmem] * len(parts) + [anywhere] * len(earlier),
        out_specs=[in_vmem] * 7,
        out_shape=[jax.ShapeDtypeStruct(shape, f32) for shape in shapes]
        + [jax.ShapeDtypeStruct((rows, 2 * STATE), bf16)],
        scratch_shapes=[pltpu.VMEM((SMALL, 2 * STATE), f32)],
        compiler_params=pltpu.CompilerParams(vmem_limit_bytes=SMALL_LIMIT),
        name="collect",
    )(*parts, *earlier)


def finish_kernel(count, *refs):
    parts, norm_gain, (shared, taps, bias, norm) = refs[:count], refs[count], refs[count + 1 :]
    shard = shared.shape[0]
    every = slice(0, 2 * STATE)
    shared[...] = add_up(parts, slice(0, shard), every)
    small = add_up(parts, slice(shard, shard + SMALL), every)
    taps[...] = small[0:CONV]
    bias[...] = small[CONV : CONV + 1]
    for piece in range(norm.shape[0]):
        row, cols = 8 + piece // 2, slice(piece % 2 * LANES, (piece % 2 + 1) * LANES)
        norm[piece : piece + 1] = small[row : row + 1, cols] / norm_gain[piece : piece + 1]


def finish(parts, norm_gain):
    rows = parts[0].shape[0]
    shapes = [(rows - SMALL, 2 * STATE), (CONV, 2 * STATE), (1, 2 * STATE), norm_gain.shape]
    return pl.pallas_call(
        functools.partial(finish_kernel, len(parts)),
        in_specs=[in_vmem] * (len(parts) + 1),
        out_specs=[in_vmem] * 4,
        out_shape=[jax.ShapeDtypeStruct(shape, f32) for shape in shapes],
        name="finish",
    )(*parts, norm_gain)


def nothing(*refs):
    pass


def pinned(values, earlier):
    anywhere = pl.BlockSpec(memory_space=pl.ANY)
    held = pl.pallas_call(
        nothing,
        in_specs=[anywhere] * (len(values) + len(earlier)),
        out_specs=[anywhere] * len(values),
        out_shape=[jax.ShapeDtypeStruct(v.shape, v.dtype) for v in values],
        input_output_aliases={i: i for i in range(len(values))},
        name="pinned",
    )(*values, *earlier)
    return list(held)


def copy_kernel(source, *refs):
    refs[-1][...] = source[...]


def copied(value, earlier):
    whole = pl.BlockSpec(memory_space=pltpu.VMEM)
    return pl.pallas_call(
        copy_kernel,
        in_specs=[whole] + [pl.BlockSpec(memory_space=pl.ANY)] * len(earlier),
        out_specs=whole,
        out_shape=jax.ShapeDtypeStruct(value.shape, value.dtype),
        name="copied",
    )(value, *earlier)


def total_of(own, arrived):
    for value in arrived:
        own = own + value.astype(f32)
    return own


class Net:
    def __init__(self, dp, tensor):
        self.dp, self.tensor = dp, tensor
        self.chips = dp // 2
        rank = lax.axis_index("tensor")
        at = lax.axis_index("dp")
        shift = rank if tensor == 4 else jnp.zeros_like(rank)
        self.place = jnp.stack([at // 2, at % 2, shift]).astype(jnp.int32)

    def over_chips(self, values, k):
        return lax.ppermute(values, "dp", [(i, i ^ (2 * k)) for i in range(self.dp)])

    def over_core(self, values):
        return lax.ppermute(values, "dp", [(i, i ^ 1) for i in range(self.dp)])

    def over_tensor(self, values, k):
        return lax.ppermute(values, "tensor", [(i, i ^ k) for i in range(self.tensor)])

    def between(self, values, pairs):
        return lax.ppermute(values, "dp", [(2 * a + c, 2 * b + c) for a, b in pairs for c in range(2)])

    def gather_near(self, shard):
        if self.chips != 4:
            return [shard] + [self.over_chips(shard, k) for k in range(1, self.chips)]
        return [shard, self.over_chips(shard, 1), self.over_chips(shard, 2)]

    def gather_far(self, near, earlier):
        if self.chips != 4:
            return pinned(near, earlier) if earlier else near
        near = pinned(near, earlier)
        middle = self.between(near[0], [(1, 2), (2, 1)])
        return near + [middle + self.between(near[2], [(1, 0), (2, 3)])]

    def gather_cores(self, mine, earlier, early):
        first = pinned(mine[:-1], early)
        last = pinned(mine[-1:], earlier)
        return first + last + [self.over_core(piece) for piece in first + last]

    def scatter_far(self, others):
        if self.chips != 4:
            return []
        return [self.between(others[2], [(0, 1), (3, 2)]), self.between(others[2], [(1, 2), (2, 1)])]

    def scatter_join(self, others, came):
        if self.chips != 4:
            return others
        one, two = pinned(others[:2], came)
        return [one, (two.astype(f32) + came[0].astype(f32)).astype(bf16)]

    def scatter_near(self, joined, came):
        return came[1:] + [self.over_chips(value, k + 1) for k, value in enumerate(joined)]

    def gather_first(self, shard):
        if self.tensor != 4:
            return [lax.all_gather(shard, "tensor", axis=0, tiled=True)]
        return [shard, self.over_tensor(shard, 1), self.over_tensor(shard, 2)]

    def gather_last(self, pieces, earlier):
        if self.tensor != 4:
            return pieces
        half = BLOCK // 2
        halves = [pieces[1][:half], pieces[2][half:]]
        if earlier:
            halves = pinned(halves, earlier)
        return pieces + [self.over_tensor(halves[0], 2), self.over_tensor(halves[1], 1)]

    def scatter_first(self, rows, earlier):
        if self.tensor != 4:
            return []
        half = BLOCK // 2
        halves = [rows[3 * BLOCK : 3 * BLOCK + half], rows[3 * BLOCK + half :]]
        if earlier:
            halves = pinned(halves, earlier)
        return [self.over_tensor(halves[0], 2), self.over_tensor(halves[1], 1)]

    def scatter_blocks(self, rows, came):
        if self.tensor != 4:
            return [rows]
        half = BLOCK // 2
        own, one, two = rows[:BLOCK], rows[BLOCK : 2 * BLOCK], rows[2 * BLOCK : 3 * BLOCK]
        one = jnp.concatenate([(one[:half].astype(f32) + came[0].astype(f32)).astype(bf16), one[half:]])
        two = jnp.concatenate([two[:half], (two[half:].astype(f32) + came[1].astype(f32)).astype(bf16)])
        return [own, one, two]

    def scatter_last(self, blocks, earlier):
        if self.tensor != 4:
            return [lax.psum_scatter(blocks[0], "tensor", scatter_dimension=0, tiled=True)]
        came = [self.over_tensor(blocks[k], k) for k in (1, 2)]
        return [blocks[0]] + (pinned(came, earlier) if earlier else came)

    def scatter_direct(self, rows, earlier):
        if self.tensor != 4:
            return [lax.psum_scatter(rows, "tensor", scatter_dimension=0, tiled=True)]
        own, *others = jnp.split(rows, 4)
        others = pinned(others, earlier)
        return [own] + [self.over_tensor(block, k + 1) for k, block in enumerate(others)]

    def spread_tensor(self, values):
        return [values] + [self.over_tensor(values, k) for k in range(1, self.tensor)]

    def sum_tensor(self, values):
        return sum(self.spread_tensor(values)[1:], values)


def local(
    net_of,
    tokens,
    norm_gain,
    gate_proj,
    inner_proj,
    shared_proj,
    step_proj,
    conv_inner,
    conv_inner_bias,
    conv_shared,
    conv_shared_bias,
    step_bias,
    decay_log,
    skip_gain,
    out_gain,
    out_proj,
    cotangent,
):
    net = net_of()
    place, chips = net.place, net.chips
    channels = gate_proj.shape[1]
    heads = step_proj.shape[1]
    width = channels + 2 * STATE
    token_rows = tokens.astype(f32)
    inverse = lax.rsqrt(jnp.mean(token_rows * token_rows, axis=-1, keepdims=True) + epsilon)
    unit = token_rows * inverse
    normed_low = (unit * norm_gain).astype(bf16)
    padding = jnp.zeros((step_proj.shape[0], LANES - heads), bf16)
    scan_shard = jnp.concatenate([inner_proj, shared_proj, step_proj, padding], axis=1)
    scan_mine = net.gather_far(net.gather_near(scan_shard), [])
    row_pieces = net.gather_first(normed_low)
    reached = scan_mine[1:]
    cot_copy = copied(cotangent, row_pieces[1:2])
    joint = joint_shard(gate_proj, out_proj, [cot_copy])
    row_pieces = net.gather_last(row_pieces, [])
    scan_pieces = net.gather_cores(scan_mine, row_pieces[3:], [])
    cot_pieces = net.gather_first(pinned([cot_copy], row_pieces[3:] + scan_pieces[chips:])[0])
    joint_mine = net.gather_near(pinned([joint], reached)[0])

    taps = jnp.concatenate(
        [
            jnp.concatenate([conv_inner, conv_inner_bias[None]]),
            jnp.concatenate([conv_shared, conv_shared_bias[None]]),
        ],
        axis=1,
    )
    taps = jnp.pad(taps, ((0, 8 - CONV - 1), (0, 0)))
    rates = -jnp.exp(decay_log)
    head_rows = jnp.pad(jnp.stack([step_bias, rates]), ((0, 6), (0, LANES - heads)))
    skip_row = jnp.repeat(skip_gain, HEAD_DIM)[None]
    gain = out_gain[None]

    raw, scan_full, rows = product(
        place,
        row_pieces,
        scan_pieces,
        raw_epilogue,
        [],
        [(width + LANES, f32)],
        "project",
    )
    scanned, pre, states = scan_forward(raw, taps, head_rows, skip_row, [])
    cot_pieces = net.gather_last(cot_pieces, [scanned])
    joint_mine = net.gather_far(joint_mine, [scanned])
    gate, gated, grad_out, token_sums, joint_full, cot_rows = product(
        place,
        cot_pieces,
        net.gather_cores(joint_mine, cot_pieces[3:], []),
        mix_epilogue,
        [(rows, False), (stay(scanned), True), (gain, False)],
        [(channels, f32), (channels, f32), (channels, f32), (None, 2)],
        "mix",
    )
    token_sums = net.sum_tensor(token_sums)
    out_low, gate_back, scan_grad, gain_grad = gating(grad_out, gated, scanned, gate, token_sums, gain)
    keep, give = weight_grads(
        place, chips, [rows, cot_rows], [gate_back, out_low], [], "grad_joint_proj"
    )
    joint_come = net.over_core(give)
    branch, _ = back(place, [out_low], [(joint_full, 1)], None, "branch", [give])
    joint_own, joint_others = pairs(keep, joint_come, False, [branch])
    came = net.scatter_far(joint_others)
    branch_parts = net.scatter_direct(branch, joint_others[:1])
    held = scan_backward(
        0, raw, pre, scan_grad, states, taps, head_rows, skip_row, None, joint_others[:1]
    )
    came = pinned(came, [held[1]]) if came else came
    joint_arrived = net.scatter_near(net.scatter_join(joint_others, came), came)
    scan_back, sums, head_sums, _, _ = scan_backward(
        1, raw, pre, scan_grad, states, taps, head_rows, skip_row, held, came
    )
    norm_rows, norm_sums = back(
        place, [gate_back, stay(scan_back)], [(joint_full, 0), (scan_full, 0)], rows, "grad_normed"
    )
    keep, give = weight_grads(
        place,
        chips,
        [rows],
        [stay(scan_back)],
        [sums, gain_grad, norm_sums, head_sums],
        "grad_scan_proj",
        joint_arrived + branch_parts[1:],
    )
    norm_came = net.scatter_first(norm_rows, joint_arrived)
    scan_own, scan_others = pairs(stay(keep), stay(net.over_core(give)), True)
    came = net.scatter_far(scan_others)
    came = pinned(came, []) if came else came
    norm_came = pinned(norm_came, scan_others[:1]) if norm_came else norm_came
    joined = net.scatter_join(scan_others, came)
    *joint_arrived, = pinned(joint_arrived, joined[1:2])
    scan_arrived = net.scatter_near(joined, came)
    norm_parts = net.scatter_last(net.scatter_blocks(norm_rows, norm_came), joined[1:])
    grad_normed = total_of(norm_parts[0].astype(f32), norm_parts[1:])
    mixed = total_of(token_rows, branch_parts).astype(bf16)
    joint_total = total_of(joint_own, joint_arrived)
    grad_gate_proj, grad_out_proj = joint_total[:, :channels], joint_total[:, channels:].T
    spread = grad_normed * norm_gain
    grad_tokens = (
        cotangent.astype(f32)
        + inverse * spread
        - unit * (inverse * jnp.mean(spread * unit, axis=-1, keepdims=True))
    )
    grad_inner_proj, step_part, grad_conv_inner, inner_bias, gain_part, head_part, common = collect(
        [scan_own] + scan_arrived, channels, []
    )
    grad_shared_proj, grad_conv_shared, shared_bias, norm_part = finish(
        net.spread_tensor(common), norm_gain.reshape(-1, LANES)
    )
    return (
        mixed,
        grad_tokens,
        norm_part.reshape(-1),
        grad_gate_proj,
        grad_inner_proj,
        grad_shared_proj,
        step_part[:, :heads],
        grad_conv_inner,
        inner_bias.reshape(-1),
        grad_conv_shared,
        shared_bias.reshape(-1),
        head_part[0, :heads],
        head_part[1, :heads] * rates,
        head_part[2, :heads],
        gain_part.reshape(-1),
        grad_out_proj,
    )


def solution(mesh):
    dp, tensor = mesh.shape["dp"], mesh.shape["tensor"]

    def on_device(*args):
        return local(lambda: Net(dp, tensor), *args)

    return jax.shard_map(
        on_device,
        mesh=mesh,
        in_specs=(
            P(("dp", "tensor"), None),
            P(),
            P("dp", "tensor"),
            P("dp", "tensor"),
            P("dp", None),
            P("dp", "tensor"),
            P(None, "tensor"),
            P("tensor"),
            P(),
            P(),
            P("tensor"),
            P("tensor"),
            P("tensor"),
            P("tensor"),
            P("tensor", "dp"),
            P(("dp", "tensor"), None),
        ),
        out_specs=(
            P(("dp", "tensor"), None),
            P(("dp", "tensor"), None),
            P(),
            P("dp", "tensor"),
            P("dp", "tensor"),
            P("dp", None),
            P("dp", "tensor"),
            P(None, "tensor"),
            P("tensor"),
            P(),
            P(),
            P("tensor"),
            P("tensor"),
            P("tensor"),
            P("tensor"),
            P("tensor", "dp"),
        ),
        check_vma=False,
    )
```

```python
import functools

import jax
import jax.numpy as jnp
from jax import lax
from jax.experimental import pallas as pl
from jax.experimental.pallas import tpu as pltpu
from jax.sharding import PartitionSpec as P

DI = 3072
epsilon = 1e-05
HEAD_DIM = 64
STATE = 128
CONV = 4
SEQ = 1024
SPAN = 256
CHUNK = 128
LANES = 128
NEVER = -1e30
NEAR = jax.ShapeDtypeStruct
f32 = jnp.float32
bf16 = jnp.bfloat16
highest = lax.Precision.HIGHEST


def dot(first, second, first_dim=1, second_dim=0, precision=None):
    return lax.dot_general(
        first,
        second,
        (((first_dim,), (second_dim,)), ((), ())),
        precision=precision,
        preferred_element_type=f32,
    )


def sigmoid(values):
    return 0.5 * jnp.tanh(0.5 * values) + 0.5


def places(dim):
    return lax.broadcasted_iota(jnp.int32, (CHUNK, LANES), dim)


def exact_dot(ones, values, parts):
    split = []
    for _ in range(parts):
        split.append(values.astype(bf16))
        values = values - split[-1].astype(f32)
    result = dot(ones, jnp.concatenate(split, axis=1))
    return sum(result[:, i * LANES : (i + 1) * LANES] for i in range(parts))


def decays(step_raw, heads_ref):
    raw = step_raw + heads_ref[0:1]
    small = jnp.exp(-jnp.abs(raw))
    log_one = jnp.where(small < 1e-3, small - 0.5 * small * small, jnp.log(1.0 + small))
    steps = jnp.maximum(raw, 0.0) + log_one
    summed = exact_dot((places(0) >= places(1)).astype(bf16), steps * heads_ref[1:2], 3)
    return steps, sigmoid(raw), summed, summed - jnp.log(steps)


def pair_of(first, second):
    return jnp.concatenate([first, second], axis=0)


def forward_kernel(raw_ref, taps_ref, heads_ref, skip_ref, *refs):
    scanned_ref, pre_ref, states_ref, state, before = refs[-5:]
    chunk = pl.program_id(0)
    channels = skip_ref.shape[1]
    width = channels + 2 * STATE

    @pl.when(chunk % (SEQ // CHUNK) == 0)
    def _():
        state[...] = jnp.zeros_like(state)
        before[...] = jnp.zeros_like(before)

    raw = raw_ref[:, :width]
    extended = jnp.concatenate([before[...], raw], axis=0)
    pre = taps_ref[CONV : CONV + 1] + taps_ref[CONV - 1 : CONV] * raw
    for tap in range(CONV - 1):
        start = 8 - (CONV - 1) + tap
        pre = pre + taps_ref[tap : tap + 1] * extended[start : start + CHUNK]
    before[...] = raw[CHUNK - 8 :]
    pre_ref[...] = pre
    act = (pre * sigmoid(pre)).astype(bf16)
    writes = act[:, channels : channels + STATE]
    reads = act[:, channels + STATE :]
    _, _, summed, shifted = decays(raw_ref[:, width:], heads_ref)
    summed_t, shifted_t = summed.T, shifted.T
    tail_t = jnp.exp(summed_t[:, CHUNK - 1 :] - shifted_t)
    scores = dot(reads, writes, 1, 1)
    writes_t = writes.astype(f32).T
    causal = places(0) >= places(1)
    left = places(1) < HEAD_DIM
    states_ref[...] = state[...].astype(bf16)
    for pair in range(channels // LANES):
        cols = slice(pair * LANES, (pair + 1) * LANES)
        values = act[:, cols].astype(f32)
        both = pair_of(jnp.where(left, values, 0.0), jnp.where(left, 0.0, values)).astype(bf16)
        mixes, tails, grown = [], [], []
        for head in (2 * pair, 2 * pair + 1):
            here = jnp.broadcast_to(summed[:, head : head + 1], (CHUNK, LANES))
            decay = jnp.exp(jnp.where(causal, here - shifted_t[head : head + 1], NEVER))
            mixes.append((scores * decay).astype(bf16))
            tails.append((writes_t * tail_t[head : head + 1]).astype(bf16))
            grown.append(here)
        stacked = pair_of(jnp.concatenate(mixes, axis=1), jnp.concatenate(tails, axis=1))
        out = dot(stacked, both)
        entering = state[:, cols]
        factor = jnp.exp(jnp.where(left, grown[0], grown[1]))
        across = dot(reads, entering.astype(bf16)) * factor
        scanned_ref[:, cols] = out[:CHUNK] + across + values * skip_ref[:, cols]
        state[:, cols] = entering * factor[CHUNK - 1 :] + out[CHUNK:]


def backward_kernel(part, n_deps, *refs):
    raw_ref, pre_ref, grad_ref, states_ref, taps_ref, heads_ref, skip_ref = refs[:7]
    n_held = 5 if part else 0
    held, refs = refs[7 : 7 + n_held], refs[7 + n_held + n_deps :]
    low_ref, sums_ref, head_sums_ref, carry, after, wide = refs
    step = pl.program_id(0)
    channels = skip_ref.shape[1]
    width = channels + 2 * STATE

    @pl.when(step == 0)
    def _():
        if part:
            for ref, source in zip((sums_ref, head_sums_ref, carry, after), held[1:], strict=True):
                ref[...] = source[...]
        else:
            sums_ref[...] = jnp.zeros_like(sums_ref)
            head_sums_ref[...] = jnp.zeros_like(head_sums_ref)

    @pl.when((step + part * pl.num_programs(0)) % (SEQ // CHUNK) == 0)
    def _():
        carry[...] = jnp.zeros_like(carry)
        after[...] = jnp.zeros_like(after)

    pre = pre_ref[...]
    gate = sigmoid(pre)
    act = (pre * gate).astype(bf16)
    writes = act[:, channels : channels + STATE]
    reads = act[:, channels + STATE :]
    steps, slopes, summed, shifted = decays(raw_ref[:, width:], heads_ref)
    summed_t = summed.T
    scores_t = dot(writes, reads, 1, 1)
    causal = places(0) <= places(1)
    earlier = places(0) < places(1)
    suffix = (places(0) >= places(1)).astype(bf16)
    left = places(1) < HEAD_DIM
    score_grads = jnp.zeros((CHUNK, LANES), f32)
    spans, inner_grads, lasts = [], [], []
    for pair in range(channels // LANES):
        cols = slice(pair * LANES, (pair + 1) * LANES)
        values = act[:, cols].astype(f32)
        both = pair_of(jnp.where(left, values, 0.0), jnp.where(left, 0.0, values)).astype(bf16)
        grad_low = grad_ref[:, cols]
        grad = grad_low.astype(f32)
        grad_both = pair_of(jnp.where(left, grad, 0.0), jnp.where(left, 0.0, grad)).astype(bf16)
        products = dot(both, grad_low, 1, 1)
        mixes, crossing, grown, tails = [], [], [], []
        for place, head in enumerate((2 * pair, 2 * pair + 1)):
            here = jnp.broadcast_to(shifted[:, head : head + 1], (CHUNK, LANES))
            decay = jnp.exp(jnp.where(causal, summed_t[head : head + 1] - here, NEVER))
            product = products[place * CHUNK : (place + 1) * CHUNK]
            score_grads = score_grads + decay * product
            mix = scores_t * decay
            mixes.append(mix.astype(bf16))
            crossing.append((mix * product).astype(bf16))
            level = jnp.broadcast_to(summed[:, head : head + 1], (CHUNK, LANES))
            grown.append(level)
            tails.append(level[CHUNK - 1 :] - here)
        sums = dot(pair_of(*crossing), suffix)
        for place in range(2):
            piece = jnp.where(earlier, sums[place * CHUNK : (place + 1) * CHUNK], 0.0)
            spans.append(jnp.sum(piece, axis=0, keepdims=True))
        within = dot(jnp.concatenate(mixes, axis=1), grad_both)
        factor = jnp.exp(jnp.where(left, grown[0], grown[1]))
        tail = jnp.exp(jnp.where(left, tails[0], tails[1]))
        leaving = carry[:, cols]
        entering = states_ref[:, cols]
        later = tail * dot(writes, leaving.astype(bf16))
        both_grads = within + later
        inner_grads.append(both_grads + skip_ref[:, cols] * grad)
        spread = factor * grad
        spread_low = spread.astype(bf16)
        wide[0:CHUNK, cols] = spread_low
        wide[CHUNK : 2 * CHUNK, cols] = (tail * values).astype(bf16)
        wide[2 * CHUNK : 3 * CHUNK, cols] = (spread * dot(reads, entering)).astype(bf16)
        wide[3 * CHUNK : 4 * CHUNK, cols] = (values * later).astype(bf16)
        wide[4 * CHUNK : 5 * CHUNK, cols] = (values * both_grads).astype(bf16)
        held = jnp.sum(entering.astype(f32) * leaving, axis=0, keepdims=True) * factor[CHUNK - 1 :]
        sums_ref[CONV + 1 : CONV + 2, cols] += jnp.sum(grad * values, axis=0, keepdims=True)
        wide[5 * CHUNK :, cols] = jnp.broadcast_to(held, (16, LANES)).astype(bf16)
        lasts.append(factor[CHUNK - 1 :])
    reads_t = reads.astype(f32).T.astype(bf16)
    score_low = score_grads.astype(bf16)
    spread_all = wide[0:CHUNK, :]
    read_grads = dot(score_low, writes, 0, 0) + dot(spread_all, states_ref[...], 1, 1)
    write_grads = dot(score_low, reads) + dot(wide[CHUNK : 2 * CHUNK, :], carry[...].astype(bf16), 1, 1)
    of_head = (
        lax.broadcasted_iota(jnp.int32, (channels, LANES), 0) // HEAD_DIM
        == lax.broadcasted_iota(jnp.int32, (channels, LANES), 1)
    )
    reduced = dot(wide[2 * CHUNK :, :], of_head.astype(bf16))
    carry[...] = carry[...] * jnp.concatenate(lasts, axis=1) + dot(reads_t, spread_all)
    both_sums = reduced[2 * CHUNK : 3 * CHUNK]
    held_heads = reduced[3 * CHUNK : 3 * CHUNK + 1]
    span_rows = jnp.concatenate(spans + [jnp.zeros((LANES - len(spans), LANES), f32)], axis=0)
    upto = [places(0) <= places(1), places(0) > places(1)]
    upto = jnp.concatenate([v.astype(bf16) for v in upto], axis=1)
    log_grads = exact_dot(upto, reduced[: 2 * CHUNK], 2) + span_rows.T + held_heads
    ratio = jnp.where(steps > 1e-30, slopes / steps, 1.0)
    step_grads = both_sums * ratio + heads_ref[1:2] * log_grads * slopes
    head_sums_ref[0:1] += jnp.sum(step_grads, axis=0, keepdims=True)
    head_sums_ref[1:2] += jnp.sum(log_grads * steps, axis=0, keepdims=True)

    @pl.when(part * pl.num_programs(0) + step == 2 * pl.num_programs(0) - 1)
    def _():
        skip_rows = jnp.broadcast_to(sums_ref[CONV + 1 : CONV + 2, :channels], (8, channels))
        head_sums_ref[2:3] = dot(skip_rows, of_head.astype(f32), precision=highest)[0:1]

    raw = raw_ref[:, :width]
    act_grads = jnp.concatenate(inner_grads + [write_grads, read_grads], axis=1)
    pre_grads = act_grads * (gate * (1.0 + pre * (1.0 - gate)))
    extended = jnp.concatenate([pre_grads, after[...]], axis=0)
    after[...] = pre_grads[:8]
    sums_ref[CONV : CONV + 1] += jnp.sum(pre_grads, axis=0, keepdims=True)
    raw_grads = taps_ref[CONV - 1 : CONV] * pre_grads
    sums_ref[CONV - 1 : CONV] += jnp.sum(raw * pre_grads, axis=0, keepdims=True)
    for tap in range(CONV - 1):
        moved = extended[CONV - 1 - tap : CONV - 1 - tap + CHUNK]
        raw_grads = raw_grads + taps_ref[tap : tap + 1] * moved
        sums_ref[tap : tap + 1] += jnp.sum(raw * moved, axis=0, keepdims=True)
    low_ref[:, :width] = raw_grads.astype(bf16)
    low_ref[:, width:] = step_grads.astype(bf16)


def stay(values):
    return pltpu.with_memory_space_constraint(values, pltpu.HBM)


def scan_forward(raw, taps, heads, skip, earlier):
    tokens, full = raw.shape
    channels = skip.shape[1]
    width = channels + 2 * STATE
    count = tokens // CHUNK
    by_chunk = lambda shape: pl.BlockSpec(shape, lambda s: (s, 0))
    whole = lambda v: pl.BlockSpec(v.shape, lambda s: (0, 0))
    return pl.pallas_call(
        forward_kernel,
        grid=(count,),
        in_specs=[by_chunk((CHUNK, full)), whole(taps), whole(heads), whole(skip)]
        + [pl.BlockSpec(memory_space=pl.ANY)] * len(earlier),
        out_specs=[
            by_chunk((CHUNK, channels)),
            by_chunk((CHUNK, width)),
            by_chunk((STATE, channels)),
        ],
        scratch_shapes=[pltpu.VMEM((STATE, channels), f32), pltpu.VMEM((8, width), f32)],
        out_shape=[
            pltpu.HBM((tokens, channels), f32),
            pltpu.HBM((tokens, width), f32),
            pltpu.HBM((count * STATE, channels), bf16),
        ],
        compiler_params=pltpu.CompilerParams(vmem_limit_bytes=12 << 20),
        name="scan_forward",
    )(stay(raw), taps, heads, skip, *earlier)


def scan_backward(part, raw, pre, grad, states, taps, heads, skip, held, earlier):
    tokens, full = raw.shape
    channels = skip.shape[1]
    width = channels + 2 * STATE
    count = tokens // CHUNK
    half = count // 2
    last = count - 1 - part * half
    by_chunk = lambda shape: pl.BlockSpec(shape, lambda s: (last - s, 0))
    whole = lambda shape: pl.BlockSpec(shape, lambda s: (0, 0))
    kept = [(8, width), (8, LANES), (STATE, channels), (8, width)]
    free = pl.BlockSpec(memory_space=pl.ANY)
    held = list(held) if part else []
    return pl.pallas_call(
        functools.partial(backward_kernel, part, len(earlier)),
        grid=(half,),
        in_specs=[
            by_chunk((CHUNK, full)),
            by_chunk((CHUNK, width)),
            by_chunk((CHUNK, channels)),
            by_chunk((STATE, channels)),
            whole(taps.shape),
            whole(heads.shape),
            whole(skip.shape),
        ]
        + ([free] + [whole(shape) for shape in kept] if part else [])
        + [free] * len(earlier),
        out_specs=[by_chunk((CHUNK, full))] + [whole(shape) for shape in kept],
        scratch_shapes=[pltpu.VMEM((5 * CHUNK + 16, channels), bf16)],
        out_shape=[pltpu.HBM((tokens, full), bf16)] + [pltpu.HBM(shape, f32) for shape in kept],
        input_output_aliases={7: 0} if part else {},
        compiler_params=pltpu.CompilerParams(vmem_limit_bytes=12 << 20),
        name=f"scan_backward_{part}",
    )(stay(raw), stay(pre), stay(grad), stay(states), taps, heads, skip, *[stay(v) for v in held], *earlier)


BLOCK = 256
LIMIT = 16 << 20
SMALL_LIMIT = 12 << 20
SMALL = 16
anywhere = pl.BlockSpec(memory_space=pl.ANY)
in_vmem = pl.BlockSpec(memory_space=pltpu.VMEM)


def column_sums(values, count):
    rows = [
        jnp.sum(values[i * LANES : (i + 1) * LANES].T, axis=0, keepdims=True)
        for i in range(count // LANES)
    ]
    return jnp.concatenate(rows, axis=0)


def fold(values):
    total = values[:, :LANES]
    for start in range(LANES, values.shape[1], LANES):
        total = total + values[:, start : start + LANES]
    return total


def shard_rows(place, index, chips, height):
    core, chip = index // chips, index % chips
    return pl.multiple_of(((place[0] ^ chip) * 2 + (place[1] ^ core)) * height, height)


def row_start(place, start):
    if isinstance(start, int):
        return pl.multiple_of((start // BLOCK ^ place[2]) * BLOCK + start % BLOCK, LANES)
    return pl.multiple_of((start // BLOCK ^ place[2]) * BLOCK, BLOCK)


def product_kernel(heights, chips, epilogue, n_extra, n_deps, n_out, place, *refs):
    n_rows, n_full = len(heights), 2 * chips
    row_refs, refs = refs[:n_rows], refs[n_rows:]
    full_refs, refs = refs[:n_full], refs[n_full:]
    extra, refs = refs[:n_extra], refs[n_extra + n_deps :]
    outs, (full, rows, sems) = refs[:n_out], refs[n_out:]
    step = pl.program_id(0)
    starts = [sum(heights[:i]) for i in range(n_rows)]
    shard = full.shape[0] // n_full
    row_copies = [
        pltpu.make_async_copy(
            row_refs[i], rows.at[pl.ds(row_start(place, starts[i]), heights[i])], sems.at[i]
        )
        for i in range(n_rows)
    ]
    full_copies = [
        pltpu.make_async_copy(
            full_refs[i], full.at[pl.ds(shard_rows(place, i, chips, shard), shard)], sems.at[n_rows + i]
        )
        for i in range(n_full)
    ]

    @pl.when(step == 0)
    def _():
        for copy in full_copies + row_copies:
            copy.start()
        for copy in full_copies:
            copy.wait()

    for i in range(n_rows):

        @pl.when(step == starts[i] // BLOCK)
        def _(i=i):
            row_copies[i].wait()

    block = rows[pl.ds(row_start(place, step * BLOCK), BLOCK), :]
    epilogue(step ^ place[2], block, full, extra, outs)


def product(place, row_pieces, full_pieces, epilogue, extra, outs, name, earlier=()):
    chips = len(full_pieces) // 2
    heights = tuple(piece.shape[0] for piece in row_pieces)
    tokens, depth = sum(heights), row_pieces[0].shape[1]
    columns = full_pieces[0].shape[1]
    by_block = lambda cols: pl.BlockSpec((BLOCK, cols), lambda s, p: (s ^ p[2], 0))
    out_specs, out_shape = [], []
    for cols, dtype in outs:
        if cols is None:
            shape = (dtype * tokens // LANES, LANES)
            out_specs.append(pl.BlockSpec(shape, lambda s, p: (0, 0)))
            out_shape.append(jax.ShapeDtypeStruct(shape, f32))
        else:
            out_specs.append(by_block(cols))
            out_shape.append((pltpu.HBM if name == "project" else NEAR)((tokens, cols), dtype))
    return pl.pallas_call(
        functools.partial(product_kernel, heights, chips, epilogue, len(extra), len(earlier), len(outs)),
        grid_spec=pltpu.PrefetchScalarGridSpec(
            num_scalar_prefetch=1,
            grid=(tokens // BLOCK,),
            in_specs=[anywhere] * (len(row_pieces) + len(full_pieces))
            + [by_block(v.shape[1]) if by else in_vmem for v, by in extra]
            + [anywhere] * len(earlier),
            out_specs=out_specs + [in_vmem, in_vmem],
            scratch_shapes=[pltpu.SemaphoreType.DMA((len(row_pieces) + len(full_pieces),))],
        ),
        out_shape=out_shape + [pltpu.VMEM((depth, columns), bf16), pltpu.VMEM((tokens, depth), bf16)],
        compiler_params=pltpu.CompilerParams(vmem_limit_bytes=LIMIT),
        name=name,
    )(place, *[stay(v) for v in row_pieces + full_pieces], *[v for v, _ in extra], *earlier)


def slices(columns):
    return [slice(start, min(start + 256, columns)) for start in range(0, columns, 256)]


def raw_epilogue(index, block, full, extra, outs):
    (raw,) = outs
    for cols in slices(raw.shape[1]):
        raw[:, cols] = dot(block, full[:, cols])


def mix_epilogue(index, block, full, extra, outs):
    rows, scanned, gain = extra
    gate, gated, grad, sums = outs
    channels = gate.shape[1]
    squares = jnp.zeros((BLOCK, LANES), f32)
    dots = jnp.zeros((BLOCK, LANES), f32)
    here = pl.ds(pl.multiple_of(index * BLOCK, BLOCK), BLOCK)
    for cols in slices(channels):
        value = dot(rows[here, :], full[:, cols])
        out = dot(block, full[:, channels + cols.start : channels + cols.stop])
        gate[:, cols] = value
        grad[:, cols] = out
        product = scanned[:, cols] * (value * sigmoid(value))
        gated[:, cols] = product
        squares = squares + fold(product * product)
        dots = dots + fold(out * gain[:, cols] * product)
    per = BLOCK // LANES
    half = sums.shape[0] // 2
    sums[pl.ds(index * per, per), :] = column_sums(squares, BLOCK)
    sums[pl.ds(half + index * per, per), :] = column_sums(dots, BLOCK)


def shard_kernel(gate_proj, out_proj, *refs):
    out = refs[-1]
    channels, height = out_proj.shape
    out[:, :channels] = gate_proj[...]
    place = [lax.broadcasted_iota(jnp.int32, (height, height), dim) for dim in range(2)]
    same = (place[0] == place[1]).astype(bf16)
    out[:, channels:] = dot(same, out_proj[...], 1, 1).astype(bf16)


def joint_shard(gate_proj, out_proj, earlier):
    return pl.pallas_call(
        shard_kernel,
        in_specs=[in_vmem] * 2 + [anywhere] * len(earlier),
        out_specs=in_vmem,
        out_shape=jax.ShapeDtypeStruct((gate_proj.shape[0], 2 * gate_proj.shape[1]), bf16),
        name="joint_shard",
    )(gate_proj, out_proj, *earlier)


def columns_of(row):
    return jnp.broadcast_to(row, (LANES, LANES)).T


def gating_kernel(grad_out, gated, gate, sums, gain, scanned, out_low, gate_back, scan_grad, gain_grad):
    step = pl.program_id(0)
    half = sums.shape[0] // 2

    @pl.when(step == 0)
    def _():
        gain_grad[...] = jnp.zeros_like(gain_grad)

    for part in range(BLOCK // LANES):
        rows = slice(part * LANES, (part + 1) * LANES)
        index = step * (BLOCK // LANES) + part
        here = pl.ds(pl.multiple_of(index * LANES, LANES), LANES)
        ratio_row = lax.rsqrt(sums[pl.ds(index, 1), :] / DI + epsilon)
        dots = sums[pl.ds(half + index, 1), :]
        ratio = columns_of(ratio_row)
        pull = columns_of(ratio_row * ratio_row * ratio_row / DI * dots)
        for start in range(0, gate.shape[1], LANES):
            cols = slice(start, start + LANES)
            held, value = gated[here, cols], gate[here, cols]
            scaled = grad_out[here, cols] * ratio
            out_low[rows, cols] = (gain[:, cols] * (held * ratio)).astype(bf16)
            gain_grad[0:1, cols] += jnp.sum(scaled * held, axis=0, keepdims=True)
            grad = gain[:, cols] * scaled - held * pull
            slope = sigmoid(value)
            scan_grad[rows, cols] = (grad * (value * slope)).astype(bf16)
            gate_grad = grad * scanned[rows, cols] * (slope * (1.0 + value * (1.0 - slope)))
            gate_back[rows, cols] = gate_grad.astype(bf16)


def gating(grad_out, gated, scanned, gate, sums, gain):
    tokens, columns = gated.shape
    block = pl.BlockSpec((BLOCK, columns), lambda s: (s, 0))
    return pl.pallas_call(
        gating_kernel,
        grid=(tokens // BLOCK,),
        in_specs=[in_vmem] * 5 + [block],
        out_specs=[block] * 3 + [pl.BlockSpec((8, columns), lambda s: (0, 0))],
        out_shape=[NEAR((tokens, columns), bf16)] * 2
        + [pltpu.HBM((tokens, columns), bf16)] + [jax.ShapeDtypeStruct((8, columns), f32)],
        compiler_params=pltpu.CompilerParams(vmem_limit_bytes=SMALL_LIMIT),
        name="gating",
    )(grad_out, gated, gate, sums, gain, stay(scanned))


def grads_kernel(n_rows, wide, place, *refs):
    rows, lows = refs[:n_rows], refs[n_rows : 2 * n_rows]
    keep, give = refs[-2:]
    shard = wide // 2
    first = place[1] == 0
    lanes = pl.ds(pl.multiple_of((pl.program_id(0) ^ place[0]) * wide, LANES), wide)
    start = 0
    for row, low in zip(rows, lows, strict=True):
        for cols in slices(low.shape[1]):
            value = dot(row[:, lanes], low[:, cols], 0, 0)
            one, two = value[:shard], value[shard:]
            out = slice(start + cols.start, start + cols.stop)
            keep[0, :shard, out] = jnp.where(first, one, two).astype(bf16)
            give[0, :shard, out] = jnp.where(first, two, one).astype(bf16)
        start += low.shape[1]


def fill_small(small, sums, gain_grad, norm_grad, head_sums):
    rest = norm_grad.shape[1] - small.shape[1]
    small[...] = jnp.zeros_like(small)
    small[0:8, : sums.shape[1]] = sums[...]
    small[8:9, : gain_grad.shape[1]] = gain_grad[0:1, :]
    small[9:10, :] = norm_grad[0:1, : small.shape[1]]
    small[10:11, :rest] = norm_grad[0:1, small.shape[1] :]
    small[11:14, :LANES] = head_sums[0:3, :]


def small_kernel(n_rows, wide, place, *refs):
    keep, give, small = refs[-3:]
    grads_kernel(n_rows, wide, place, *refs[:-1])
    fill_small(small, *refs[2 * n_rows : 2 * n_rows + 4])
    low = small[...].astype(bf16)
    shard = keep.shape[1] - SMALL
    keep[0, shard:] = low
    give[0, shard:] = low


def whole_grads_kernel(chips, n_rows, n_small, place, *refs):
    rows, lows = refs[:n_rows], refs[n_rows : 2 * n_rows]
    keep, give, acc, small = refs[-4:]
    depth = acc.shape[0]
    shard = depth // (2 * chips)
    start = 0
    for row, low in zip(rows, lows, strict=True):
        cols = slice(start, start + low.shape[1])
        for lanes in slices(depth):
            acc[lanes, cols] = dot(row[:, lanes], low[...], 0, 0)
        start = cols.stop
    for k in range(chips):
        for out, core in ((keep, place[1]), (give, 1 - place[1])):
            at = pl.multiple_of(((place[0] ^ k) * 2 + core) * shard, shard)
            out[k, :shard] = acc[pl.ds(at, shard), :].astype(bf16)
    if n_small:
        fill_small(small, *refs[2 * n_rows : 2 * n_rows + n_small])
        for k in range(chips):
            keep[k, shard:] = small[...].astype(bf16)
            give[k, shard:] = small[...].astype(bf16)


def weight_grads(place, chips, rows, lows, small, name, earlier=()):
    tokens, depth = rows[0].shape
    columns = sum(v.shape[1] for v in lows)
    wide = depth // chips
    shard = wide // 2
    height = shard + (SMALL if small else 0)
    if wide % LANES:
        return pl.pallas_call(
            functools.partial(whole_grads_kernel, chips, len(rows), len(small)),
            in_specs=[pl.BlockSpec(memory_space=pltpu.SMEM)]
            + [in_vmem] * (2 * len(rows) + len(small))
            + [anywhere] * len(earlier),
            out_specs=[in_vmem] * 2,
            out_shape=[jax.ShapeDtypeStruct((chips, height, columns), bf16)] * 2,
            scratch_shapes=[pltpu.VMEM((depth, columns), f32), pltpu.VMEM((SMALL, columns), f32)],
            compiler_params=pltpu.CompilerParams(vmem_limit_bytes=2 * LIMIT),
            name=name,
        )(place, *rows, *lows, *small, *earlier)
    out = pl.BlockSpec((1, height, columns), lambda k, p: (k, 0, 0))
    return pl.pallas_call(
        functools.partial(small_kernel if small else grads_kernel, len(rows), wide),
        grid_spec=pltpu.PrefetchScalarGridSpec(
            num_scalar_prefetch=1,
            grid=(chips,),
            in_specs=[in_vmem] * (2 * len(rows) + len(small))
            + [anywhere] * len(earlier),
            out_specs=[out, out],
            scratch_shapes=[pltpu.VMEM((SMALL, columns), f32)] if small else [],
        ),
        out_shape=[(pltpu.HBM if small else NEAR)((chips, height, columns), bf16)] * 2,
        compiler_params=pltpu.CompilerParams(vmem_limit_bytes=SMALL_LIMIT),
        name=name,
    )(place, *rows, *lows, *small, *earlier)


def pairs_kernel(chips, streamed, keep, come, *refs):
    if streamed:
        refs, (kept, arrived, sems) = refs[:-3], refs[-3:]
        copies = []
        for k in range(chips):
            for i, (source, target) in enumerate(((keep, kept), (come, arrived))):
                copies.append(pltpu.make_async_copy(source.at[k], target.at[k], sems.at[2 * k + i]))
        for copy in copies:
            copy.start()
        keep, come = kept, arrived
    for k, out in enumerate(refs[-chips:]):
        if streamed:
            copies[2 * k].wait()
            copies[2 * k + 1].wait()
        out[...] = (keep[k].astype(f32) + come[k].astype(f32)).astype(out.dtype)


def pairs(keep, come, streamed, earlier=()):
    chips, rows, columns = keep.shape
    scratch = [pltpu.VMEM(keep.shape, bf16)] * 2 + [pltpu.SemaphoreType.DMA((2 * chips,))]
    out = pl.pallas_call(
        functools.partial(pairs_kernel, chips, streamed),
        in_specs=[anywhere if streamed else in_vmem] * 2 + [anywhere] * len(earlier),
        out_specs=[in_vmem] * chips,
        out_shape=[pltpu.HBM((rows, columns), f32)] + [pltpu.HBM((rows, columns), bf16)] * (chips - 1),
        scratch_shapes=scratch if streamed else [],
        compiler_params=pltpu.CompilerParams(vmem_limit_bytes=SMALL_LIMIT),
        name="pairs",
    )(keep, come, *earlier)
    return out[0], list(out[1:])


def back_kernel(parts, with_rows, place, *refs):
    count = len(parts)
    lows, fulls, refs = refs[:count], refs[count : 2 * count], refs[2 * count :]
    rows, out, sums = (refs[0], refs[-2], refs[-1]) if with_rows else (None, refs[-1], None)
    step = pl.program_id(0)
    if with_rows:

        @pl.when(step == 0)
        def _():
            sums[...] = jnp.zeros_like(sums)

    here = pl.ds(pl.multiple_of((step ^ place[2]) * BLOCK, BLOCK), BLOCK)
    for cols in slices(out.shape[1]):
        value = 0.0
        for low, full, part in zip(lows, fulls, parts, strict=True):
            wide = low.shape[1]
            value = value + dot(low[...], full[cols, part * wide : (part + 1) * wide], 1, 1)
        out[:, cols] = value.astype(bf16)
        if with_rows:
            sums[0:1, cols] += jnp.sum(value * rows[here, cols].astype(f32), axis=0, keepdims=True)


def back(place, lows, fulls, rows, name, earlier=()):
    tokens, depth = lows[0].shape[0], fulls[0][0].shape[0]
    by_block = lambda cols: pl.BlockSpec((BLOCK, cols), lambda s, p: (s ^ p[2], 0))
    extra = [] if rows is None else [rows]
    out = pl.pallas_call(
        functools.partial(back_kernel, tuple(part for _, part in fulls), rows is not None),
        grid_spec=pltpu.PrefetchScalarGridSpec(
            num_scalar_prefetch=1,
            grid=(tokens // BLOCK,),
            in_specs=[by_block(v.shape[1]) for v in lows]
            + [in_vmem] * (len(fulls) + len(extra))
            + [anywhere] * len(earlier),
            out_specs=[pl.BlockSpec((BLOCK, depth), lambda s, p: (s, 0))]
            + [pl.BlockSpec((8, depth), lambda s, p: (0, 0)) for _ in extra],
        ),
        out_shape=[jax.ShapeDtypeStruct((tokens, depth), bf16)]
        + [jax.ShapeDtypeStruct((8, depth), f32) for _ in extra],
        compiler_params=pltpu.CompilerParams(vmem_limit_bytes=SMALL_LIMIT),
        name=name,
    )(place, *lows, *[v for v, _ in fulls], *extra, *earlier)
    return out[0], out[1] if extra else None


def add_up(parts, rows, cols):
    value = parts[0][rows, cols].astype(f32)
    for part in parts[1:]:
        value = value + part[rows, cols].astype(f32)
    return value


def collect_kernel(count, n_deps, *refs):
    parts = refs[:count]
    inner, step, taps, bias, gain, heads, common, rest = refs[count + n_deps :]
    shard, channels = inner.shape
    full = parts[0].shape[1]
    own = slice(0, shard)
    for start in range(0, channels, 256):
        cols = slice(start, min(start + 256, channels))
        inner[:, cols] = add_up(parts, own, cols)
    step[...] = add_up(parts, own, slice(full - LANES, full))
    shared = slice(channels, channels + 2 * STATE)
    common[0:shard] = add_up(parts, own, shared).astype(bf16)
    small = add_up(parts, slice(shard, shard + SMALL), slice(0, full))
    taps[...] = small[0:CONV, :channels]
    bias[...] = small[CONV : CONV + 1, :channels]
    gain[...] = small[8:9, :channels]
    heads[...] = jnp.zeros_like(heads)
    heads[0:3] = small[11:14, :LANES]
    rest[...] = jnp.zeros_like(rest)
    rest[0:8] = small[0:8, shared]
    for piece in range(12):
        row, start = divmod(piece * LANES, full)
        target = slice(piece % 2 * LANES, (piece % 2 + 1) * LANES)
        rest[8 + piece // 2 : 9 + piece // 2, target] = small[9 + row : 10 + row, start : start + LANES]
    common[shard:] = rest[...].astype(bf16)


def collect(parts, channels, earlier):
    rows = parts[0].shape[0]
    shapes = [
        (rows - SMALL, channels), (rows - SMALL, LANES), (CONV, channels), (1, channels), (1, channels), (8, LANES)
    ]
    return pl.pallas_call(
        functools.partial(collect_kernel, len(parts), len(earlier)),
        in_specs=[in_vmem] * len(parts) + [anywhere] * len(earlier),
        out_specs=[in_vmem] * 7,
        out_shape=[jax.ShapeDtypeStruct(shape, f32) for shape in shapes]
        + [jax.ShapeDtypeStruct((rows, 2 * STATE), bf16)],
        scratch_shapes=[pltpu.VMEM((SMALL, 2 * STATE), f32)],
        compiler_params=pltpu.CompilerParams(vmem_limit_bytes=SMALL_LIMIT),
        name="collect",
    )(*parts, *earlier)


def finish_kernel(count, *refs):
    parts, norm_gain, (shared, taps, bias, norm) = refs[:count], refs[count], refs[count + 1 :]
    shard = shared.shape[0]
    every = slice(0, 2 * STATE)
    shared[...] = add_up(parts, slice(0, shard), every)
    small = add_up(parts, slice(shard, shard + SMALL), every)
    taps[...] = small[0:CONV]
    bias[...] = small[CONV : CONV + 1]
    for piece in range(norm.shape[0]):
        row, cols = 8 + piece // 2, slice(piece % 2 * LANES, (piece % 2 + 1) * LANES)
        norm[piece : piece + 1] = small[row : row + 1, cols] / norm_gain[piece : piece + 1]


def finish(parts, norm_gain):
    rows = parts[0].shape[0]
    shapes = [(rows - SMALL, 2 * STATE), (CONV, 2 * STATE), (1, 2 * STATE), norm_gain.shape]
    return pl.pallas_call(
        functools.partial(finish_kernel, len(parts)),
        in_specs=[in_vmem] * (len(parts) + 1),
        out_specs=[in_vmem] * 4,
        out_shape=[jax.ShapeDtypeStruct(shape, f32) for shape in shapes],
        name="finish",
    )(*parts, norm_gain)


def nothing(*refs):
    pass


def pinned(values, earlier):
    anywhere = pl.BlockSpec(memory_space=pl.ANY)
    held = pl.pallas_call(
        nothing,
        in_specs=[anywhere] * (len(values) + len(earlier)),
        out_specs=[anywhere] * len(values),
        out_shape=[jax.ShapeDtypeStruct(v.shape, v.dtype) for v in values],
        input_output_aliases={i: i for i in range(len(values))},
        name="pinned",
    )(*values, *earlier)
    return list(held)


def copy_kernel(source, *refs):
    refs[-1][...] = source[...]


def copied(value, earlier):
    whole = pl.BlockSpec(memory_space=pltpu.VMEM)
    return pl.pallas_call(
        copy_kernel,
        in_specs=[whole] + [pl.BlockSpec(memory_space=pl.ANY)] * len(earlier),
        out_specs=whole,
        out_shape=jax.ShapeDtypeStruct(value.shape, value.dtype),
        name="copied",
    )(value, *earlier)


def total_of(own, arrived):
    for value in arrived:
        own = own + value.astype(f32)
    return own


class Net:
    def __init__(self, dp, tensor):
        self.dp, self.tensor = dp, tensor
        self.chips = dp // 2
        rank = lax.axis_index("tensor")
        at = lax.axis_index("dp")
        shift = rank if tensor == 4 else jnp.zeros_like(rank)
        self.place = jnp.stack([at // 2, at % 2, shift]).astype(jnp.int32)

    def over_chips(self, values, k):
        return lax.ppermute(values, "dp", [(i, i ^ (2 * k)) for i in range(self.dp)])

    def over_core(self, values):
        return lax.ppermute(values, "dp", [(i, i ^ 1) for i in range(self.dp)])

    def over_tensor(self, values, k):
        return lax.ppermute(values, "tensor", [(i, i ^ k) for i in range(self.tensor)])

    def between(self, values, pairs):
        return lax.ppermute(values, "dp", [(2 * a + c, 2 * b + c) for a, b in pairs for c in range(2)])

    def gather_near(self, shard):
        if self.chips != 4:
            return [shard] + [self.over_chips(shard, k) for k in range(1, self.chips)]
        return [shard, self.over_chips(shard, 1), self.over_chips(shard, 2)]

    def gather_far(self, near, earlier):
        if self.chips != 4:
            return pinned(near, earlier) if earlier else near
        near = pinned(near, earlier)
        middle = self.between(near[0], [(1, 2), (2, 1)])
        return near + [middle + self.between(near[2], [(1, 0), (2, 3)])]

    def gather_cores(self, mine, earlier, early):
        first = pinned(mine[:-1], early)
        last = pinned(mine[-1:], earlier)
        return first + last + [self.over_core(piece) for piece in first + last]

    def scatter_far(self, others):
        if self.chips != 4:
            return []
        return [self.between(others[2], [(0, 1), (3, 2)]), self.between(others[2], [(1, 2), (2, 1)])]

    def scatter_join(self, others, came):
        if self.chips != 4:
            return others
        one, two = pinned(others[:2], came)
        return [one, (two.astype(f32) + came[0].astype(f32)).astype(bf16)]

    def scatter_near(self, joined, came):
        return came[1:] + [self.over_chips(value, k + 1) for k, value in enumerate(joined)]

    def gather_first(self, shard):
        if self.tensor != 4:
            return [lax.all_gather(shard, "tensor", axis=0, tiled=True)]
        return [shard, self.over_tensor(shard, 1), self.over_tensor(shard, 2)]

    def gather_direct(self, shard):
        if self.tensor != 4:
            return self.gather_first(shard)
        return [shard] + [self.over_tensor(shard, k) for k in range(1, 4)]

    def gather_last(self, pieces, earlier):
        if self.tensor != 4:
            return pieces
        half = BLOCK // 2
        halves = [pieces[1][:half], pieces[2][half:]]
        if earlier:
            halves = pinned(halves, earlier)
        return pieces + [self.over_tensor(halves[0], 2), self.over_tensor(halves[1], 1)]

    def scatter_first(self, rows, earlier):
        if self.tensor != 4:
            return []
        half = BLOCK // 2
        halves = [rows[3 * BLOCK : 3 * BLOCK + half], rows[3 * BLOCK + half :]]
        if earlier:
            halves = pinned(halves, earlier)
        return [self.over_tensor(halves[0], 2), self.over_tensor(halves[1], 1)]

    def scatter_blocks(self, rows, came):
        if self.tensor != 4:
            return [rows]
        half = BLOCK // 2
        own, one, two = rows[:BLOCK], rows[BLOCK : 2 * BLOCK], rows[2 * BLOCK : 3 * BLOCK]
        one = jnp.concatenate([(one[:half].astype(f32) + came[0].astype(f32)).astype(bf16), one[half:]])
        two = jnp.concatenate([two[:half], (two[half:].astype(f32) + came[1].astype(f32)).astype(bf16)])
        return [own, one, two]

    def scatter_last(self, blocks, earlier):
        if self.tensor != 4:
            return [lax.psum_scatter(blocks[0], "tensor", scatter_dimension=0, tiled=True)]
        came = [self.over_tensor(blocks[k], k) for k in (1, 2)]
        return [blocks[0]] + (pinned(came, earlier) if earlier else came)

    def scatter_direct(self, rows, earlier):
        if self.tensor != 4:
            return [lax.psum_scatter(rows, "tensor", scatter_dimension=0, tiled=True)]
        own, *others = jnp.split(rows, 4)
        others = pinned(others, earlier)
        return [own] + [self.over_tensor(block, k + 1) for k, block in enumerate(others)]

    def spread_tensor(self, values):
        return [values] + [self.over_tensor(values, k) for k in range(1, self.tensor)]

    def sum_tensor(self, values):
        return sum(self.spread_tensor(values)[1:], values)


def local(
    net_of,
    tokens,
    norm_gain,
    gate_proj,
    inner_proj,
    shared_proj,
    step_proj,
    conv_inner,
    conv_inner_bias,
    conv_shared,
    conv_shared_bias,
    step_bias,
    decay_log,
    skip_gain,
    out_gain,
    out_proj,
    cotangent,
):
    net = net_of()
    place, chips = net.place, net.chips
    channels = gate_proj.shape[1]
    heads = step_proj.shape[1]
    width = channels + 2 * STATE
    token_rows = tokens.astype(f32)
    inverse = lax.rsqrt(jnp.mean(token_rows * token_rows, axis=-1, keepdims=True) + epsilon)
    unit = token_rows * inverse
    normed_low = (unit * norm_gain).astype(bf16)
    padding = jnp.zeros((step_proj.shape[0], LANES - heads), bf16)
    scan_shard = jnp.concatenate([inner_proj, shared_proj, step_proj, padding], axis=1)
    scan_mine = net.gather_far(net.gather_near(scan_shard), [])
    row_pieces = net.gather_first(normed_low)
    reached = scan_mine[1:]
    cot_copy = copied(cotangent, row_pieces[1:2])
    joint = joint_shard(gate_proj, out_proj, [cot_copy])
    row_pieces = net.gather_last(row_pieces, [])
    scan_pieces = net.gather_cores(scan_mine, row_pieces[3:], [])
    cot_pieces = net.gather_direct(pinned([cot_copy], row_pieces[3:] + scan_pieces[chips:])[0])
    joint_mine = net.gather_near(pinned([joint], reached)[0])

    taps = jnp.concatenate(
        [
            jnp.concatenate([conv_inner, conv_inner_bias[None]]),
            jnp.concatenate([conv_shared, conv_shared_bias[None]]),
        ],
        axis=1,
    )
    taps = jnp.pad(taps, ((0, 8 - CONV - 1), (0, 0)))
    rates = -jnp.exp(decay_log)
    head_rows = jnp.pad(jnp.stack([step_bias, rates]), ((0, 6), (0, LANES - heads)))
    skip_row = jnp.repeat(skip_gain, HEAD_DIM)[None]
    gain = out_gain[None]

    raw, scan_full, rows = product(
        place,
        row_pieces,
        scan_pieces,
        raw_epilogue,
        [],
        [(width + LANES, f32)],
        "project",
    )
    scanned, pre, states = scan_forward(raw, taps, head_rows, skip_row, [])
    joint_mine = net.gather_far(joint_mine, [scanned])
    gate, gated, grad_out, token_sums, joint_full, cot_rows = product(
        place,
        cot_pieces,
        net.gather_cores(joint_mine, cot_pieces[1:], []),
        mix_epilogue,
        [(rows, False), (stay(scanned), True), (gain, False)],
        [(channels, f32), (channels, f32), (channels, f32), (None, 2)],
        "mix",
    )
    token_sums = net.sum_tensor(token_sums)
    out_low, gate_back, scan_grad, gain_grad = gating(grad_out, gated, scanned, gate, token_sums, gain)
    keep, give = weight_grads(
        place, chips, [rows, cot_rows], [gate_back, out_low], [], "grad_joint_proj"
    )
    joint_come = net.over_core(give)
    branch, _ = back(place, [out_low], [(joint_full, 1)], None, "branch", [give])
    joint_own, joint_others = pairs(keep, joint_come, False, [branch])
    came = net.scatter_far(joint_others)
    branch_parts = net.scatter_direct(branch, joint_others[:1])
    held = scan_backward(
        0, raw, pre, scan_grad, states, taps, head_rows, skip_row, None, joint_others[:1]
    )
    came = pinned(came, [held[1]]) if came else came
    joint_arrived = net.scatter_near(net.scatter_join(joint_others, came), came)
    scan_back, sums, head_sums, _, _ = scan_backward(
        1, raw, pre, scan_grad, states, taps, head_rows, skip_row, held, came
    )
    norm_rows, norm_sums = back(
        place, [gate_back, stay(scan_back)], [(joint_full, 0), (scan_full, 0)], rows, "grad_normed"
    )
    keep, give = weight_grads(
        place,
        chips,
        [rows],
        [stay(scan_back)],
        [sums, gain_grad, norm_sums, head_sums],
        "grad_scan_proj",
        joint_arrived + branch_parts[1:],
    )
    norm_came = net.scatter_first(norm_rows, joint_arrived)
    scan_own, scan_others = pairs(stay(keep), stay(net.over_core(give)), True)
    came = net.scatter_far(scan_others)
    came = pinned(came, []) if came else came
    norm_came = pinned(norm_came, scan_others[:1]) if norm_came else norm_came
    joined = net.scatter_join(scan_others, came)
    *joint_arrived, = pinned(joint_arrived, joined[1:2])
    scan_arrived = net.scatter_near(joined, came)
    norm_parts = net.scatter_last(net.scatter_blocks(norm_rows, norm_came), joined[1:])
    grad_normed = total_of(norm_parts[0].astype(f32), norm_parts[1:])
    mixed = total_of(token_rows, branch_parts).astype(bf16)
    joint_total = total_of(joint_own, joint_arrived)
    grad_gate_proj, grad_out_proj = joint_total[:, :channels], joint_total[:, channels:].T
    spread = grad_normed * norm_gain
    grad_tokens = (
        cotangent.astype(f32)
        + inverse * spread
        - unit * (inverse * jnp.mean(spread * unit, axis=-1, keepdims=True))
    )
    grad_inner_proj, step_part, grad_conv_inner, inner_bias, gain_part, head_part, common = collect(
        [scan_own] + scan_arrived, channels, []
    )
    grad_shared_proj, grad_conv_shared, shared_bias, norm_part = finish(
        net.spread_tensor(common), norm_gain.reshape(-1, LANES)
    )
    return (
        mixed,
        grad_tokens,
        norm_part.reshape(-1),
        grad_gate_proj,
        grad_inner_proj,
        grad_shared_proj,
        step_part[:, :heads],
        grad_conv_inner,
        inner_bias.reshape(-1),
        grad_conv_shared,
        shared_bias.reshape(-1),
        head_part[0, :heads],
        head_part[1, :heads] * rates,
        head_part[2, :heads],
        gain_part.reshape(-1),
        grad_out_proj,
    )


def solution(mesh):
    dp, tensor = mesh.shape["dp"], mesh.shape["tensor"]

    def on_device(*args):
        return local(lambda: Net(dp, tensor), *args)

    return jax.shard_map(
        on_device,
        mesh=mesh,
        in_specs=(
            P(("dp", "tensor"), None),
            P(),
            P("dp", "tensor"),
            P("dp", "tensor"),
            P("dp", None),
            P("dp", "tensor"),
            P(None, "tensor"),
            P("tensor"),
            P(),
            P(),
            P("tensor"),
            P("tensor"),
            P("tensor"),
            P("tensor"),
            P("tensor", "dp"),
            P(("dp", "tensor"), None),
        ),
        out_specs=(
            P(("dp", "tensor"), None),
            P(("dp", "tensor"), None),
            P(),
            P("dp", "tensor"),
            P("dp", "tensor"),
            P("dp", None),
            P("dp", "tensor"),
            P(None, "tensor"),
            P("tensor"),
            P(),
            P(),
            P("tensor"),
            P("tensor"),
            P("tensor"),
            P("tensor"),
            P("tensor", "dp"),
        ),
        check_vma=False,
    )
```
